512 devices in a mesh: dp: 32 (over x, z_lo, core), tensor: 16 (over z_hi, y).
Axes of the slice: x: 4, y: 8, z: 8 (z_hi: 2, z_lo: 4; z = z_hi * 4 + z_lo), core: 2. Of those that a mesh axis runs over, the one named last changes fastest.
Arguments:
- learn_input: bfloat16 [8192, 8192], P('dp', 'tensor'), may hold values from -6 to 6
- cotangent: bfloat16 [8192, 2, 1024], P('dp', None, 'tensor'), may hold values from -6 to 6
- rewards: float32 [256], P('dp'), may hold values from -6 to 6
- group_ids: int32 [256], P('dp'), may hold values from 0 to 3
- adapter_down: float32 [2, 64, 8192], P(None, None, 'tensor'), may hold values from -0.0625 to 0.0625
- adapter_up: float32 [2, 64, 1024], P(None, None, 'tensor'), may hold values from -0.12 to 0.12
- frozen_weight: bfloat16 [2, 8192, 1024], P(None, 'tensor'), may hold values from -0.0625 to 0.0625
- hidden: bfloat16 [256, 4, 8192], P('dp', None, 'tensor'), may hold values from -6 to 6
- queries: bfloat16 [256, 4, 32, 128], P('dp'), may hold values from -128 to 128
- key_cache: bfloat16 [256, 768, 8, 128], P('dp', 'tensor'), may hold values from -4 to 4
- value_cache: bfloat16 [256, 768, 8, 128], P('dp', 'tensor'), may hold values from -6 to 6
- cache_lengths: int32 [256], P('dp'), may hold values from 384 to 768, as said below
Outputs:
- updated_down: float32 [2, 64, 8192], P(None, None, 'tensor')
- updated_up: float32 [2, 64, 1024], P(None, None, 'tensor')
- attended: bfloat16 [256, 4, 4096], P('dp', None, 'tensor')
The draws below stay inside these ranges and needn't reach their ends.
Inputs may be any that keep to these rules, and one draw needn't show every extreme that they name: `group_ids`: ids number the prompts of the 8 completions of one learner shard. `cache_lengths`: positions 0 to length - 1 of a row's cache are filled; some row has 768, some row 384.
All inputs are finite; a program needn't handle non-finite values.
Results may differ from the reference program's by a relative error of at most 0.012.
Values may be sent and summed in bfloat16 or wider, within the bound.
A program may use at most 64 MiB of HBM per device.

```python
import math
import jax
import jax.numpy as jnp
from jax import lax

D = 8192
KVH = 8
HD = 128
QH = 32
RANK = 64
KVW = 1024
GROUPS_DEV = 4
SEQ_LEN = 32
SEQ_DEV = 8
CACHE_DEV = 48
STEPS = 4
SEQS = 256
TOKENS = 8192
ROWS = 256
CACHE = 768
N_DP = 32


def draw_key_cache(key, part):
    key = jax.random.fold_in(key, 1)
    sample = jnp.clip(jax.random.normal(key, (ROWS, CACHE, KVH, HD), jnp.float32), -4.0, 4.0)
    return sample.astype(jnp.bfloat16)


def draw_queries(key, part):
    key = jax.random.fold_in(key, 2)
    sample = jnp.clip(jax.random.normal(key, (ROWS, STEPS, QH, HD), jnp.float32), -4.0, 4.0)
    return sample.astype(jnp.bfloat16)


def draw_cache_lengths(key, part):
    key = jax.random.fold_in(key, 3)
    lengths = jax.random.randint(key, (ROWS,), CACHE // 2, CACHE + 1)
    top_row = jax.random.randint(jax.random.fold_in(key, 1), (), 0, ROWS)
    low_row = (top_row + 1 + jax.random.randint(jax.random.fold_in(key, 2), (), 0, ROWS - 1)) % ROWS
    row_index = jnp.arange(ROWS)
    lengths = jnp.where(row_index == top_row, CACHE, lengths)
    lengths = jnp.where(row_index == low_row, CACHE // 2, lengths)
    return lengths.astype(jnp.int32)


def touch_ends(values, stream_key, smallest, high):
    longest = values.shape.index(max(values.shape))
    spots = []
    for shift in (0, 1):
        where = [jax.random.randint(jax.random.fold_in(stream_key, axis), (), 0, length) for axis, length in enumerate(values.shape)]
        where[longest] = (where[longest] + shift) % values.shape[longest]
        spots.append(tuple(where))
    return values.at[spots[0]].set(smallest).at[spots[1]].set(high)


def block_levels(stream_key, shape, shards, least, high):
    gain, own = 1.0, jax.random.fold_in(stream_key, 6)
    for axis_at, shards_of in shards:
        steps = jnp.exp(jax.random.uniform(jax.random.fold_in(own, axis_at), (shards_of,), jnp.float32, least / len(shards), high / len(shards)))
        gain = gain * jnp.repeat(steps, shape[axis_at] // shards_of).reshape([-1 if axis == axis_at else 1 for axis in range(len(shape))])
    return gain


def scatter_about(stream_key, dims, scale, bound, pieces=(), kind=jnp.bfloat16):
    gain = block_levels(stream_key, dims, pieces, -0.22, 0.18) if pieces else 1.0
    array = jax.random.normal(stream_key, dims, jnp.float32) * scale * gain
    return jnp.minimum(jnp.maximum(array, -bound), bound).astype(kind)


def setup_inputs(seed: int = 0) -> dict:
    key_of = jax.random.split(jax.random.key(seed), 13)
    learn_input = scatter_about(key_of[0], (TOKENS, D), 1.0, 6.0, ((0, 32), (1, 16)))
    cotangent = scatter_about(key_of[1], (TOKENS, 2, KVW), 1.0, 6.0, ((0, 32), (2, 16)))
    rewards = scatter_about(key_of[2], (SEQS,), 1.0, 6.0, ((0, 32),), jnp.float32)
    group_ids = touch_ends(jax.random.randint(key_of[3], (SEQS,), 0, GROUPS_DEV), jax.random.fold_in(key_of[3], 1), 0, GROUPS_DEV - 1).astype(jnp.int32)
    adapter_down = scatter_about(key_of[4], (2, RANK, D), D ** -0.5, 0.0625, ((2, 16),), jnp.float32)
    adapter_up = scatter_about(key_of[5], (2, RANK, KVW), 0.02, 0.12, ((2, 16),), jnp.float32)
    frozen_weight = scatter_about(key_of[6], (2, D, KVW), D ** -0.5, 0.0625, ((1, 16),))
    hidden = scatter_about(key_of[7], (ROWS, STEPS, D), 1.0, 6.0, ((0, 32), (2, 16)))
    queries = draw_queries(jax.random.fold_in(key_of[12], 71), 0)
    key_cache = draw_key_cache(jax.random.fold_in(key_of[12], 71), 0)
    value_cache = scatter_about(key_of[10], (ROWS, CACHE, KVH, HD), 1.0, 6.0, ((0, 32), (1, 16)))
    cache_lengths = draw_cache_lengths(jax.random.fold_in(key_of[12], 71), 0)
    return dict(learn_input=learn_input, cotangent=cotangent, rewards=rewards, group_ids=group_ids, adapter_down=adapter_down, adapter_up=adapter_up, frozen_weight=frozen_weight, hidden=hidden, queries=queries, key_cache=key_cache, value_cache=value_cache, cache_lengths=cache_lengths)


adapter_scale = 2.0
step_size = 0.004
masked_score = -1e+30

def group_advantage(rewards, group_ids):
    member = (group_ids[:, None] == jnp.arange(GROUPS_DEV, dtype=jnp.int32)[None, :]).astype(jnp.float32)
    counts = jnp.maximum(lax.optimization_barrier(jnp.sum(member, axis=0)), 1.0)
    group_mean = lax.optimization_barrier(jnp.sum(member * rewards[:, None], axis=0)) / counts
    own_mean = lax.optimization_barrier(jnp.sum(member * group_mean[None, :], axis=1))
    offset = rewards - own_mean
    spread = lax.optimization_barrier(jnp.sum(member * (offset * offset)[:, None], axis=0)) / counts
    own_std = lax.optimization_barrier(jnp.sum(member * jnp.sqrt(spread)[None, :], axis=1))
    return offset / jnp.maximum(own_std, 1.0)

def reference(learn_input, cotangent, rewards, group_ids, adapter_down, adapter_up, frozen_weight, hidden, queries, key_cache, value_cache, cache_lengths):
    advantage = jax.vmap(group_advantage)(rewards.reshape(N_DP, SEQ_DEV), group_ids.reshape(N_DP, SEQ_DEV)).reshape(SEQS)
    token_weight = jnp.repeat(advantage / SEQ_LEN, SEQ_LEN)
    weighted_rows = (cotangent.astype(jnp.float32) * token_weight[:, None, None]).astype(jnp.bfloat16)
    rounded_down = adapter_down.astype(jnp.bfloat16)
    rounded_up = adapter_up.astype(jnp.bfloat16)
    widened_inputs = learn_input.astype(jnp.float32)
    projected_rows = jnp.einsum('td,krd->tkr', widened_inputs, rounded_down.astype(jnp.float32)).astype(jnp.bfloat16)
    reverse_pass = jnp.einsum('tkc,krc->tkr', weighted_rows.astype(jnp.float32), rounded_up.astype(jnp.float32)).astype(jnp.bfloat16)
    down_gradient = adapter_scale * jnp.einsum('xnu,xh->nuh', reverse_pass.astype(jnp.float32), widened_inputs)
    up_gradient = adapter_scale * jnp.einsum('nhj,nhf->hjf', projected_rows.astype(jnp.float32), weighted_rows.astype(jnp.float32))
    updated_down = adapter_down + step_size * down_gradient
    updated_up = adapter_up + step_size * up_gradient
    roll_down = updated_down.astype(jnp.bfloat16)
    roll_up = updated_up.astype(jnp.bfloat16)
    reduced_rank = jnp.einsum('krd,krc->kdc', roll_down.astype(jnp.float32), roll_up.astype(jnp.float32))
    combined_weight = (frozen_weight.astype(jnp.float32) + adapter_scale * reduced_rank).astype(jnp.bfloat16)
    recent_kv = jnp.einsum('rtd,kdc->rtkc', hidden.astype(jnp.float32), combined_weight.astype(jnp.float32)).astype(jnp.bfloat16)
    new_keys = recent_kv[:, :, 0].reshape(ROWS, STEPS, KVH, HD).astype(jnp.float32)
    new_values = recent_kv[:, :, 1].reshape(ROWS, STEPS, KVH, HD).astype(jnp.float32)
    score_scale = 1.0 / math.sqrt(HD)
    blocks = CACHE // CACHE_DEV
    grouped = queries.astype(jnp.float32).reshape(ROWS, STEPS, KVH, QH // KVH, HD)
    cached = jnp.einsum('rtgqd,rpgd->rtgqp', grouped, key_cache.astype(jnp.float32)) * score_scale
    cached = cached.reshape(ROWS, STEPS, KVH, QH // KVH, blocks, CACHE_DEV)
    valid_mask = jnp.arange(CACHE, dtype=jnp.int32)[None, :] < cache_lengths[:, None]
    valid_block = valid_mask.reshape(ROWS, blocks, CACHE_DEV)[:, None, None, None]
    cached = jnp.where(valid_block, cached, masked_score)
    block_high = lax.optimization_barrier(jnp.max(cached, axis=-1))
    block_weight = jnp.where(valid_block, jnp.exp(cached - block_high[..., None]), 0.0)
    block_total = lax.optimization_barrier(jnp.sum(block_weight, axis=-1))
    value_blocks = value_cache.astype(jnp.float32).reshape(ROWS, blocks, CACHE_DEV, KVH, HD)
    block_mix = jnp.einsum('rtgqbp,rbpgd->rtgqbd', block_weight.astype(jnp.bfloat16).astype(jnp.float32), value_blocks)
    recent = jnp.einsum('rtgqd,rjgd->rtgqj', grouped, new_keys) * score_scale
    causal = jnp.arange(STEPS)[:, None] >= jnp.arange(STEPS)[None, :]
    recent = jnp.where(causal[None, :, None, None, :], recent, masked_score)
    new_high = lax.optimization_barrier(jnp.max(recent, axis=-1))
    new_weight = jnp.where(causal[None, :, None, None, :], jnp.exp(recent - new_high[..., None]), 0.0)
    new_total = lax.optimization_barrier(jnp.sum(new_weight, axis=-1))
    new_mix = jnp.einsum('rtgqj,rjgd->rtgqd', new_weight.astype(jnp.bfloat16).astype(jnp.float32), new_values)
    highest = jnp.maximum(lax.optimization_barrier(jnp.max(block_high, axis=-1)), new_high)
    block_factor = jnp.exp(block_high - highest[..., None])
    new_factor = jnp.exp(new_high - highest)
    total = lax.optimization_barrier(jnp.sum(block_factor * block_total, axis=-1)) + new_factor * new_total
    mixed = lax.optimization_barrier(jnp.sum(block_factor[..., None] * block_mix, axis=-2)) + new_factor[..., None] * new_mix
    mixed = mixed / total[..., None]
    attended = mixed.reshape(ROWS, STEPS, QH * HD).astype(jnp.bfloat16)
    return (updated_down, updated_up, attended)
```

```python
import functools
import math

import jax
import jax.numpy as jnp
from jax import lax
from jax.experimental import pallas as pl
from jax.experimental.pallas import tpu as pltpu
from jax.sharding import PartitionSpec as P

MESH = pl.DeviceIdType.MESH
F32 = jnp.float32
BF16 = jnp.bfloat16

N_DP = 32
N_TP = 16
RANK = 64
SEQ_DEV = 8
SEQ_LEN = 32
TOK = SEQ_DEV * SEQ_LEN
FEAT = 512
ROWS = 8
STEPS = 4
CACHE_DEV = 48
KVH = 8
HD = 128
KVW = KVH * HD
TILES = 32
UP_TILES = 4
UP_STRIDE = 10

adapter_scale = 2.0
step_size = 0.004
masked_score = -1e30
score_scale = 1.0 / math.sqrt(HD)

(X, COT, DOWN, UP, HID, FRO, QRY, KEY, VAL) = range(9)
(RS1, AG1, RS2, RS2U, AG2, AG2U, BASE, MIX, STAT, LOW, UPX) = range(11)


def dot(a, b):
    return lax.dot_general(a, b, (((1,), (0,)), ((), ())), preferred_element_type=F32)


def dot_nt(a, b):
    return lax.dot_general(a, b, (((1,), (1,)), ((), ())), preferred_element_type=F32)


def iota(shape, axis):
    return lax.broadcasted_iota(jnp.int32, shape, axis)


def kernel(
    rew,
    gid,
    lens,
    x_h,
    cot_h,
    down_h,
    up_h,
    hid_h,
    fro_h,
    q_h,
    k_h,
    v_h,
    od,
    ou,
    oa,
    x,
    cot,
    down,
    up,
    hid,
    fro,
    qry,
    key,
    val,
    hid_f,
    wt,
    pb_send,
    rs1,
    ag1,
    g_send,
    rs2,
    rs2u,
    ag2,
    base_send,
    base_r,
    mix_send,
    mix_r,
    st_send,
    st_r,
    low_send,
    low_r,
    upx_send,
    upx_r,
    qp,
    cmix,
    cmax,
    ctot,
    base_s,
    in_sem,
    send,
    recv,
):
    dp = lax.axis_index("dp")
    tp = lax.axis_index("tensor")

    hbm = (x_h, cot_h, down_h, up_h, hid_h, fro_h, q_h, k_h, v_h)
    vmem = (x, cot, down, up, hid, fro, qry, key, val)
    loads = [pltpu.make_async_copy(h, v, in_sem.at[n]) for n, (h, v) in enumerate(zip(hbm, vmem))]
    for load in loads:
        load.start()

    barrier = pltpu.get_barrier_semaphore()

    def greet_tp(s, c):
        pl.semaphore_signal(
            barrier, inc=1, device_id={"tensor": lax.rem(tp + s, N_TP)}, device_id_type=MESH
        )
        return c

    def greet_dp(s, c):
        pl.semaphore_signal(
            barrier, inc=1, device_id={"dp": lax.rem(dp + s, N_DP)}, device_id_type=MESH
        )
        return c

    lax.fori_loop(1, N_TP, greet_tp, 0)
    lax.fori_loop(1, N_DP, greet_dp, 0)

    def to_tp(src, dst, chan):
        def body(s, c):
            peer = lax.rem(tp + s, N_TP)
            pltpu.make_async_remote_copy(
                src_ref=src(peer),
                dst_ref=dst(s),
                send_sem=send.at[chan],
                recv_sem=recv.at[chan],
                device_id={"tensor": peer},
                device_id_type=MESH,
            ).start()
            return c

        lax.fori_loop(1, N_TP, body, 0)

    def to_dp(src, dst, chan):
        def body(s, c):
            peer = lax.rem(dp + s, N_DP)
            pltpu.make_async_remote_copy(
                src_ref=src(peer),
                dst_ref=dst(s),
                send_sem=send.at[chan],
                recv_sem=recv.at[chan],
                device_id={"dp": peer},
                device_id_type=MESH,
            ).start()
            return c

        lax.fori_loop(1, N_DP, body, 0)

    def landed(ref, chan):
        pltpu.make_async_copy(ref, ref, recv.at[chan]).wait()

    def sent(ref, chan):
        pltpu.make_async_copy(ref, ref, send.at[chan]).wait()

    def summed(own, ref, count):
        return lax.fori_loop(0, count, lambda s, acc: acc + ref[s].astype(F32), own.astype(F32))

    lane_seq = lax.div(iota((1, TOK), 1), SEQ_LEN)
    rew_l = jnp.zeros((1, TOK), F32)
    gid_l = jnp.zeros((1, TOK), jnp.int32)
    for s in range(SEQ_DEV):
        rew_l = jnp.where(lane_seq == s, rew[s], rew_l)
        gid_l = jnp.where(lane_seq == s, gid[s], gid_l)
    cnt = jnp.zeros((1, TOK), F32)
    tot = jnp.zeros((1, TOK), F32)
    for s in range(SEQ_DEV):
        same = gid_l == gid[s]
        cnt = cnt + jnp.where(same, 1.0, 0.0)
        tot = tot + jnp.where(same, rew[s], 0.0)
    mean = tot / cnt
    spread = jnp.zeros((1, TOK), F32)
    for s in range(SEQ_DEV):
        off = rew[s] - mean
        spread = spread + jnp.where(gid_l == gid[s], off * off, 0.0)
    adv = (rew_l - mean) / jnp.maximum(jnp.sqrt(spread / cnt), 1.0)
    token_weight = adv / SEQ_LEN

    loads[X].wait()
    loads[COT].wait()
    loads[DOWN].wait()
    loads[UP].wait()
    proj = dot_nt(down[...].astype(BF16), x[...])
    pb_send[0:8] = proj.astype(BF16).reshape(8, 16, TOK)
    wt[...] = (cot[...].astype(F32) * token_weight).astype(BF16)
    same_k = lax.div(iota((128, 128), 0), RANK) == lax.div(iota((128, 128), 1), RANK)
    up2 = jnp.concatenate([up[...], up[...]], axis=1)
    back = dot(jnp.where(same_k, up2, 0.0).astype(BF16), wt[...])
    pb_send[8:16] = back.astype(BF16).reshape(8, 16, TOK)

    pl.semaphore_wait(barrier, N_TP + N_DP - 2)
    to_tp(lambda peer: pb_send.at[peer], lambda s: rs1.at[s - 1], RS1)

    loads[HID].wait()
    for i in range(ROWS):
        hid_f[STEPS * i : STEPS * (i + 1), :] = hid[i].astype(F32)
    loads[FRO].wait()
    hid_b = hid_f[...].astype(BF16)
    for kv in range(2):
        for part in range(4):
            cols = slice(part * 256, (part + 1) * 256)
            block = dot(hid_b, fro[kv, :, cols]).astype(BF16)
            base_send[2 * part, kv] = block[:, 0:HD]
            base_send[2 * part + 1, kv] = block[:, HD : 2 * HD]

    landed(rs1, RS1)
    ag1[tp] = summed(pb_send[tp], rs1, N_TP - 1).astype(BF16)
    to_tp(lambda peer: ag1.at[tp], lambda s: ag1.at[tp], AG1)
    to_tp(lambda peer: base_send.at[lax.div(peer, 2)], lambda s: base_r.at[s - 1], BASE)

    loads[QRY].wait()
    loads[KEY].wait()
    loads[VAL].wait()
    out_row = iota((128, 128), 0)
    head = 2 * lax.div(out_row, 8) + lax.rem(lax.div(out_row, STEPS), 2)
    source = lax.rem(out_row, STEPS) * 32 + head
    perm = jnp.where(iota((128, 128), 1) == source, 1.0, 0.0).astype(BF16)
    lane_n = iota((128, CACHE_DEV * KVH), 1)
    own_group = lax.rem(lane_n, KVH) == lax.div(iota((128, CACHE_DEV * KVH), 0), 16)
    position = tp * CACHE_DEV + lax.div(lane_n, KVH)
    st_lane = iota((128, 128), 1)

    def attend(i, stats):
        q = dot(perm, qry[i])
        qp[i] = q
        score = dot_nt(q.astype(BF16), key[i]) * score_scale
        valid = jnp.logical_and(own_group, position < lens[i])
        score = jnp.where(valid, score, masked_score)
        high = jnp.max(score, axis=1, keepdims=True)
        weight = jnp.where(valid, jnp.exp(score - high), 0.0)
        total = jnp.sum(weight, axis=1, keepdims=True)
        mix = dot(weight.astype(BF16), val[i])
        stats = jnp.where(st_lane == i, high, stats)
        stats = jnp.where(st_lane == i + ROWS, total, stats)
        return mix.reshape(N_TP, 8, HD), stats

    def attend_pair(n, stats):
        m0, stats = attend(2 * n, stats)
        m1, stats = attend(2 * n + 1, stats)
        mix_send[:, pl.ds(pl.multiple_of(16 * n, 16), 16), :] = jnp.concatenate(
            [m0, m1], axis=1
        ).astype(BF16)
        return stats

    stats = lax.fori_loop(0, 2, attend_pair, jnp.zeros((128, 128), F32))

    landed(ag1.at[pl.ds(0, N_TP - 1)], AG1)
    g_down = dot(ag1[8:16].reshape(128, TOK), x[...]).astype(BF16)
    for n in range(TILES):
        r, c = n // 4, n % 4
        g_send[n] = g_down[16 * r : 16 * (r + 1), 128 * c : 128 * (c + 1)]
    g_up = dot_nt(ag1[0:8].reshape(128, TOK), wt[...])
    first_half = iota((RANK, 128), 1) < RANK
    g_up = jnp.where(first_half, g_up[0:RANK], g_up[RANK:])
    g_send[TILES : TILES + UP_TILES] = g_up.astype(BF16).reshape(UP_TILES, 16, 128)

    to_dp(lambda peer: g_send.at[peer], lambda s: rs2.at[s - 1], RS2)
    up_owner = lax.rem(dp, UP_STRIDE) == 0
    up_tile = TILES + lax.div(dp, UP_STRIDE)
    for u in range(UP_TILES):
        peer = UP_STRIDE * u

        @pl.when(dp != peer)
        def _(u=u, peer=peer):
            pltpu.make_async_remote_copy(
                src_ref=g_send.at[TILES + u],
                dst_ref=rs2u.at[lax.rem(peer - dp + N_DP, N_DP) - 1],
                send_sem=send.at[RS2U],
                recv_sem=recv.at[RS2U],
                device_id={"dp": peer},
                device_id_type=MESH,
            ).start()

    stats = lax.fori_loop(2, 4, attend_pair, stats)
    st_send[...] = stats.reshape(N_TP, 8, 128)
    to_tp(lambda peer: st_send.at[peer], lambda s: st_r.at[s - 1], STAT)
    to_tp(lambda peer: mix_send.at[peer], lambda s: mix_r.at[s - 1], MIX)

    landed(rs2, RS2)
    ag2[dp] = summed(g_send[dp], rs2, N_DP - 1).astype(BF16)
    to_dp(lambda peer: ag2.at[dp], lambda s: ag2.at[dp], AG2)

    @pl.when(up_owner)
    def _():
        landed(rs2u, RS2U)
        ag2[up_tile] = summed(g_send[up_tile], rs2u, N_DP - 1).astype(BF16)
        to_dp(lambda peer: ag2.at[up_tile], lambda s: ag2.at[up_tile], AG2U)

    landed(base_r, BASE)
    base = lax.fori_loop(
        0,
        N_TP - 1,
        lambda s, acc: acc + base_r[s].astype(F32),
        base_send[lax.div(tp, 2)].astype(F32),
    )
    base_s[...] = base
    landed(st_r, STAT)
    landed(mix_r, MIX)
    own_st = st_send[tp]
    top = lax.fori_loop(0, N_TP - 1, lambda s, acc: jnp.maximum(acc, st_r[s]), own_st)

    def part(st, mix, total, acc):
        factor = jnp.exp(st - top)
        total = total + factor * pltpu.roll(st, 128 - ROWS, 1)
        acc = tuple(
            acc[i] + factor[:, i : i + 1] * mix[8 * i : 8 * (i + 1)].astype(F32)
            for i in range(ROWS)
        )
        return total, acc

    zero = jnp.zeros((8, 128), F32)
    carry = part(own_st, mix_send[tp], zero, (zero,) * ROWS)
    total, acc = lax.fori_loop(
        0, N_TP - 1, lambda s, carry: part(st_r[s], mix_r[s], *carry), carry
    )
    for i in range(ROWS):
        rows = slice(8 * i, 8 * (i + 1))
        cmix[rows, :] = acc[i]
        cmax[rows, :] = jnp.broadcast_to(top[:, i : i + 1], (8, 128))
        ctot[rows, :] = jnp.broadcast_to(total[:, i : i + 1], (8, 128))

    landed(ag2.at[pl.ds(0, N_DP - 1)], AG2)
    for n in range(TILES):
        r, c = n // 4, n % 4
        rows, cols = slice(16 * r, 16 * (r + 1)), slice(128 * c, 128 * (c + 1))
        od[rows, cols] = down[rows, cols] + step_size * (adapter_scale * ag2[n].astype(F32))
    low = dot_nt(hid_b, od[...].astype(BF16))
    low_send[...] = low.astype(BF16)
    to_tp(lambda peer: low_send, lambda s: low_r.at[s - 1], LOW)

    @pl.when(up_owner)
    def _():
        landed(ag2.at[pl.ds(0, UP_TILES - 1)], AG2U)

    @pl.when(jnp.logical_not(up_owner))
    def _():
        landed(ag2.at[pl.ds(0, UP_TILES)], AG2U)

    up_old = jnp.where(first_half, up2[0:RANK], up2[RANK:])
    up_grad = ag2[TILES : TILES + UP_TILES].reshape(RANK, 128).astype(F32)
    up_new = up_old + step_size * (adapter_scale * up_grad)
    ou[0:RANK] = up_new[:, 0:RANK]
    ou[RANK:] = pltpu.roll(up_new, RANK, 1)[:, 0:RANK]
    upx_send[...] = up_new.astype(BF16)
    pair = tp + 1 - 2 * lax.rem(tp, 2)
    swap = pltpu.make_async_remote_copy(
        src_ref=upx_send,
        dst_ref=upx_r,
        send_sem=send.at[UPX],
        recv_sem=recv.at[UPX],
        device_id={"tensor": pair},
        device_id_type=MESH,
    )
    swap.start()

    own_q = qp[:, pl.ds(pl.multiple_of(8 * tp, 8), 8), :].reshape(64, HD).astype(BF16)

    swap.wait_recv()
    even = lax.rem(tp, 2) == 0
    mine = upx_send[...].astype(F32)
    theirs = upx_r[...].astype(F32)
    left = jnp.where(even, mine, theirs)
    right = jnp.where(even, theirs, mine)
    up_k = jnp.where(first_half, left, pltpu.roll(right, RANK, 1)).astype(BF16)
    up_v = jnp.where(first_half, pltpu.roll(left, RANK, 1), right).astype(BF16)

    landed(low_r, LOW)
    low = summed(low_send[...], low_r, N_TP - 1).astype(BF16)
    new_k = (base_s[0] + adapter_scale * dot(low[:, 0:RANK], up_k)).astype(BF16)
    new_v = (base_s[1] + adapter_scale * dot(low[:, RANK:], up_v)).astype(BF16)
    row = iota((64, 32), 0)
    col = iota((64, 32), 1)
    causal = jnp.logical_and(
        lax.div(row, 8) == lax.div(col, STEPS), lax.rem(col, STEPS) <= lax.rem(row, STEPS)
    )
    score = jnp.where(causal, dot_nt(own_q, new_k) * score_scale, masked_score)
    new_high = jnp.max(score, axis=1, keepdims=True)
    weight = jnp.where(causal, jnp.exp(score - new_high), 0.0)
    new_total = jnp.sum(weight, axis=1, keepdims=True)
    new_mix = dot(weight.astype(BF16), new_v)
    old_high = cmax[...]
    highest = jnp.maximum(old_high, new_high)
    f_old = jnp.exp(old_high - highest)
    f_new = jnp.exp(new_high - highest)
    out = (f_old * cmix[...] + f_new * new_mix) / (f_old * ctot[...] + f_new * new_total)
    out = out.reshape(ROWS, 8, HD)
    oa[:, :, 0:HD] = out[:, 0:STEPS].astype(BF16)
    oa[:, :, HD:] = out[:, STEPS:].astype(BF16)

    sent(rs1, RS1)
    sent(rs1, AG1)
    sent(base_r, BASE)
    sent(st_r, STAT)
    sent(mix_r, MIX)
    sent(rs2, RS2)
    sent(rs2, AG2)
    sent(low_r, LOW)
    swap.wait_send()

    @pl.when(up_owner)
    def _():
        sent(ag2.at[pl.ds(0, UP_TILES - 1)], RS2U)
        sent(rs2u, AG2U)

    @pl.when(jnp.logical_not(up_owner))
    def _():
        sent(ag2.at[pl.ds(0, UP_TILES)], RS2U)


def shards(
    learn_input,
    cotangent,
    rewards,
    group_ids,
    adapter_down,
    adapter_up,
    frozen_weight,
    hidden,
    queries,
    key_cache,
    value_cache,
    cache_lengths,
):
    smem = pl.BlockSpec(memory_space=pltpu.SMEM)
    hbm = pl.BlockSpec(memory_space=pl.ANY)
    vmem = pl.BlockSpec(memory_space=pltpu.VMEM)
    operands = (
        learn_input,
        jnp.transpose(cotangent, (1, 2, 0)).reshape(128, TOK),
        adapter_down.reshape(128, FEAT),
        adapter_up.reshape(128, RANK),
        hidden,
        frozen_weight,
        queries.reshape(ROWS, 128, HD),
        key_cache.reshape(ROWS, CACHE_DEV * KVH, HD),
        value_cache.reshape(ROWS, CACHE_DEV * KVH, HD),
    )
    out_down, out_up, attended = pl.pallas_call(
        kernel,
        out_shape=(
            jax.ShapeDtypeStruct((128, FEAT), F32),
            jax.ShapeDtypeStruct((128, RANK), F32),
            jax.ShapeDtypeStruct((ROWS, STEPS, 2 * HD), BF16),
        ),
        in_specs=[smem] * 3 + [hbm] * 9,
        out_specs=(vmem, vmem, vmem),
        scratch_shapes=[pltpu.VMEM(o.shape, o.dtype) for o in operands]
        + [
            pltpu.VMEM((ROWS * STEPS, FEAT), F32),
            pltpu.VMEM((128, TOK), BF16),
            pltpu.VMEM((16, 16, TOK), BF16),
            pltpu.VMEM((15, 16, TOK), BF16),
            pltpu.VMEM((16, 16, TOK), BF16),
            pltpu.VMEM((36, 16, 128), BF16),
            pltpu.VMEM((31, 16, 128), BF16),
            pltpu.VMEM((31, 16, 128), BF16),
            pltpu.VMEM((36, 16, 128), BF16),
            pltpu.VMEM((8, 2, 32, HD), BF16),
            pltpu.VMEM((15, 2, 32, HD), BF16),
            pltpu.VMEM((16, 64, HD), BF16),
            pltpu.VMEM((15, 64, HD), BF16),
            pltpu.VMEM((16, 8, 128), F32),
            pltpu.VMEM((15, 8, 128), F32),
            pltpu.VMEM((32, 128), BF16),
            pltpu.VMEM((15, 32, 128), BF16),
            pltpu.VMEM((RANK, 128), BF16),
            pltpu.VMEM((RANK, 128), BF16),
            pltpu.VMEM((ROWS, 128, HD), F32),
            pltpu.VMEM((64, HD), F32),
            pltpu.VMEM((64, HD), F32),
            pltpu.VMEM((64, HD), F32),
            pltpu.VMEM((2, 32, HD), F32),
            pltpu.SemaphoreType.DMA((9,)),
            pltpu.SemaphoreType.DMA((11,)),
            pltpu.SemaphoreType.DMA((11,)),
        ],
        compiler_params=pltpu.CompilerParams(
            collective_id=0, has_side_effects=True, vmem_limit_bytes=32 * 1024 * 1024
        ),
    )(rewards, group_ids, cache_lengths, *operands)
    return (
        out_down.reshape(2, RANK, FEAT),
        out_up.reshape(2, RANK, RANK),
        attended,
    )


def solution(mesh):
    return jax.shard_map(
        shards,
        mesh=mesh,
        in_specs=(
            P("dp", "tensor"),
            P("dp", None, "tensor"),
            P("dp"),
            P("dp"),
            P(None, None, "tensor"),
            P(None, None, "tensor"),
            P(None, "tensor", None),
            P("dp", None, "tensor"),
            P("dp", None, None, None),
            P("dp", "tensor", None, None),
            P("dp", "tensor", None, None),
            P("dp"),
        ),
        out_specs=(P(None, None, "tensor"), P(None, None, "tensor"), P("dp", None, "tensor")),
        check_vma=False,
    )
```

```python
import math

import jax
import jax.numpy as jnp
from jax import lax
from jax.experimental import pallas as pl
from jax.experimental.pallas import tpu as pltpu
from jax.sharding import PartitionSpec as P

MESH = pl.DeviceIdType.MESH
F32 = jnp.float32
BF16 = jnp.bfloat16

N_TP = 16
N_Y = 8
N_CHIP = 16
RANK = 64
SEQ_DEV = 8
SEQ_LEN = 32
TOK = SEQ_DEV * SEQ_LEN
FEAT = 512
ROWS = 8
STEPS = 4
CACHE_DEV = 48
KVH = 8
HD = 128
UP_OWNERS = (5, 10)
VMEM_LIMIT = 60 * 1024 * 1024

adapter_scale = 2.0
step_size = 0.004
masked_score = -1e30
score_scale = 1.0 / math.sqrt(HD)

(REW, GID, COT, UP, X, DOWN, HID, FRO, LEN, QRY, KEY, VAL) = range(12)
(
    RS1B,
    RS1P,
    AG1B,
    AG1P,
    XC,
    WC,
    HC,
    RS2,
    RS2U,
    AG2,
    AG2U,
    BASEY,
    BASEZ,
    BASEP,
    MIXY,
    STATY,
    MIXZ,
    STATZ,
    LOW,
    DOWNC,
    UPC,
    UPX,
    N_CHAN,
) = range(23)


def dot(a, b):
    return lax.dot_general(a, b, (((1,), (0,)), ((), ())), preferred_element_type=F32)


def dot_nt(a, b):
    return lax.dot_general(a, b, (((1,), (1,)), ((), ())), preferred_element_type=F32)


def iota(shape, axis):
    return lax.broadcasted_iota(jnp.int32, shape, axis)


def fold(a):
    n = a.shape[0] // 2
    return jnp.concatenate([a[:n], a[n:]], axis=1)


def unfold(a):
    return jnp.concatenate([a[:, :RANK], a[:, RANK:]], axis=0)


def by_tiles(tiles):
    return jnp.concatenate(
        [jnp.concatenate([tiles[r, 0], tiles[r, 1]], axis=1) for r in range(4)], axis=0
    )


def kernel(
    rew_h,
    gid_h,
    len_h,
    x_h,
    cot_h,
    down_h,
    up_h,
    hid_h,
    fro_h,
    q_h,
    k_h,
    v_h,
    od_h,
    ou_h,
    oa_h,
    rew,
    gid,
    lens,
    x,
    cot,
    down,
    up,
    hid,
    fro,
    qry,
    key,
    val,
    od,
    ou,
    oa,
    x_c,
    wt,
    wt_c,
    hid_c,
    hid_f,
    pb_send,
    rs1,
    ag1_send,
    ag1,
    g_send,
    rs2,
    ag2,
    ag2_c,
    gu_send,
    rs2u,
    agu,
    agu_c,
    base_send,
    base_r,
    basez_send,
    basez_r,
    basep_send,
    basep_r,
    mix_send,
    mix_r,
    mixz_send,
    mixz_r,
    st_send,
    st_r,
    stz_send,
    stz_r,
    low_send,
    low_r,
    upx_send,
    upx_r,
    qp,
    in_sem,
    out_sem,
    send,
    recv,
):
    dp = lax.axis_index("dp")
    tp = lax.axis_index("tensor")
    chip = lax.div(dp, 2)
    core = lax.rem(dp, 2)
    z_hi = lax.div(tp, N_Y)
    y = lax.rem(tp, N_Y)
    middle = 2 * (chip + 2 - 4 * lax.rem(lax.div(chip, 2), 2))
    other_core = 2 * chip + 1 - core
    pair = tp + 1 - 2 * lax.rem(tp, 2)
    other_half = y + N_Y * (1 - z_hi)

    barrier = pltpu.get_barrier_semaphore()

    def greet(device):
        pl.semaphore_signal(barrier, inc=1, device_id=device, device_id_type=MESH)

    def greet_middle(s, c):
        t = lax.rem(tp + s, N_TP)
        greet({"dp": middle + core, "tensor": t})
        greet({"dp": middle + 1 - core, "tensor": t})
        return c

    def greet_chips(s, c):
        greet({"dp": 2 * lax.rem(chip + s, N_CHIP) + core})
        return c

    lax.fori_loop(0, N_TP, greet_middle, 0)
    lax.fori_loop(1, N_CHIP, greet_chips, 0)
    greet({"dp": other_core})

    hbm = (rew_h, gid_h, cot_h, up_h, x_h, down_h, hid_h, fro_h, len_h, q_h, k_h, v_h)
    own = (rew, gid, cot, up, x, down, hid, fro, lens, qry, key, val)
    loads = [pltpu.make_async_copy(h, v, in_sem.at[n]) for n, (h, v) in enumerate(zip(hbm, own))]
    for load in loads:
        load.start()

    def remote(src, dst, chan, device):
        return pltpu.make_async_remote_copy(
            src_ref=src,
            dst_ref=dst,
            send_sem=send.at[chan],
            recv_sem=recv.at[chan],
            device_id=device,
            device_id_type=MESH,
        )

    def each(first, last, step):
        def body(s, c):
            step(s)
            return c

        lax.fori_loop(first, last, body, 0)

    def landed(ref, chan):
        pltpu.make_async_copy(ref, ref, recv.at[chan]).wait()

    def sent(ref, chan):
        pltpu.make_async_copy(ref, ref, send.at[chan]).wait()

    def summed(first, ref, start, stop):
        return lax.fori_loop(start, stop, lambda s, acc: acc + ref[s].astype(F32), first)

    loads[REW].wait()
    loads[GID].wait()
    lane_seq = lax.div(iota((1, TOK), 1), SEQ_LEN)
    rew_l = jnp.zeros((1, TOK), F32)
    gid_l = jnp.zeros((1, TOK), jnp.int32)
    for s in range(SEQ_DEV):
        rew_l = jnp.where(lane_seq == s, rew[s], rew_l)
        gid_l = jnp.where(lane_seq == s, gid[s], gid_l)
    cnt = jnp.zeros((1, TOK), F32)
    tot = jnp.zeros((1, TOK), F32)
    for s in range(SEQ_DEV):
        same = gid_l == gid[s]
        cnt = cnt + jnp.where(same, 1.0, 0.0)
        tot = tot + jnp.where(same, rew[s], 0.0)
    mean = tot / cnt
    spread = jnp.zeros((1, TOK), F32)
    for s in range(SEQ_DEV):
        off = rew[s] - mean
        spread = spread + jnp.where(gid_l == gid[s], off * off, 0.0)
    adv = (rew_l - mean) / jnp.maximum(jnp.sqrt(spread / cnt), 1.0)
    token_weight = adv / SEQ_LEN

    def put_pieces(part, k, product):
        product = product.astype(BF16)
        for r in range(4):
            for half in range(2):
                pb_send[part, (4 * k + r) * 2 + half] = product[
                    16 * r : 16 * (r + 1), 128 * half : 128 * (half + 1)
                ]

    loads[COT].wait()
    loads[UP].wait()
    for k in range(2):
        wt[k] = (cot[RANK * k : RANK * (k + 1)].astype(F32) * token_weight).astype(BF16)
        put_pieces(0, k, dot(up[k].astype(BF16), wt[k]))
    loads[X].wait()
    loads[DOWN].wait()
    for k in range(2):
        put_pieces(1, k, dot_nt(down[k].astype(BF16), x[...]))
    loads[HID].wait()

    pl.semaphore_wait(barrier, 2 * N_TP + N_CHIP)

    for part, chan in ((0, RS1B), (1, RS1P)):

        def send_piece(s, part=part, chan=chan):
            t = lax.rem(tp + s, N_TP)
            device = {"dp": middle + core, "tensor": t}
            remote(pb_send.at[part, t], rs1.at[part, s], chan, device).start()

        each(0, N_TP, send_piece)
    to_core = {"dp": other_core}
    remote(wt.at[1 - core], wt_c, WC, to_core).start()
    remote(x, x_c, XC, to_core).start()
    remote(hid, hid_c, HC, to_core).start()

    for i in range(ROWS):
        hid_f[STEPS * i : STEPS * (i + 1), :] = hid[i].astype(F32)
    hid_b = hid_f[...].astype(BF16)
    loads[FRO].wait()
    for part in range(4):
        cols = slice(part * 256, (part + 1) * 256)
        new_k = dot(hid_b, fro[0, :, cols]).astype(BF16)
        new_v = dot(hid_b, fro[1, :, cols]).astype(BF16)
        for n in range(4):
            half = slice(RANK * n, RANK * (n + 1))
            base_send[4 * part + n] = jnp.concatenate([new_k[:, half], new_v[:, half]], axis=1)

    loads[LEN].wait()
    loads[QRY].wait()
    loads[KEY].wait()
    loads[VAL].wait()
    out_row = iota((128, 128), 0)
    head = 2 * lax.div(out_row, 8) + lax.rem(lax.div(out_row, STEPS), 2)
    source = lax.rem(out_row, STEPS) * 32 + head
    perm = jnp.where(iota((128, 128), 1) == source, 1.0, 0.0).astype(BF16)
    lane_n = iota((128, CACHE_DEV * KVH), 1)
    own_group = lax.rem(lane_n, KVH) == lax.div(iota((128, CACHE_DEV * KVH), 0), 16)
    position = tp * CACHE_DEV + lax.div(lane_n, KVH)
    st_lane = iota((128, 128), 1)

    def attend(i, stats):
        q = dot(perm, qry[i])
        qp[i] = q
        score = dot_nt(q.astype(BF16), key[i]) * score_scale
        valid = jnp.logical_and(own_group, position < lens[i])
        score = jnp.where(valid, score, masked_score)
        high = jnp.max(score, axis=1, keepdims=True)
        weight = jnp.where(valid, jnp.exp(score - high), 0.0)
        total = jnp.sum(weight, axis=1, keepdims=True)
        mix = dot(weight.astype(BF16), val[i])
        stats = jnp.where(st_lane == i, high, stats)
        stats = jnp.where(st_lane == i + ROWS, total, stats)
        return mix.reshape(N_TP, 8, HD), stats

    def attend_pair(n, stats):
        m0, stats = attend(2 * n, stats)
        m1, stats = attend(2 * n + 1, stats)
        mix_send[:, pl.ds(pl.multiple_of(16 * n, 16), 16), :] = jnp.concatenate(
            [m0, m1], axis=1
        ).astype(BF16)
        return stats

    stats = lax.fori_loop(0, 4, attend_pair, jnp.zeros((128, 128), F32))
    st_send[...] = stats.reshape(N_TP, 8, 128)

    owned_k = lax.div(tp, N_Y)
    owned_r = lax.div(lax.rem(tp, N_Y), 2)
    owned_half = lax.rem(tp, 2)
    for part, chan_in, chan_out in ((0, RS1B, AG1B), (1, RS1P, AG1P)):
        landed(rs1.at[part], chan_in)
        ag1_send[part] = summed(jnp.zeros((16, 128), F32), rs1.at[part], 0, N_TP).astype(BF16)

        def send_sum(s, part=part, chan=chan_out):
            device = {"dp": middle + owned_k, "tensor": lax.rem(tp + s, N_TP)}
            remote(
                ag1_send.at[part], ag1.at[part, core, owned_r, owned_half], chan, device
            ).start()

        each(0, N_TP, send_sum)

    landed(x_c, XC)
    landed(wt_c, WC)
    landed(hid_c, HC)

    landed(ag1.at[0], AG1B)

    g_down = dot(by_tiles(ag1[0, core]), x[...]) + dot(by_tiles(ag1[0, 1 - core]), x_c[...])
    g_down = g_down.astype(BF16)
    for n in range(N_CHIP):
        r, c = n // 4, n % 4
        g_send[n] = g_down[16 * r : 16 * (r + 1), 128 * c : 128 * (c + 1)]

    def send_tile(s):
        q = lax.rem(chip + s, N_CHIP)
        remote(g_send.at[q], rs2.at[s - 1], RS2, {"dp": 2 * q + core}).start()

    each(1, N_CHIP, send_tile)

    landed(ag1.at[1], AG1P)

    g_up = dot_nt(by_tiles(ag1[1, core]), wt[core]) + dot_nt(by_tiles(ag1[1, 1 - core]), wt_c[...])
    gu_send[...] = fold(g_up).astype(BF16).reshape(2, 16, 128)
    for u, q in enumerate(UP_OWNERS):

        @pl.when(chip != q)
        def _(u=u, q=q):
            slot = lax.rem(q - chip + N_CHIP, N_CHIP) - 1
            remote(gu_send.at[u], rs2u.at[slot], RS2U, {"dp": 2 * q + core}).start()

    def send_along_y(s):
        to = lax.rem(y + s, N_Y)
        device = {"tensor": N_Y * z_hi + to}
        for z in range(2):
            t = N_Y * z + to
            remote(base_send.at[t], base_r.at[s - 1, z], BASEY, device).start()

    def send_mix_along_y(s):
        to = lax.rem(y + s, N_Y)
        device = {"tensor": N_Y * z_hi + to}
        for z in range(2):
            t = N_Y * z + to
            remote(st_send.at[t], st_r.at[s - 1, z], STATY, device).start()
            remote(mix_send.at[t], mix_r.at[s - 1, z], MIXY, device).start()

    each(1, N_Y, send_along_y)
    each(1, N_Y, send_mix_along_y)
    for i in range(ROWS):
        hid_f[STEPS * i : STEPS * (i + 1), :] = hid_c[i].astype(F32)
    hid_cb = hid_f[...].astype(BF16)

    landed(rs2, RS2)

    ag2[chip] = summed(g_send[chip].astype(F32), rs2, 0, N_CHIP - 1).astype(BF16)

    def send_total(s):
        q = lax.rem(chip + s, N_CHIP)
        remote(ag2.at[chip], ag2.at[chip], AG2, {"dp": 2 * q + core}).start()

    each(1, N_CHIP, send_total)

    is_owner = jnp.logical_or(chip == UP_OWNERS[0], chip == UP_OWNERS[1])
    up_tile = jnp.where(chip == UP_OWNERS[0], 0, 1)

    @pl.when(is_owner)
    def _():
        landed(rs2u, RS2U)
        agu[up_tile] = summed(gu_send[up_tile].astype(F32), rs2u, 0, N_CHIP - 1).astype(BF16)

        def send_up(s):
            q = lax.rem(chip + s, N_CHIP)
            remote(agu.at[up_tile], agu.at[up_tile], AG2U, {"dp": 2 * q + core}).start()

        each(1, N_CHIP, send_up)

    landed(base_r, BASEY)

    def base_sum(z):
        first = base_send[N_Y * z + y].astype(F32)
        return lax.fori_loop(
            0, N_Y - 1, lambda s, acc: acc + base_r[s, z].astype(F32), first
        )

    to_half = {"tensor": other_half}
    basez_send[...] = base_sum(1 - z_hi)
    remote(basez_send, basez_r, BASEZ, to_half).start()
    base = base_sum(z_hi)

    landed(ag2.at[pl.ds(0, N_CHIP - 1)], AG2)

    def tiles_of(ref):
        return jnp.concatenate(
            [jnp.concatenate([ref[4 * r + c] for c in range(4)], axis=1) for r in range(4)], axis=0
        ).astype(F32)

    new_down = down[core] + step_size * (adapter_scale * tiles_of(ag2))
    roll_down = new_down.astype(BF16)
    low_send[0] = fold(dot_nt(hid_b, roll_down)).astype(BF16)
    low_send[1] = fold(dot_nt(hid_cb, roll_down)).astype(BF16)

    def send_low(s):
        t = lax.rem(tp + s, N_TP)
        remote(low_send.at[0], low_r.at[s], LOW, {"tensor": t}).start()
        remote(
            low_send.at[1], low_r.at[N_TP + s], LOW, {"dp": other_core, "tensor": t}
        ).start()

    each(1, N_TP, send_low)
    remote(low_send.at[1], low_r.at[N_TP], LOW, to_core).start()
    remote(ag2, ag2_c, DOWNC, to_core).start()
    od[core] = new_down

    @pl.when(is_owner)
    def _():
        landed(agu.at[0], AG2U)

    @pl.when(jnp.logical_not(is_owner))
    def _():
        landed(agu, AG2U)

    def up_updated(k, grad):
        return up[k] + step_size * (adapter_scale * unfold(grad.reshape(32, 128)).astype(F32))

    new_up = up_updated(core, agu[...])
    upx_send[...] = fold(new_up).astype(BF16).reshape(2, 16, 128)
    remote(agu, agu_c, UPC, to_core).start()
    remote(upx_send, upx_r.at[0], UPX, {"tensor": pair}).start()
    remote(upx_send, upx_r.at[1], UPX, {"dp": other_core, "tensor": pair}).start()
    ou[core] = new_up

    landed(basez_r, BASEZ)
    base = base + basez_r[...]
    basep_send[...] = base
    remote(basep_send, basep_r, BASEP, {"tensor": pair}).start()

    landed(st_r, STATY)
    landed(mix_r, MIXY)

    def combine(st, mix, count):
        top = st(0)
        for s in range(1, count):
            top = jnp.maximum(top, st(s))
        total = jnp.zeros((8, 128), F32)
        acc = [jnp.zeros((8, 128), F32)] * ROWS
        for s in range(count):
            factor = jnp.exp(st(s) - top)
            total = total + factor * pltpu.roll(st(s), 128 - ROWS, 1)
            block = mix(s)
            for i in range(ROWS):
                acc[i] = acc[i] + factor[:, i : i + 1] * block[8 * i : 8 * (i + 1)].astype(F32)
        return top, total, acc

    def combine_y(z):
        t = N_Y * z + y
        return combine(
            lambda s: st_send[t] if s == 0 else st_r[s - 1, z],
            lambda s: mix_send[t] if s == 0 else mix_r[s - 1, z],
            N_Y,
        )

    def packed(top, total):
        return jnp.where(iota((8, 128), 1) < ROWS, top, pltpu.roll(total, ROWS, 1))

    top, total, acc = combine_y(1 - z_hi)
    stz_send[...] = packed(top, total)
    remote(stz_send, stz_r, STATZ, to_half).start()
    mixz_send[...] = jnp.concatenate(acc, axis=0).astype(BF16)
    remote(mixz_send, mixz_r, MIXZ, to_half).start()
    top, total, acc = combine_y(z_hi)
    own_st = packed(top, total)
    own_mix = jnp.concatenate(acc, axis=0)

    landed(ag2_c, DOWNC)
    od[1 - core] = down[1 - core] + step_size * (adapter_scale * tiles_of(ag2_c))
    store_down = pltpu.make_async_copy(od, od_h, out_sem.at[0])
    store_down.start()
    landed(agu_c, UPC)
    new_up_c = up_updated(1 - core, agu_c[...])
    ou[1 - core] = new_up_c
    store_up = pltpu.make_async_copy(ou, ou_h, out_sem.at[1])
    store_up.start()

    landed(upx_r, UPX)
    even = lax.rem(tp, 2) == 0

    def both(mine, theirs):
        left = jnp.where(even, mine, theirs)
        right = jnp.where(even, theirs, mine)
        return jnp.concatenate([left, right], axis=1)

    def columns(mine, theirs):
        return both(mine, unfold(theirs.reshape(32, 128)).astype(F32)).astype(BF16)

    up_own = columns(new_up, upx_r[0])
    up_oth = columns(new_up_c, upx_r[1])
    landed(basep_r, BASEP)
    base_k = both(base[:, :RANK], basep_r[:, :RANK])
    base_v = both(base[:, RANK:], basep_r[:, RANK:])

    landed(stz_r, STATZ)
    landed(mixz_r, MIXZ)
    top, total, acc = combine(
        lambda s: stz_r[...] if s else own_st, lambda s: mixz_r[...] if s else own_mix, 2
    )
    old_high = jnp.concatenate([top[:, i : i + 1] for i in range(ROWS)], axis=0)
    old_total = jnp.concatenate([total[:, i : i + 1] for i in range(ROWS)], axis=0)
    old_mix = jnp.concatenate(acc, axis=0)
    own_q = qp[:, pl.ds(pl.multiple_of(8 * tp, 8), 8), :].reshape(64, HD).astype(BF16)

    landed(low_r.at[pl.ds(1, 2 * N_TP - 1)], LOW)

    low_own = unfold(summed(low_send[0].astype(F32), low_r, 1, N_TP)).astype(BF16)
    low_oth = unfold(summed(jnp.zeros((16, 128), F32), low_r, N_TP, 2 * N_TP)).astype(BF16)
    from_own = adapter_scale * dot(low_own, up_own)
    from_oth = adapter_scale * dot(low_oth, up_oth)
    first = core == 0
    new_k = (base_k + jnp.where(first, from_own, from_oth)).astype(BF16)
    new_v = (base_v + jnp.where(first, from_oth, from_own)).astype(BF16)
    row = iota((64, 32), 0)
    col = iota((64, 32), 1)
    causal = jnp.logical_and(
        lax.div(row, 8) == lax.div(col, STEPS), lax.rem(col, STEPS) <= lax.rem(row, STEPS)
    )
    score = jnp.where(causal, dot_nt(own_q, new_k) * score_scale, masked_score)
    new_high = jnp.max(score, axis=1, keepdims=True)
    weight = jnp.where(causal, jnp.exp(score - new_high), 0.0)
    new_total = jnp.sum(weight, axis=1, keepdims=True)
    new_mix = dot(weight.astype(BF16), new_v)
    highest = jnp.maximum(old_high, new_high)
    f_old = jnp.exp(old_high - highest)
    f_new = jnp.exp(new_high - highest)
    out = (f_old * old_mix + f_new * new_mix) / (f_old * old_total + f_new * new_total)
    out = out.reshape(ROWS, 8, HD)
    oa[:, :, 0:HD] = out[:, 0:STEPS].astype(BF16)
    oa[:, :, HD:] = out[:, STEPS:].astype(BF16)
    store_att = pltpu.make_async_copy(oa, oa_h, out_sem.at[2])
    store_att.start()

    for ref, chan in (
        (rs1.at[0], RS1B),
        (rs1.at[1], RS1P),
        (ag1.at[0], AG1B),
        (ag1.at[1], AG1P),
        (x_c, XC),
        (wt_c, WC),
        (hid_c, HC),
        (rs2, RS2),
        (rs2, AG2),
        (base_r, BASEY),
        (basez_r, BASEZ),
        (basep_r, BASEP),
        (mix_r, MIXY),
        (st_r, STATY),
        (mixz_r, MIXZ),
        (stz_r, STATZ),
        (low_r.at[pl.ds(1, 2 * N_TP - 1)], LOW),
        (ag2_c, DOWNC),
        (agu_c, UPC),
        (upx_r, UPX),
    ):
        sent(ref, chan)

    @pl.when(is_owner)
    def _():
        sent(agu.at[0], RS2U)
        sent(rs2u, AG2U)

    @pl.when(jnp.logical_not(is_owner))
    def _():
        sent(agu, RS2U)

    store_down.wait()
    store_up.wait()
    store_att.wait()


def shards(
    learn_input,
    cotangent,
    rewards,
    group_ids,
    adapter_down,
    adapter_up,
    frozen_weight,
    hidden,
    queries,
    key_cache,
    value_cache,
    cache_lengths,
):
    hbm = pl.BlockSpec(memory_space=pltpu.HBM)
    operands = (
        learn_input,
        jnp.transpose(cotangent, (1, 2, 0)).reshape(128, TOK),
        adapter_down,
        adapter_up,
        hidden,
        frozen_weight,
        queries.reshape(ROWS, 128, HD),
        key_cache.reshape(ROWS, CACHE_DEV * KVH, HD),
        value_cache.reshape(ROWS, CACHE_DEV * KVH, HD),
    )
    out_shape = (
        jax.ShapeDtypeStruct((2, RANK, FEAT), F32),
        jax.ShapeDtypeStruct((2, RANK, RANK), F32),
        jax.ShapeDtypeStruct((ROWS, STEPS, 2 * HD), BF16),
    )
    return pl.pallas_call(
        kernel,
        out_shape=out_shape,
        in_specs=[hbm] * 12,
        out_specs=(hbm,) * 3,
        scratch_shapes=[
            pltpu.SMEM((SEQ_DEV,), F32),
            pltpu.SMEM((SEQ_DEV,), jnp.int32),
            pltpu.SMEM((ROWS,), jnp.int32),
        ]
        + [pltpu.VMEM(o.shape, o.dtype) for o in operands + out_shape]
        + [
            pltpu.VMEM((TOK, FEAT), BF16),
            pltpu.VMEM((2, RANK, TOK), BF16),
            pltpu.VMEM((RANK, TOK), BF16),
            pltpu.VMEM((ROWS, STEPS, FEAT), BF16),
            pltpu.VMEM((ROWS * STEPS, FEAT), F32),
            pltpu.VMEM((2, 16, 16, 128), BF16),
            pltpu.VMEM((2, 16, 16, 128), BF16),
            pltpu.VMEM((2, 16, 128), BF16),
            pltpu.VMEM((2, 2, 4, 2, 16, 128), BF16),
            pltpu.VMEM((16, 16, 128), BF16),
            pltpu.VMEM((15, 16, 128), BF16),
            pltpu.VMEM((16, 16, 128), BF16),
            pltpu.VMEM((16, 16, 128), BF16),
            pltpu.VMEM((2, 16, 128), BF16),
            pltpu.VMEM((15, 16, 128), BF16),
            pltpu.VMEM((2, 16, 128), BF16),
            pltpu.VMEM((2, 16, 128), BF16),
            pltpu.VMEM((16, 32, 128), BF16),
            pltpu.VMEM((7, 2, 32, 128), BF16),
            pltpu.VMEM((32, 128), F32),
            pltpu.VMEM((32, 128), F32),
            pltpu.VMEM((32, 128), F32),
            pltpu.VMEM((32, 128), F32),
            pltpu.VMEM((16, 64, HD), BF16),
            pltpu.VMEM((7, 2, 64, HD), BF16),
            pltpu.VMEM((64, HD), BF16),
            pltpu.VMEM((64, HD), BF16),
            pltpu.VMEM((16, 8, 128), F32),
            pltpu.VMEM((7, 2, 8, 128), F32),
            pltpu.VMEM((8, 128), F32),
            pltpu.VMEM((8, 128), F32),
            pltpu.VMEM((2, 16, 128), BF16),
            pltpu.VMEM((32, 16, 128), BF16),
            pltpu.VMEM((2, 16, 128), BF16),
            pltpu.VMEM((2, 2, 16, 128), BF16),
            pltpu.VMEM((ROWS, 128, HD), F32),
            pltpu.SemaphoreType.DMA((12,)),
            pltpu.SemaphoreType.DMA((3,)),
            pltpu.SemaphoreType.DMA((N_CHAN,)),
            pltpu.SemaphoreType.DMA((N_CHAN,)),
        ],
        compiler_params=pltpu.CompilerParams(
            collective_id=0, has_side_effects=True, vmem_limit_bytes=VMEM_LIMIT
        ),
    )(rewards, group_ids, cache_lengths, *operands)


def solution(mesh):
    return jax.shard_map(
        shards,
        mesh=mesh,
        in_specs=(
            P("dp", "tensor"),
            P("dp", None, "tensor"),
            P("dp"),
            P("dp"),
            P(None, None, "tensor"),
            P(None, None, "tensor"),
            P(None, "tensor", None),
            P("dp", None, "tensor"),
            P("dp", None, None, None),
            P("dp", "tensor", None, None),
            P("dp", "tensor", None, None),
            P("dp"),
        ),
        out_specs=(P(None, None, "tensor"), P(None, None, "tensor"), P("dp", None, "tensor")),
        check_vma=False,
    )
```

```python
import math

import jax
import jax.numpy as jnp
from jax import lax
from jax.experimental import pallas as pl
from jax.experimental.pallas import tpu as pltpu
from jax.sharding import PartitionSpec as P

MESH = pl.DeviceIdType.MESH
F32 = jnp.float32
BF16 = jnp.bfloat16

N_TP = 16
N_Y = 8
N_CHIP = 16
RANK = 64
SEQ_DEV = 8
SEQ_LEN = 32
TOK = SEQ_DEV * SEQ_LEN
FEAT = 512
ROWS = 8
STEPS = 4
CACHE_DEV = 48
KVH = 8
HD = 128
UP_OWNERS = (5, 10)
VMEM_LIMIT = 32 * 1024 * 1024

adapter_scale = 2.0
step_size = 0.004
masked_score = -1e30
score_scale = 1.0 / math.sqrt(HD)

(REW, GID, COT, UP, X, DOWN, HID, FRO, LEN, QRY, KEY, VAL) = range(12)
(
    RS1B,
    RS1P,
    AG1B,
    AG1P,
    XC,
    WC,
    HC,
    RS2,
    RS2U,
    AG2,
    AG2U,
    BASEY,
    BASEZ,
    BASEP,
    MIXY,
    STATY,
    MIXZ,
    STATZ,
    LOW,
    DOWNC,
    UPC,
    UPX,
    N_CHAN,
) = range(23)


def dot(a, b):
    return lax.dot_general(a, b, (((1,), (0,)), ((), ())), preferred_element_type=F32)


def dot_nt(a, b):
    return lax.dot_general(a, b, (((1,), (1,)), ((), ())), preferred_element_type=F32)


def iota(shape, axis):
    return lax.broadcasted_iota(jnp.int32, shape, axis)


def fold(a):
    n = a.shape[0] // 2
    return jnp.concatenate([a[:n], a[n:]], axis=1)


def unfold(a):
    return jnp.concatenate([a[:, :RANK], a[:, RANK:]], axis=0)


def by_tiles(tiles):
    return jnp.concatenate(
        [jnp.concatenate([tiles[r, 0], tiles[r, 1]], axis=1) for r in range(4)], axis=0
    )


def kernel(
    rew_h,
    gid_h,
    len_h,
    x_h,
    cot_h,
    down_h,
    up_h,
    hid_h,
    fro_h,
    q_h,
    k_h,
    v_h,
    od,
    ou,
    oa,
    rew,
    gid,
    lens,
    x,
    cot,
    down,
    up,
    hid,
    fro,
    qry,
    key,
    val,
    x_c,
    wt,
    wt_c,
    hid_c,
    hid_f,
    pb_send,
    rs1,
    ag1_send,
    ag1,
    g_send,
    rs2,
    ag2,
    ag2_c,
    gu_send,
    rs2u,
    agu,
    agu_c,
    base_send,
    base_r,
    basez_send,
    basez_r,
    basep_send,
    basep_r,
    mix_send,
    mix_r,
    mixz_send,
    mixz_r,
    st_send,
    st_r,
    stz_send,
    stz_r,
    low_send,
    low_r,
    upx_send,
    upx_r,
    qp,
    in_sem,
    send,
    recv,
):
    dp = lax.axis_index("dp")
    tp = lax.axis_index("tensor")
    chip = lax.div(dp, 2)
    core = lax.rem(dp, 2)
    z_hi = lax.div(tp, N_Y)
    y = lax.rem(tp, N_Y)
    middle = 2 * (chip + 2 - 4 * lax.rem(lax.div(chip, 2), 2))
    other_core = 2 * chip + 1 - core
    pair = tp + 1 - 2 * lax.rem(tp, 2)
    other_half = y + N_Y * (1 - z_hi)

    hbm = (rew_h, gid_h, cot_h, up_h, x_h, down_h, hid_h, fro_h, len_h, q_h, k_h, v_h)
    own = (rew, gid, cot, up, x, down, hid, fro, lens, qry, key, val)
    loads = [pltpu.make_async_copy(h, v, in_sem.at[n]) for n, (h, v) in enumerate(zip(hbm, own))]
    for load in loads:
        load.start()

    ys = [lax.rem(y + o, N_Y) for o in (4, 3, 5, 2, 6, 1, 7, 0)]
    tps = [N_Y * h + t for t in ys for h in (1 - z_hi, z_hi)]
    chips = [lax.rem(chip + o, N_CHIP) for o in (8, 7, 9, 6, 10, 5, 11, 4, 12, 3, 13, 2, 14, 1, 15)]

    barrier = pltpu.get_barrier_semaphore()

    def greet(device):
        pl.semaphore_signal(barrier, inc=1, device_id=device, device_id_type=MESH)

    for t in tps:
        greet({"dp": middle + core, "tensor": t})
    for q in chips:
        greet({"dp": 2 * q + core})
    greet({"dp": other_core})

    def remote(src, dst, chan, device):
        return pltpu.make_async_remote_copy(
            src_ref=src,
            dst_ref=dst,
            send_sem=send.at[chan],
            recv_sem=recv.at[chan],
            device_id=device,
            device_id_type=MESH,
        )

    def landed(ref, chan):
        pltpu.make_async_copy(ref, ref, recv.at[chan]).wait()

    def sent(ref, chan):
        pltpu.make_async_copy(ref, ref, send.at[chan]).wait()

    def summed(first, ref, start, stop):
        return lax.fori_loop(start, stop, lambda s, acc: acc + ref[s].astype(F32), first)

    loads[REW].wait()
    loads[GID].wait()
    lane_seq = lax.div(iota((1, TOK), 1), SEQ_LEN)
    rew_l = jnp.zeros((1, TOK), F32)
    gid_l = jnp.zeros((1, TOK), jnp.int32)
    for s in range(SEQ_DEV):
        rew_l = jnp.where(lane_seq == s, rew[s], rew_l)
        gid_l = jnp.where(lane_seq == s, gid[s], gid_l)
    cnt = jnp.zeros((1, TOK), F32)
    tot = jnp.zeros((1, TOK), F32)
    for s in range(SEQ_DEV):
        same = gid_l == gid[s]
        cnt = cnt + jnp.where(same, 1.0, 0.0)
        tot = tot + jnp.where(same, rew[s], 0.0)
    mean = tot / cnt
    spread = jnp.zeros((1, TOK), F32)
    for s in range(SEQ_DEV):
        off = rew[s] - mean
        spread = spread + jnp.where(gid_l == gid[s], off * off, 0.0)
    adv = (rew_l - mean) / jnp.maximum(jnp.sqrt(spread / cnt), 1.0)
    token_weight = adv / SEQ_LEN

    def put_pieces(part, k, product):
        product = product.astype(BF16)
        for r in range(4):
            for half in range(2):
                pb_send[part, (4 * k + r) * 2 + half] = product[
                    16 * r : 16 * (r + 1), 128 * half : 128 * (half + 1)
                ]

    loads[COT].wait()
    loads[UP].wait()
    for k in range(2):
        wt[k] = (cot[RANK * k : RANK * (k + 1)].astype(F32) * token_weight).astype(BF16)
        put_pieces(0, k, dot(up[k].astype(BF16), wt[k]))

    pl.semaphore_wait(barrier, N_TP + N_CHIP)

    def send_pieces(part, chan):
        for s, t in enumerate(tps):
            device = {"dp": middle + core, "tensor": t}
            remote(pb_send.at[part, t], rs1.at[part, s], chan, device).start()

    send_pieces(0, RS1B)
    loads[X].wait()
    loads[DOWN].wait()
    for k in range(2):
        put_pieces(1, k, dot_nt(down[k].astype(BF16), x[...]))
    send_pieces(1, RS1P)
    loads[HID].wait()
    to_core = {"dp": other_core}
    remote(wt.at[1 - core], wt_c, WC, to_core).start()
    remote(x, x_c, XC, to_core).start()
    remote(hid, hid_c, HC, to_core).start()

    for i in range(ROWS):
        hid_f[STEPS * i : STEPS * (i + 1), :] = hid[i].astype(F32)
    hid_b = hid_f[...].astype(BF16)
    loads[FRO].wait()
    for part in range(4):
        cols = slice(part * 256, (part + 1) * 256)
        new_k = dot(hid_b, fro[0, :, cols]).astype(BF16)
        new_v = dot(hid_b, fro[1, :, cols]).astype(BF16)
        for n in range(4):
            half = slice(RANK * n, RANK * (n + 1))
            base_send[4 * part + n] = jnp.concatenate([new_k[:, half], new_v[:, half]], axis=1)

    loads[LEN].wait()
    loads[QRY].wait()
    loads[KEY].wait()
    loads[VAL].wait()
    out_row = iota((128, 128), 0)
    head = 2 * lax.div(out_row, 8) + lax.rem(lax.div(out_row, STEPS), 2)
    source = lax.rem(out_row, STEPS) * 32 + head
    perm = jnp.where(iota((128, 128), 1) == source, 1.0, 0.0).astype(BF16)
    lane_n = iota((128, CACHE_DEV * KVH), 1)
    own_group = lax.rem(lane_n, KVH) == lax.div(iota((128, CACHE_DEV * KVH), 0), 16)
    position = tp * CACHE_DEV + lax.div(lane_n, KVH)
    st_lane = iota((128, 128), 1)

    def attend(i, stats):
        q = dot(perm, qry[i])
        qp[i] = q
        score = dot_nt(q.astype(BF16), key[i]) * score_scale
        valid = jnp.logical_and(own_group, position < lens[i])
        score = jnp.where(valid, score, masked_score)
        high = jnp.max(score, axis=1, keepdims=True)
        weight = jnp.where(valid, jnp.exp(score - high), 0.0)
        total = jnp.sum(weight, axis=1, keepdims=True)
        mix = dot(weight.astype(BF16), val[i])
        stats = jnp.where(st_lane == i, high, stats)
        stats = jnp.where(st_lane == i + ROWS, total, stats)
        return mix.reshape(N_TP, 8, HD), stats

    def attend_pair(n, stats):
        m0, stats = attend(2 * n, stats)
        m1, stats = attend(2 * n + 1, stats)
        mix_send[:, pl.ds(pl.multiple_of(16 * n, 16), 16), :] = jnp.concatenate(
            [m0, m1], axis=1
        ).astype(BF16)
        return stats

    stats = lax.fori_loop(0, 4, attend_pair, jnp.zeros((128, 128), F32))
    st_send[...] = stats.reshape(N_TP, 8, 128)

    owned_k = lax.div(tp, N_Y)
    owned_r = lax.div(lax.rem(tp, N_Y), 2)
    owned_half = lax.rem(tp, 2)
    for part, chan_in, chan_out in ((0, RS1B, AG1B), (1, RS1P, AG1P)):
        landed(rs1.at[part], chan_in)
        ag1_send[part] = summed(jnp.zeros((16, 128), F32), rs1.at[part], 0, N_TP).astype(BF16)
        for t in tps:
            device = {"dp": middle + owned_k, "tensor": t}
            place = ag1.at[part, core, owned_r, owned_half]
            remote(ag1_send.at[part], place, chan_out, device).start()

    for s, to in enumerate(ys[:-1]):
        for z in range(2):
            t = N_Y * z + to
            device = {"tensor": N_Y * z_hi + to}
            remote(base_send.at[t], base_r.at[s, z], BASEY, device).start()

    landed(x_c, XC)
    landed(wt_c, WC)
    landed(hid_c, HC)

    landed(ag1.at[0], AG1B)

    g_down = dot(by_tiles(ag1[0, core]), x[...]) + dot(by_tiles(ag1[0, 1 - core]), x_c[...])
    g_down = g_down.astype(BF16)
    for n in range(N_CHIP):
        r, c = n // 4, n % 4
        g_send[n] = g_down[16 * r : 16 * (r + 1), 128 * c : 128 * (c + 1)]

    for s, q in enumerate(chips):
        remote(g_send.at[q], rs2.at[s], RS2, {"dp": 2 * q + core}).start()

    for s, to in enumerate(ys[:-1]):
        for z in range(2):
            t = N_Y * z + to
            device = {"tensor": N_Y * z_hi + to}
            remote(st_send.at[t], st_r.at[s, z], STATY, device).start()
            remote(mix_send.at[t], mix_r.at[s, z], MIXY, device).start()

    landed(ag1.at[1], AG1P)

    g_up = dot_nt(by_tiles(ag1[1, core]), wt[core]) + dot_nt(by_tiles(ag1[1, 1 - core]), wt_c[...])
    gu_send[...] = fold(g_up).astype(BF16).reshape(2, 16, 128)
    for u, q in enumerate(UP_OWNERS):

        @pl.when(chip != q)
        def _(u=u, q=q):
            slot = lax.rem(q - chip + N_CHIP, N_CHIP) - 1
            remote(gu_send.at[u], rs2u.at[slot], RS2U, {"dp": 2 * q + core}).start()

    for i in range(ROWS):
        hid_f[STEPS * i : STEPS * (i + 1), :] = hid_c[i].astype(F32)
    hid_cb = hid_f[...].astype(BF16)

    landed(rs2, RS2)

    ag2[chip] = summed(g_send[chip].astype(F32), rs2, 0, N_CHIP - 1).astype(BF16)

    for q in chips:
        remote(ag2.at[chip], ag2.at[chip], AG2, {"dp": 2 * q + core}).start()

    is_owner = jnp.logical_or(chip == UP_OWNERS[0], chip == UP_OWNERS[1])
    up_tile = jnp.where(chip == UP_OWNERS[0], 0, 1)

    @pl.when(is_owner)
    def _():
        landed(rs2u, RS2U)
        agu[up_tile] = summed(gu_send[up_tile].astype(F32), rs2u, 0, N_CHIP - 1).astype(BF16)
        for q in chips:
            remote(agu.at[up_tile], agu.at[up_tile], AG2U, {"dp": 2 * q + core}).start()

    landed(base_r, BASEY)

    def base_sum(z):
        first = base_send[N_Y * z + y].astype(F32)
        return lax.fori_loop(
            0, N_Y - 1, lambda s, acc: acc + base_r[s, z].astype(F32), first
        )

    to_half = {"tensor": other_half}
    basez_send[...] = base_sum(1 - z_hi)
    remote(basez_send, basez_r, BASEZ, to_half).start()
    base = base_sum(z_hi)

    landed(ag2.at[pl.ds(0, N_CHIP - 1)], AG2)

    def tiles_of(ref):
        return jnp.concatenate(
            [jnp.concatenate([ref[4 * r + c] for c in range(4)], axis=1) for r in range(4)], axis=0
        ).astype(F32)

    new_down = down[core] + step_size * (adapter_scale * tiles_of(ag2))
    roll_down = new_down.astype(BF16)
    low_send[0] = fold(dot_nt(hid_b, roll_down)).astype(BF16)
    low_send[1] = fold(dot_nt(hid_cb, roll_down)).astype(BF16)

    for s, t in enumerate(tps):
        if s < N_TP - 1:
            remote(low_send.at[0], low_r.at[s], LOW, {"tensor": t}).start()
        device = {"dp": other_core, "tensor": t}
        remote(low_send.at[1], low_r.at[N_TP - 1 + s], LOW, device).start()
    remote(ag2, ag2_c, DOWNC, to_core).start()
    od[core] = new_down

    @pl.when(is_owner)
    def _():
        landed(agu.at[0], AG2U)

    @pl.when(jnp.logical_not(is_owner))
    def _():
        landed(agu, AG2U)

    def up_updated(k, grad):
        return up[k] + step_size * (adapter_scale * unfold(grad.reshape(32, 128)).astype(F32))

    new_up = up_updated(core, agu[...])
    upx_send[...] = fold(new_up).astype(BF16).reshape(2, 16, 128)
    remote(agu, agu_c, UPC, to_core).start()
    remote(upx_send, upx_r.at[0], UPX, {"tensor": pair}).start()
    remote(upx_send, upx_r.at[1], UPX, {"dp": other_core, "tensor": pair}).start()
    ou[core] = new_up

    landed(basez_r, BASEZ)
    base = base + basez_r[...]
    basep_send[...] = base
    remote(basep_send, basep_r, BASEP, {"tensor": pair}).start()

    landed(st_r, STATY)
    landed(mix_r, MIXY)

    def combine(st, mix, count):
        top = st(0)
        for s in range(1, count):
            top = jnp.maximum(top, st(s))
        total = jnp.zeros((8, 128), F32)
        acc = [jnp.zeros((8, 128), F32)] * ROWS
        for s in range(count):
            factor = jnp.exp(st(s) - top)
            total = total + factor * pltpu.roll(st(s), 128 - ROWS, 1)
            block = mix(s)
            for i in range(ROWS):
                acc[i] = acc[i] + factor[:, i : i + 1] * block[8 * i : 8 * (i + 1)].astype(F32)
        return top, total, acc

    def combine_y(z):
        t = N_Y * z + y
        return combine(
            lambda s: st_send[t] if s == 0 else st_r[s - 1, z],
            lambda s: mix_send[t] if s == 0 else mix_r[s - 1, z],
            N_Y,
        )

    def packed(top, total):
        return jnp.where(iota((8, 128), 1) < ROWS, top, pltpu.roll(total, ROWS, 1))

    top, total, acc = combine_y(1 - z_hi)
    stz_send[...] = packed(top, total)
    remote(stz_send, stz_r, STATZ, to_half).start()
    mixz_send[...] = jnp.concatenate(acc, axis=0).astype(BF16)
    remote(mixz_send, mixz_r, MIXZ, to_half).start()
    top, total, acc = combine_y(z_hi)
    own_st = packed(top, total)
    own_mix = jnp.concatenate(acc, axis=0)

    landed(ag2_c, DOWNC)
    od[1 - core] = down[1 - core] + step_size * (adapter_scale * tiles_of(ag2_c))
    landed(agu_c, UPC)
    new_up_c = up_updated(1 - core, agu_c[...])
    ou[1 - core] = new_up_c

    landed(upx_r, UPX)
    even = lax.rem(tp, 2) == 0

    def both(mine, theirs):
        left = jnp.where(even, mine, theirs)
        right = jnp.where(even, theirs, mine)
        return jnp.concatenate([left, right], axis=1)

    def columns(mine, theirs):
        return both(mine, unfold(theirs.reshape(32, 128)).astype(F32)).astype(BF16)

    up_own = columns(new_up, upx_r[0])
    up_oth = columns(new_up_c, upx_r[1])
    landed(basep_r, BASEP)
    base_k = both(base[:, :RANK], basep_r[:, :RANK])
    base_v = both(base[:, RANK:], basep_r[:, RANK:])

    landed(stz_r, STATZ)
    landed(mixz_r, MIXZ)
    top, total, acc = combine(
        lambda s: stz_r[...] if s else own_st, lambda s: mixz_r[...] if s else own_mix, 2
    )
    old_high = jnp.concatenate([top[:, i : i + 1] for i in range(ROWS)], axis=0)
    old_total = jnp.concatenate([total[:, i : i + 1] for i in range(ROWS)], axis=0)
    old_mix = jnp.concatenate(acc, axis=0)
    own_q = qp[:, pl.ds(pl.multiple_of(8 * tp, 8), 8), :].reshape(64, HD).astype(BF16)

    landed(low_r, LOW)

    low_own = unfold(summed(low_send[0].astype(F32), low_r, 0, N_TP - 1)).astype(BF16)
    low_oth = unfold(summed(jnp.zeros((16, 128), F32), low_r, N_TP - 1, 2 * N_TP - 1)).astype(BF16)
    from_own = adapter_scale * dot(low_own, up_own)
    from_oth = adapter_scale * dot(low_oth, up_oth)
    first = core == 0
    new_k = (base_k + jnp.where(first, from_own, from_oth)).astype(BF16)
    new_v = (base_v + jnp.where(first, from_oth, from_own)).astype(BF16)
    row = iota((64, 32), 0)
    col = iota((64, 32), 1)
    causal = jnp.logical_and(
        lax.div(row, 8) == lax.div(col, STEPS), lax.rem(col, STEPS) <= lax.rem(row, STEPS)
    )
    score = jnp.where(causal, dot_nt(own_q, new_k) * score_scale, masked_score)
    new_high = jnp.max(score, axis=1, keepdims=True)
    weight = jnp.where(causal, jnp.exp(score - new_high), 0.0)
    new_total = jnp.sum(weight, axis=1, keepdims=True)
    new_mix = dot(weight.astype(BF16), new_v)
    highest = jnp.maximum(old_high, new_high)
    f_old = jnp.exp(old_high - highest)
    f_new = jnp.exp(new_high - highest)
    out = (f_old * old_mix + f_new * new_mix) / (f_old * old_total + f_new * new_total)
    out = out.reshape(ROWS, 8, HD)
    oa[:, :, 0:HD] = out[:, 0:STEPS].astype(BF16)
    oa[:, :, HD:] = out[:, STEPS:].astype(BF16)

    for ref, chan in (
        (rs1.at[0], RS1B),
        (rs1.at[1], RS1P),
        (ag1.at[0], AG1B),
        (ag1.at[1], AG1P),
        (x_c, XC),
        (wt_c, WC),
        (hid_c, HC),
        (rs2, RS2),
        (rs2, AG2),
        (base_r, BASEY),
        (basez_r, BASEZ),
        (basep_r, BASEP),
        (mix_r, MIXY),
        (st_r, STATY),
        (mixz_r, MIXZ),
        (stz_r, STATZ),
        (low_r, LOW),
        (ag2_c, DOWNC),
        (agu_c, UPC),
        (upx_r, UPX),
    ):
        sent(ref, chan)

    @pl.when(is_owner)
    def _():
        sent(agu.at[0], RS2U)
        sent(rs2u, AG2U)

    @pl.when(jnp.logical_not(is_owner))
    def _():
        sent(agu, RS2U)


def shards(
    learn_input,
    cotangent,
    rewards,
    group_ids,
    adapter_down,
    adapter_up,
    frozen_weight,
    hidden,
    queries,
    key_cache,
    value_cache,
    cache_lengths,
):
    hbm = pl.BlockSpec(memory_space=pltpu.HBM)
    operands = (
        learn_input,
        jnp.transpose(cotangent, (1, 2, 0)).reshape(128, TOK),
        adapter_down,
        adapter_up,
        hidden,
        frozen_weight,
        queries.reshape(ROWS, 128, HD),
        key_cache.reshape(ROWS, CACHE_DEV * KVH, HD),
        value_cache.reshape(ROWS, CACHE_DEV * KVH, HD),
    )
    out_shape = (
        jax.ShapeDtypeStruct((2, RANK, FEAT), F32),
        jax.ShapeDtypeStruct((2, RANK, RANK), F32),
        jax.ShapeDtypeStruct((ROWS, STEPS, 2 * HD), BF16),
    )
    vmem = pl.BlockSpec(memory_space=pltpu.VMEM)
    return pl.pallas_call(
        kernel,
        out_shape=out_shape,
        in_specs=[hbm] * 12,
        out_specs=(vmem,) * 3,
        scratch_shapes=[
            pltpu.SMEM((SEQ_DEV,), F32),
            pltpu.SMEM((SEQ_DEV,), jnp.int32),
            pltpu.SMEM((ROWS,), jnp.int32),
        ]
        + [pltpu.VMEM(o.shape, o.dtype) for o in operands]
        + [
            pltpu.VMEM((TOK, FEAT), BF16),
            pltpu.VMEM((2, RANK, TOK), BF16),
            pltpu.VMEM((RANK, TOK), BF16),
            pltpu.VMEM((ROWS, STEPS, FEAT), BF16),
            pltpu.VMEM((ROWS * STEPS, FEAT), F32),
            pltpu.VMEM((2, 16, 16, 128), BF16),
            pltpu.VMEM((2, 16, 16, 128), BF16),
            pltpu.VMEM((2, 16, 128), BF16),
            pltpu.VMEM((2, 2, 4, 2, 16, 128), BF16),
            pltpu.VMEM((16, 16, 128), BF16),
            pltpu.VMEM((15, 16, 128), BF16),
            pltpu.VMEM((16, 16, 128), BF16),
            pltpu.VMEM((16, 16, 128), BF16),
            pltpu.VMEM((2, 16, 128), BF16),
            pltpu.VMEM((15, 16, 128), BF16),
            pltpu.VMEM((2, 16, 128), BF16),
            pltpu.VMEM((2, 16, 128), BF16),
            pltpu.VMEM((16, 32, 128), BF16),
            pltpu.VMEM((7, 2, 32, 128), BF16),
            pltpu.VMEM((32, 128), F32),
            pltpu.VMEM((32, 128), F32),
            pltpu.VMEM((32, 128), F32),
            pltpu.VMEM((32, 128), F32),
            pltpu.VMEM((16, 64, HD), BF16),
            pltpu.VMEM((7, 2, 64, HD), BF16),
            pltpu.VMEM((64, HD), BF16),
            pltpu.VMEM((64, HD), BF16),
            pltpu.VMEM((16, 8, 128), F32),
            pltpu.VMEM((7, 2, 8, 128), F32),
            pltpu.VMEM((8, 128), F32),
            pltpu.VMEM((8, 128), F32),
            pltpu.VMEM((2, 16, 128), BF16),
            pltpu.VMEM((31, 16, 128), BF16),
            pltpu.VMEM((2, 16, 128), BF16),
            pltpu.VMEM((2, 2, 16, 128), BF16),
            pltpu.VMEM((ROWS, 128, HD), F32),
            pltpu.SemaphoreType.DMA((12,)),
            pltpu.SemaphoreType.DMA((N_CHAN,)),
            pltpu.SemaphoreType.DMA((N_CHAN,)),
        ],
        compiler_params=pltpu.CompilerParams(
            collective_id=0, has_side_effects=True, vmem_limit_bytes=VMEM_LIMIT
        ),
    )(
        *(
            pltpu.with_memory_space_constraint(o, pltpu.HBM)
            for o in (rewards, group_ids, cache_lengths, *operands)
        )
    )


def solution(mesh):
    return jax.shard_map(
        shards,
        mesh=mesh,
        in_specs=(
            P("dp", "tensor"),
            P("dp", None, "tensor"),
            P("dp"),
            P("dp"),
            P(None, None, "tensor"),
            P(None, None, "tensor"),
            P(None, "tensor", None),
            P("dp", None, "tensor"),
            P("dp", None, None, None),
            P("dp", "tensor", None, None),
            P("dp", "tensor", None, None),
            P("dp"),
        ),
        out_specs=(P(None, None, "tensor"), P(None, None, "tensor"), P("dp", None, "tensor")),
        check_vma=False,
    )
```

```python
import math

import jax
import jax.numpy as jnp
from jax import lax
from jax.experimental import pallas as pl
from jax.experimental.pallas import tpu as pltpu
from jax.sharding import PartitionSpec as P

MESH = pl.DeviceIdType.MESH
F32 = jnp.float32
BF16 = jnp.bfloat16

N_TP = 16
N_Y = 8
N_CHIP = 16
RANK = 64
SEQ_DEV = 8
SEQ_LEN = 32
TOK = SEQ_DEV * SEQ_LEN
FEAT = 512
ROWS = 8
STEPS = 4
CACHE_DEV = 48
KVH = 8
HD = 128
VMEM_LIMIT = 32 * 1024 * 1024

adapter_scale = 2.0
step_size = 0.004
masked_score = -1e30
score_scale = 1.0 / math.sqrt(HD)

(REW, GID, COT, UP, X, DOWN, HID, FRO, LEN, QRY, KEY, VAL) = range(12)
(
    RS1B,
    RS1P,
    AG1B,
    AG1P,
    XC,
    WC,
    HZ,
    HX,
    HC1,
    HC2,
    LRS,
    RS2,
    RS2U,
    AG2,
    AG2U,
    BASEY,
    BASEZ,
    BASEP,
    MIXY,
    STATY,
    MIXZ,
    STATZ,
    LOW,
    DOWNC,
    UPC,
    UPX,
    N_CHAN,
) = range(27)


def dot(a, b):
    return lax.dot_general(a, b, (((1,), (0,)), ((), ())), preferred_element_type=F32)


def dot_nt(a, b):
    return lax.dot_general(a, b, (((1,), (1,)), ((), ())), preferred_element_type=F32)


def iota(shape, axis):
    return lax.broadcasted_iota(jnp.int32, shape, axis)


def fold(a):
    n = a.shape[0] // 2
    return jnp.concatenate([a[:n], a[n:]], axis=1)


def unfold(a):
    return jnp.concatenate([a[:, :RANK], a[:, RANK:]], axis=0)


def by_tiles(tiles):
    return jnp.concatenate(
        [jnp.concatenate([tiles[r, 0], tiles[r, 1]], axis=1) for r in range(4)], axis=0
    )


def kernel(
    rew_h,
    gid_h,
    len_h,
    x_h,
    cot_h,
    down_h,
    up_h,
    hid_h,
    fro_h,
    q_h,
    k_h,
    v_h,
    od,
    ou,
    oa,
    rew,
    gid,
    lens,
    x,
    cot,
    down,
    up,
    hid,
    fro,
    qry,
    key,
    val,
    x_c,
    wt,
    wt_c,
    hid_f,
    h_all,
    h_down,
    l_send,
    l_r,
    pb_send,
    rs1,
    ag1_send,
    ag1,
    g_send,
    rs2,
    ag2,
    ag2_c,
    gu_send,
    rs2u,
    agu,
    agu_c,
    base_send,
    base_r,
    basez_send,
    basez_r,
    basep_send,
    basep_r,
    mix_send,
    mix_r,
    mixz_send,
    mixz_r,
    st_send,
    st_r,
    stz_send,
    stz_r,
    low_send,
    low_r,
    upx_send,
    upx_r,
    qp,
    in_sem,
    send,
    recv,
):
    dp = lax.axis_index("dp")
    tp = lax.axis_index("tensor")
    chip = lax.div(dp, 2)
    core = lax.rem(dp, 2)
    z_hi = lax.div(tp, N_Y)
    y = lax.rem(tp, N_Y)
    def two_along_z(q):
        return q + 2 - 4 * lax.rem(lax.div(q, 2), 2)

    middle = 2 * two_along_z(chip)
    column = 4 * lax.div(chip, 4)
    z_lo = lax.rem(chip, 4)
    other_core = 2 * chip + 1 - core
    pair = tp + 1 - 2 * lax.rem(tp, 2)
    other_half = y + N_Y * (1 - z_hi)

    hbm = (rew_h, gid_h, cot_h, up_h, x_h, down_h, hid_h, fro_h, len_h, q_h, k_h, v_h)
    own = (rew, gid, cot, up, x, down, hid, fro, lens, qry, key, val)
    loads = [pltpu.make_async_copy(h, v, in_sem.at[n]) for n, (h, v) in enumerate(zip(hbm, own))]
    for load in loads:
        load.start()

    ys = [lax.rem(y + o, N_Y) for o in (4, 3, 5, 2, 6, 1, 7, 0)]
    tps = [N_Y * h + t for t in ys for h in (1 - z_hi, z_hi)]
    chips = [lax.rem(chip + o, N_CHIP) for o in (8, 7, 9, 6, 10, 5, 11, 4, 12, 3, 13, 2, 14, 1, 15)]

    sheet = [(q, h) for q in chips + [chip] for h in (1 - z_hi, z_hi)][:-1]
    z_near = [column + lax.rem(z_lo + o, 4) for o in (2, 1, 3)]
    x_near = [lax.rem(chip + 4 * o, N_CHIP) for o in (2, 1, 3)]

    barrier = pltpu.get_barrier_semaphore()

    def greet(device):
        pl.semaphore_signal(barrier, inc=1, device_id=device, device_id_type=MESH)

    for t in tps:
        greet({"dp": middle + core, "tensor": t})
    for q, h in sheet:
        greet({"dp": 2 * q + core, "tensor": N_Y * h + y})
    greet({"dp": other_core})

    def remote(src, dst, chan, device):
        return pltpu.make_async_remote_copy(
            src_ref=src,
            dst_ref=dst,
            send_sem=send.at[chan],
            recv_sem=recv.at[chan],
            device_id=device,
            device_id_type=MESH,
        )

    def landed(ref, chan):
        pltpu.make_async_copy(ref, ref, recv.at[chan]).wait()

    def sent(ref, chan):
        pltpu.make_async_copy(ref, ref, send.at[chan]).wait()

    def summed(first, ref, start, stop):
        return lax.fori_loop(start, stop, lambda s, acc: acc + ref[s].astype(F32), first)

    loads[REW].wait()
    loads[GID].wait()
    lane_seq = lax.div(iota((1, TOK), 1), SEQ_LEN)
    rew_l = jnp.zeros((1, TOK), F32)
    gid_l = jnp.zeros((1, TOK), jnp.int32)
    for s in range(SEQ_DEV):
        rew_l = jnp.where(lane_seq == s, rew[s], rew_l)
        gid_l = jnp.where(lane_seq == s, gid[s], gid_l)
    cnt = jnp.zeros((1, TOK), F32)
    tot = jnp.zeros((1, TOK), F32)
    for s in range(SEQ_DEV):
        same = gid_l == gid[s]
        cnt = cnt + jnp.where(same, 1.0, 0.0)
        tot = tot + jnp.where(same, rew[s], 0.0)
    mean = tot / cnt
    spread = jnp.zeros((1, TOK), F32)
    for s in range(SEQ_DEV):
        off = rew[s] - mean
        spread = spread + jnp.where(gid_l == gid[s], off * off, 0.0)
    adv = (rew_l - mean) / jnp.maximum(jnp.sqrt(spread / cnt), 1.0)
    token_weight = adv / SEQ_LEN

    def put_pieces(part, k, product):
        product = product.astype(BF16)
        for r in range(4):
            for half in range(2):
                pb_send[part, (4 * k + r) * 2 + half] = product[
                    16 * r : 16 * (r + 1), 128 * half : 128 * (half + 1)
                ]

    loads[COT].wait()
    loads[UP].wait()
    for k in range(2):
        wt[k] = (cot[RANK * k : RANK * (k + 1)].astype(F32) * token_weight).astype(BF16)
        put_pieces(0, k, dot(up[k].astype(BF16), wt[k]))

    pl.semaphore_wait(barrier, N_TP + 2 * N_CHIP)

    def send_pieces(part, chan):
        for s, t in enumerate(tps):
            device = {"dp": middle + core, "tensor": t}
            remote(pb_send.at[part, t], rs1.at[part, s], chan, device).start()

    send_pieces(0, RS1B)
    loads[X].wait()
    loads[DOWN].wait()
    for k in range(2):
        put_pieces(1, k, dot_nt(down[k].astype(BF16), x[...]))
    send_pieces(1, RS1P)
    to_core = {"dp": other_core}
    remote(wt.at[1 - core], wt_c, WC, to_core).start()
    remote(x, x_c, XC, to_core).start()

    loads[HID].wait()
    for i in range(ROWS):
        hid_f[STEPS * i : STEPS * (i + 1), :] = hid[i].astype(F32)
    hid_b = hid_f[...].astype(BF16)
    h_all[core, chip] = hid_b
    rows = h_all.at[core, chip]
    for q in z_near:
        remote(rows, rows, HZ, {"dp": 2 * q + core}).start()
    for q in x_near:
        remote(rows, rows, HX, {"dp": 2 * q + core}).start()

    loads[FRO].wait()
    for part in range(4):
        cols = slice(part * 256, (part + 1) * 256)
        new_k = dot(hid_b, fro[0, :, cols]).astype(BF16)
        new_v = dot(hid_b, fro[1, :, cols]).astype(BF16)
        for n in range(4):
            half = slice(RANK * n, RANK * (n + 1))
            base_send[4 * part + n] = jnp.concatenate([new_k[:, half], new_v[:, half]], axis=1)

    loads[LEN].wait()
    loads[QRY].wait()
    loads[KEY].wait()
    loads[VAL].wait()
    out_row = iota((128, 128), 0)
    head = 2 * lax.div(out_row, 8) + lax.rem(lax.div(out_row, STEPS), 2)
    source = lax.rem(out_row, STEPS) * 32 + head
    perm = jnp.where(iota((128, 128), 1) == source, 1.0, 0.0).astype(BF16)
    lane_n = iota((128, CACHE_DEV * KVH), 1)
    own_group = lax.rem(lane_n, KVH) == lax.div(iota((128, CACHE_DEV * KVH), 0), 16)
    position = tp * CACHE_DEV + lax.div(lane_n, KVH)
    st_lane = iota((128, 128), 1)

    def attend(i, stats):
        q = dot(perm, qry[i])
        qp[i] = q
        score = dot_nt(q.astype(BF16), key[i]) * score_scale
        valid = jnp.logical_and(own_group, position < lens[i])
        score = jnp.where(valid, score, masked_score)
        high = jnp.max(score, axis=1, keepdims=True)
        weight = jnp.where(valid, jnp.exp(score - high), 0.0)
        total = jnp.sum(weight, axis=1, keepdims=True)
        mix = dot(weight.astype(BF16), val[i])
        stats = jnp.where(st_lane == i, high, stats)
        stats = jnp.where(st_lane == i + ROWS, total, stats)
        return mix.reshape(N_TP, 8, HD), stats

    def attend_pair(n, stats):
        m0, stats = attend(2 * n, stats)
        m1, stats = attend(2 * n + 1, stats)
        mix_send[:, pl.ds(pl.multiple_of(16 * n, 16), 16), :] = jnp.concatenate(
            [m0, m1], axis=1
        ).astype(BF16)
        return stats

    stats = lax.fori_loop(0, 4, attend_pair, jnp.zeros((128, 128), F32))
    st_send[...] = stats.reshape(N_TP, 8, 128)

    owned_k = lax.div(tp, N_Y)
    owned_r = lax.div(lax.rem(tp, N_Y), 2)
    owned_half = lax.rem(tp, 2)
    for part, chan_in, chan_out in ((0, RS1B, AG1B), (1, RS1P, AG1P)):
        landed(rs1.at[part], chan_in)
        ag1_send[part] = summed(jnp.zeros((16, 128), F32), rs1.at[part], 0, N_TP).astype(BF16)
        for t in tps:
            device = {"dp": middle + owned_k, "tensor": t}
            place = ag1.at[part, core, owned_r, owned_half]
            remote(ag1_send.at[part], place, chan_out, device).start()
        if part == 0:
            landed(h_all.at[0, pl.ds(0, 3)], HZ)
            for q in x_near:
                for n in z_near:
                    rows = h_all.at[core, n]
                    remote(rows, rows, HX, {"dp": 2 * q + core}).start()
            rows = h_all.at[core, pl.ds(column, 4)]
            remote(rows, rows, HC1, to_core).start()

    for s, to in enumerate(ys[:-1]):
        for z in range(2):
            t = N_Y * z + to
            device = {"tensor": N_Y * z_hi + to}
            remote(base_send.at[t], base_r.at[s, z], BASEY, device).start()

    landed(x_c, XC)
    landed(wt_c, WC)
    landed(h_all.at[0, pl.ds(0, 4)], HC1)
    down_b = down[core].astype(BF16)
    for c in range(2):
        h_down[c] = fold(dot_nt(h_all[c, chip], down_b))

    for s, to in enumerate(ys[:-1]):
        for z in range(2):
            t = N_Y * z + to
            device = {"tensor": N_Y * z_hi + to}
            remote(st_send.at[t], st_r.at[s, z], STATY, device).start()
            remote(mix_send.at[t], mix_r.at[s, z], MIXY, device).start()

    landed(ag1.at[0], AG1B)

    landed(h_all.at[0, pl.ds(0, 12)], HX)
    for q in x_near:
        rows = h_all.at[core, pl.ds(4 * lax.div(q, 4), 4)]
        remote(rows, rows, HC2, to_core).start()

    g_down = dot(by_tiles(ag1[0, core]), x[...]) + dot(by_tiles(ag1[0, 1 - core]), x_c[...])
    g_down = g_down.astype(BF16)
    for n in range(N_CHIP):
        r, c = n // 4, n % 4
        g_send[n] = g_down[16 * r : 16 * (r + 1), 128 * c : 128 * (c + 1)]
    for s, q in enumerate(chips):
        remote(g_send.at[q], rs2.at[s], RS2, {"dp": 2 * q + core}).start()

    def rows_product(c):
        part = step_size * adapter_scale * dot_nt(h_all[c].reshape(512, FEAT), g_down)
        part = part.reshape(N_CHIP, 2, 16, RANK)
        l_send[c] = jnp.concatenate([part[:, 0], part[:, 1]], axis=2).astype(BF16)
        own = step_size * adapter_scale * fold(dot_nt(h_all[c, chip], g_down))
        l_send[c, chip] = (own + h_down[c]).astype(BF16)

    rows_product(core)

    landed(ag1.at[1], AG1P)

    g_up = dot_nt(by_tiles(ag1[1, core]), wt[core]) + dot_nt(by_tiles(ag1[1, 1 - core]), wt_c[...])
    g_up = fold(g_up)
    for n in range(N_CHIP):
        gu_send[n] = g_up[2 * n : 2 * (n + 1)]
    for s, q in enumerate(chips):
        remote(gu_send.at[q], rs2u.at[s], RS2U, {"dp": 2 * q + core}).start()

    landed(h_all.at[0, pl.ds(0, 12)], HC2)
    rows_product(1 - core)

    for s, (q, h) in enumerate(sheet):
        device = {"dp": 2 * q + core, "tensor": N_Y * h + y}
        remote(l_send.at[h, two_along_z(q)], l_r.at[s], LRS, device).start()

    landed(base_r, BASEY)

    def base_sum(z):
        first = base_send[N_Y * z + y].astype(F32)
        return lax.fori_loop(
            0, N_Y - 1, lambda s, acc: acc + base_r[s, z].astype(F32), first
        )

    to_half = {"tensor": other_half}
    basez_send[...] = base_sum(1 - z_hi)
    remote(basez_send, basez_r, BASEZ, to_half).start()
    base = base_sum(z_hi)

    landed(rs2, RS2)

    ag2[chip] = summed(g_send[chip].astype(F32), rs2, 0, N_CHIP - 1).astype(BF16)

    for q in chips:
        remote(ag2.at[chip], ag2.at[chip], AG2, {"dp": 2 * q + core}).start()

    landed(rs2u, RS2U)
    agu[chip] = summed(gu_send[chip], rs2u, 0, N_CHIP - 1)
    for q in chips:
        remote(agu.at[chip], agu.at[chip], AG2U, {"dp": 2 * q + core}).start()

    landed(st_r, STATY)
    landed(mix_r, MIXY)

    def combine(st, mix, count):
        top = st(0)
        for s in range(1, count):
            top = jnp.maximum(top, st(s))
        total = jnp.zeros((8, 128), F32)
        acc = [jnp.zeros((8, 128), F32)] * ROWS
        for s in range(count):
            factor = jnp.exp(st(s) - top)
            total = total + factor * pltpu.roll(st(s), 128 - ROWS, 1)
            block = mix(s)
            for i in range(ROWS):
                acc[i] = acc[i] + factor[:, i : i + 1] * block[8 * i : 8 * (i + 1)].astype(F32)
        return top, total, acc

    def combine_y(z):
        t = N_Y * z + y
        return combine(
            lambda s: st_send[t] if s == 0 else st_r[s - 1, z],
            lambda s: mix_send[t] if s == 0 else mix_r[s - 1, z],
            N_Y,
        )

    def packed(top, total):
        return jnp.where(iota((8, 128), 1) < ROWS, top, pltpu.roll(total, ROWS, 1))

    top, total, acc = combine_y(1 - z_hi)
    stz_send[...] = packed(top, total)
    remote(stz_send, stz_r, STATZ, to_half).start()
    mixz_send[...] = jnp.concatenate(acc, axis=0).astype(BF16)
    remote(mixz_send, mixz_r, MIXZ, to_half).start()
    top, total, acc = combine_y(z_hi)
    own_st = packed(top, total)
    own_mix = jnp.concatenate(acc, axis=0)

    landed(l_r, LRS)

    low_send[...] = summed(
        l_send[z_hi, two_along_z(chip)].astype(F32), l_r, 0, 2 * N_CHIP - 1
    ).astype(BF16)
    for t in tps:
        device = {"dp": middle + z_hi, "tensor": t}
        remote(low_send, low_r.at[core, y], LOW, device).start()

    landed(basez_r, BASEZ)
    base = base + basez_r[...]
    basep_send[...] = base
    remote(basep_send, basep_r, BASEP, {"tensor": pair}).start()

    landed(ag2.at[pl.ds(0, N_CHIP - 1)], AG2)
    remote(ag2, ag2_c, DOWNC, to_core).start()

    def tiles_of(ref):
        return jnp.concatenate(
            [jnp.concatenate([ref[4 * r + c] for c in range(4)], axis=1) for r in range(4)], axis=0
        ).astype(F32)

    od[core] = down[core] + step_size * (adapter_scale * tiles_of(ag2))

    landed(agu.at[pl.ds(0, N_CHIP - 1)], AG2U)

    def up_updated(k, grad):
        return up[k] + step_size * (adapter_scale * unfold(grad.reshape(32, 128)))

    new_up = up_updated(core, agu[...])
    upx_send[...] = fold(new_up).astype(BF16).reshape(2, 16, 128)
    remote(agu, agu_c, UPC, to_core).start()
    remote(upx_send, upx_r.at[0], UPX, {"tensor": pair}).start()
    remote(upx_send, upx_r.at[1], UPX, {"dp": other_core, "tensor": pair}).start()
    ou[core] = new_up

    landed(ag2_c, DOWNC)
    od[1 - core] = down[1 - core] + step_size * (adapter_scale * tiles_of(ag2_c))
    landed(agu_c, UPC)
    new_up_c = up_updated(1 - core, agu_c[...])
    ou[1 - core] = new_up_c

    landed(upx_r, UPX)
    even = lax.rem(tp, 2) == 0

    def both(mine, theirs):
        left = jnp.where(even, mine, theirs)
        right = jnp.where(even, theirs, mine)
        return jnp.concatenate([left, right], axis=1)

    def columns(mine, theirs):
        return both(mine, unfold(theirs.reshape(32, 128)).astype(F32)).astype(BF16)

    up_own = columns(new_up, upx_r[0])
    up_oth = columns(new_up_c, upx_r[1])
    landed(basep_r, BASEP)
    base_k = both(base[:, :RANK], basep_r[:, :RANK])
    base_v = both(base[:, RANK:], basep_r[:, RANK:])

    landed(stz_r, STATZ)
    landed(mixz_r, MIXZ)
    top, total, acc = combine(
        lambda s: stz_r[...] if s else own_st, lambda s: mixz_r[...] if s else own_mix, 2
    )
    old_high = jnp.concatenate([top[:, i : i + 1] for i in range(ROWS)], axis=0)
    old_total = jnp.concatenate([total[:, i : i + 1] for i in range(ROWS)], axis=0)
    old_mix = jnp.concatenate(acc, axis=0)
    own_q = qp[:, pl.ds(pl.multiple_of(8 * tp, 8), 8), :].reshape(64, HD).astype(BF16)

    landed(low_r, LOW)

    none = jnp.zeros((16, 128), F32)
    low_own = unfold(summed(none, low_r.at[core], 0, N_Y)).astype(BF16)
    low_oth = unfold(summed(none, low_r.at[1 - core], 0, N_Y)).astype(BF16)
    from_own = adapter_scale * dot(low_own, up_own)
    from_oth = adapter_scale * dot(low_oth, up_oth)
    first = core == 0
    new_k = (base_k + jnp.where(first, from_own, from_oth)).astype(BF16)
    new_v = (base_v + jnp.where(first, from_oth, from_own)).astype(BF16)
    row = iota((64, 32), 0)
    col = iota((64, 32), 1)
    causal = jnp.logical_and(
        lax.div(row, 8) == lax.div(col, STEPS), lax.rem(col, STEPS) <= lax.rem(row, STEPS)
    )
    score = jnp.where(causal, dot_nt(own_q, new_k) * score_scale, masked_score)
    new_high = jnp.max(score, axis=1, keepdims=True)
    weight = jnp.where(causal, jnp.exp(score - new_high), 0.0)
    new_total = jnp.sum(weight, axis=1, keepdims=True)
    new_mix = dot(weight.astype(BF16), new_v)
    highest = jnp.maximum(old_high, new_high)
    f_old = jnp.exp(old_high - highest)
    f_new = jnp.exp(new_high - highest)
    out = (f_old * old_mix + f_new * new_mix) / (f_old * old_total + f_new * new_total)
    out = out.reshape(ROWS, 8, HD)
    oa[:, :, 0:HD] = out[:, 0:STEPS].astype(BF16)
    oa[:, :, HD:] = out[:, STEPS:].astype(BF16)

    for ref, chan in (
        (rs1.at[0], RS1B),
        (rs1.at[1], RS1P),
        (ag1.at[0], AG1B),
        (ag1.at[1], AG1P),
        (x_c, XC),
        (wt_c, WC),
        (h_all.at[0, pl.ds(0, 3)], HZ),
        (h_all.at[0, pl.ds(0, 12)], HX),
        (h_all.at[0, pl.ds(0, 4)], HC1),
        (h_all.at[0, pl.ds(0, 12)], HC2),
        (l_r, LRS),
        (rs2u, RS2U),
        (rs2u, AG2U),
        (rs2, RS2),
        (rs2, AG2),
        (base_r, BASEY),
        (basez_r, BASEZ),
        (basep_r, BASEP),
        (mix_r, MIXY),
        (st_r, STATY),
        (mixz_r, MIXZ),
        (stz_r, STATZ),
        (low_r, LOW),
        (ag2_c, DOWNC),
        (agu_c, UPC),
        (upx_r, UPX),
    ):
        sent(ref, chan)


def shards(
    learn_input,
    cotangent,
    rewards,
    group_ids,
    adapter_down,
    adapter_up,
    frozen_weight,
    hidden,
    queries,
    key_cache,
    value_cache,
    cache_lengths,
):
    hbm = pl.BlockSpec(memory_space=pltpu.HBM)
    operands = (
        learn_input,
        jnp.transpose(cotangent, (1, 2, 0)).reshape(128, TOK),
        adapter_down,
        adapter_up,
        hidden,
        frozen_weight,
        queries.reshape(ROWS, 128, HD),
        key_cache.reshape(ROWS, CACHE_DEV * KVH, HD),
        value_cache.reshape(ROWS, CACHE_DEV * KVH, HD),
    )
    out_shape = (
        jax.ShapeDtypeStruct((2, RANK, FEAT), F32),
        jax.ShapeDtypeStruct((2, RANK, RANK), F32),
        jax.ShapeDtypeStruct((ROWS, STEPS, 2 * HD), BF16),
    )
    vmem = pl.BlockSpec(memory_space=pltpu.VMEM)
    return pl.pallas_call(
        kernel,
        out_shape=out_shape,
        in_specs=[hbm] * 12,
        out_specs=(vmem,) * 3,
        scratch_shapes=[
            pltpu.SMEM((SEQ_DEV,), F32),
            pltpu.SMEM((SEQ_DEV,), jnp.int32),
            pltpu.SMEM((ROWS,), jnp.int32),
        ]
        + [pltpu.VMEM(o.shape, o.dtype) for o in operands]
        + [
            pltpu.VMEM((TOK, FEAT), BF16),
            pltpu.VMEM((2, RANK, TOK), BF16),
            pltpu.VMEM((RANK, TOK), BF16),
            pltpu.VMEM((ROWS * STEPS, FEAT), F32),
            pltpu.VMEM((2, 16, ROWS * STEPS, FEAT), BF16),
            pltpu.VMEM((2, 16, 128), F32),
            pltpu.VMEM((2, 16, 16, 128), BF16),
            pltpu.VMEM((31, 16, 128), BF16),
            pltpu.VMEM((2, 16, 16, 128), BF16),
            pltpu.VMEM((2, 16, 16, 128), BF16),
            pltpu.VMEM((2, 16, 128), BF16),
            pltpu.VMEM((2, 2, 4, 2, 16, 128), BF16),
            pltpu.VMEM((16, 16, 128), BF16),
            pltpu.VMEM((15, 16, 128), BF16),
            pltpu.VMEM((16, 16, 128), BF16),
            pltpu.VMEM((16, 16, 128), BF16),
            pltpu.VMEM((16, 2, 128), F32),
            pltpu.VMEM((15, 2, 128), F32),
            pltpu.VMEM((16, 2, 128), F32),
            pltpu.VMEM((16, 2, 128), F32),
            pltpu.VMEM((16, 32, 128), BF16),
            pltpu.VMEM((7, 2, 32, 128), BF16),
            pltpu.VMEM((32, 128), F32),
            pltpu.VMEM((32, 128), F32),
            pltpu.VMEM((32, 128), F32),
            pltpu.VMEM((32, 128), F32),
            pltpu.VMEM((16, 64, HD), BF16),
            pltpu.VMEM((7, 2, 64, HD), BF16),
            pltpu.VMEM((64, HD), BF16),
            pltpu.VMEM((64, HD), BF16),
            pltpu.VMEM((16, 8, 128), F32),
            pltpu.VMEM((7, 2, 8, 128), F32),
            pltpu.VMEM((8, 128), F32),
            pltpu.VMEM((8, 128), F32),
            pltpu.VMEM((16, 128), BF16),
            pltpu.VMEM((2, 8, 16, 128), BF16),
            pltpu.VMEM((2, 16, 128), BF16),
            pltpu.VMEM((2, 2, 16, 128), BF16),
            pltpu.VMEM((ROWS, 128, HD), F32),
            pltpu.SemaphoreType.DMA((12,)),
            pltpu.SemaphoreType.DMA((N_CHAN,)),
            pltpu.SemaphoreType.DMA((N_CHAN,)),
        ],
        compiler_params=pltpu.CompilerParams(
            collective_id=0, has_side_effects=True, vmem_limit_bytes=VMEM_LIMIT
        ),
    )(
        *(
            pltpu.with_memory_space_constraint(o, pltpu.HBM)
            for o in (rewards, group_ids, cache_lengths, *operands)
        )
    )


def solution(mesh):
    return jax.shard_map(
        shards,
        mesh=mesh,
        in_specs=(
            P("dp", "tensor"),
            P("dp", None, "tensor"),
            P("dp"),
            P("dp"),
            P(None, None, "tensor"),
            P(None, None, "tensor"),
            P(None, "tensor", None),
            P("dp", None, "tensor"),
            P("dp", None, None, None),
            P("dp", "tensor", None, None),
            P("dp", "tensor", None, None),
            P("dp"),
        ),
        out_specs=(P(None, None, "tensor"), P(None, None, "tensor"), P("dp", None, "tensor")),
        check_vma=False,
    )
```

```python
import math

import jax
import jax.numpy as jnp
from jax import lax
from jax.experimental import pallas as pl
from jax.experimental.pallas import tpu as pltpu
from jax.sharding import PartitionSpec as P

MESH = pl.DeviceIdType.MESH
F32 = jnp.float32
BF16 = jnp.bfloat16

N_TP = 16
N_Y = 8
N_CHIP = 16
RANK = 64
SEQ_DEV = 8
SEQ_LEN = 32
TOK = SEQ_DEV * SEQ_LEN
FEAT = 512
ROWS = 8
STEPS = 4
CACHE_DEV = 48
KVH = 8
HD = 128
VMEM_LIMIT = 32 * 1024 * 1024

adapter_scale = 2.0
step_size = 0.004
masked_score = -1e30
score_scale = 1.0 / math.sqrt(HD)

(REW, GID, COT, UP, X, DOWN, HID, FRO, LEN, QRY, KEY, VAL) = range(12)
(
    RS1B,
    RS1P,
    AG1B,
    AG1P,
    XC,
    WC,
    HZ,
    HX,
    HC1,
    HC2,
    LRS,
    RS2,
    RS2U,
    AG2,
    AG2U,
    BASEY,
    BASEZ,
    BASEP,
    MIXY,
    STATY,
    MIXZ,
    STATZ,
    LOW,
    DOWNC,
    UPC,
    UPX,
    N_CHAN,
) = range(27)


TILE = 4
SENT_BOTH = (
    2 * 16 * TILE
    + 32 + 256
    + (3 + 12 + 4 + 12) * 32
    + 31 * TILE
    + 2 * 15 * TILE + 64
    + 2 * 15 + 16 + 2 * 8
    + 14 * 8 + 2 * 16
    + 14 * (16 + TILE) + 16 + TILE
)
SENT_0 = SENT_BOTH + TILE
SENT_1 = SENT_BOTH + 2 * 2 * 16 * TILE + 16 * 2 * TILE


def dot(a, b):
    return lax.dot_general(a, b, (((1,), (0,)), ((), ())), preferred_element_type=F32)


def dot_nt(a, b):
    return lax.dot_general(a, b, (((1,), (1,)), ((), ())), preferred_element_type=F32)


def iota(shape, axis):
    return lax.broadcasted_iota(jnp.int32, shape, axis)


def fold(a):
    n = a.shape[0] // 2
    return jnp.concatenate([a[:n], a[n:]], axis=1)


def unfold(a):
    return jnp.concatenate([a[:, :RANK], a[:, RANK:]], axis=0)


def by_tiles(tiles):
    return jnp.concatenate(
        [jnp.concatenate([tiles[r, 0], tiles[r, 1]], axis=1) for r in range(4)], axis=0
    )


def kernel(
    rew_h,
    gid_h,
    len_h,
    x_h,
    cot_h,
    down_h,
    up_h,
    hid_h,
    fro_h,
    q_h,
    k_h,
    v_h,
    od,
    ou,
    oa,
    rew,
    gid,
    lens,
    x,
    cot,
    down,
    up,
    hid,
    fro,
    qry,
    key,
    val,
    x_c,
    wt,
    wt_c,
    hid_f,
    h_all,
    h_down,
    l_send,
    l_r,
    pb_send,
    rs1,
    ag1_send,
    ag1,
    g_send,
    rs2,
    ag2,
    ag2_c,
    gu_send,
    rs2u,
    agu,
    agu_c,
    base_send,
    base_r,
    basez_send,
    basez_r,
    basep_send,
    basep_r,
    mix_send,
    mix_r,
    mixz_send,
    mixz_r,
    st_send,
    st_r,
    stz_send,
    stz_r,
    low_send,
    low_r,
    upx_send,
    upx_r,
    qp,
    all_sent,
    in_sem,
    send,
    recv,
):
    dp = lax.axis_index("dp")
    tp = lax.axis_index("tensor")
    chip = lax.div(dp, 2)
    core = lax.rem(dp, 2)
    z_hi = lax.div(tp, N_Y)
    y = lax.rem(tp, N_Y)
    def two_along_z(q):
        return q + 2 - 4 * lax.rem(lax.div(q, 2), 2)

    middle = 2 * two_along_z(chip)
    column = 4 * lax.div(chip, 4)
    z_lo = lax.rem(chip, 4)
    other_core = 2 * chip + 1 - core
    pair = tp + 1 - 2 * lax.rem(tp, 2)
    other_half = y + N_Y * (1 - z_hi)

    hbm = (rew_h, gid_h, cot_h, up_h, x_h, down_h, hid_h, fro_h, len_h, q_h, k_h, v_h)
    own = (rew, gid, cot, up, x, down, hid, fro, lens, qry, key, val)
    loads = [pltpu.make_async_copy(h, v, in_sem.at[n]) for n, (h, v) in enumerate(zip(hbm, own))]
    for load in loads:
        load.start()

    ys = [lax.rem(y + o, N_Y) for o in (4, 3, 5, 2, 6, 1, 7, 0)]
    tps = [N_Y * h + t for t in ys for h in (1 - z_hi, z_hi)]
    chips = [lax.rem(chip + o, N_CHIP) for o in (8, 7, 9, 6, 10, 5, 11, 4, 12, 3, 13, 2, 14, 1, 15)]

    z_near = [column + lax.rem(z_lo + o, 4) for o in (2, 1, 3)]
    x_near = [lax.rem(chip + 4 * o, N_CHIP) for o in (2, 1, 3)]

    barrier = pltpu.get_barrier_semaphore()

    def greet(device):
        pl.semaphore_signal(barrier, inc=1, device_id=device, device_id_type=MESH)

    @pl.when(core == 1)
    def _():
        for t in tps:
            greet({"dp": middle, "tensor": t})
            greet({"dp": middle + 1, "tensor": t})

    for q in chips:
        greet({"dp": 2 * q + core})
    greet({"dp": other_core})
    for t in ys[:-1]:
        greet({"tensor": N_Y * z_hi + t})

    def remote(src, dst, chan, device):
        return pltpu.make_async_remote_copy(
            src_ref=src,
            dst_ref=dst,
            send_sem=send.at[0],
            recv_sem=recv.at[chan],
            device_id=device,
            device_id_type=MESH,
        )

    def landed(ref, chan):
        pltpu.make_async_copy(ref, ref, recv.at[chan]).wait()

    def sent(size):
        ref = all_sent.at[pl.ds(0, size)]
        pltpu.make_async_copy(ref, ref, send.at[0]).wait()

    def summed(first, ref, start, stop):
        return lax.fori_loop(start, stop, lambda s, acc: acc + ref[s].astype(F32), first)

    loads[REW].wait()
    loads[GID].wait()
    lane_seq = lax.div(iota((1, TOK), 1), SEQ_LEN)
    rew_l = jnp.zeros((1, TOK), F32)
    gid_l = jnp.zeros((1, TOK), jnp.int32)
    for s in range(SEQ_DEV):
        rew_l = jnp.where(lane_seq == s, rew[s], rew_l)
        gid_l = jnp.where(lane_seq == s, gid[s], gid_l)
    cnt = jnp.zeros((1, TOK), F32)
    tot = jnp.zeros((1, TOK), F32)
    for s in range(SEQ_DEV):
        same = gid_l == gid[s]
        cnt = cnt + jnp.where(same, 1.0, 0.0)
        tot = tot + jnp.where(same, rew[s], 0.0)
    mean = tot / cnt
    spread = jnp.zeros((1, TOK), F32)
    for s in range(SEQ_DEV):
        off = rew[s] - mean
        spread = spread + jnp.where(gid_l == gid[s], off * off, 0.0)
    adv = (rew_l - mean) / jnp.maximum(jnp.sqrt(spread / cnt), 1.0)
    token_weight = adv / SEQ_LEN

    def put_pieces(part, k, product):
        product = product.astype(BF16)
        for r in range(4):
            for half in range(2):
                pb_send[part, (4 * k + r) * 2 + half] = product[
                    16 * r : 16 * (r + 1), 128 * half : 128 * (half + 1)
                ]

    loads[COT].wait()
    loads[UP].wait()
    for k in range(2):
        wt[k] = (cot[RANK * k : RANK * (k + 1)].astype(F32) * token_weight).astype(BF16)
        put_pieces(0, k, dot(up[k].astype(BF16), wt[k]))

    pl.semaphore_wait(barrier, N_TP + N_CHIP + N_Y - 1)

    def send_pieces(part, chan):
        for s, t in enumerate(tps):
            device = {"dp": middle + 1, "tensor": t}
            remote(pb_send.at[part, t], rs1.at[part, core, s], chan, device).start()

    send_pieces(0, RS1B)
    loads[X].wait()
    loads[DOWN].wait()
    for k in range(2):
        put_pieces(1, k, dot_nt(down[k].astype(BF16), x[...]))
    send_pieces(1, RS1P)
    to_core = {"dp": other_core}
    remote(wt.at[1 - core], wt_c, WC, to_core).start()
    remote(x, x_c, XC, to_core).start()

    loads[HID].wait()
    for i in range(ROWS):
        hid_f[STEPS * i : STEPS * (i + 1), :] = hid[i].astype(F32)
    hid_b = hid_f[...].astype(BF16)
    h_all[core, chip] = hid_b
    rows = h_all.at[core, chip]
    for q in z_near:
        remote(rows, rows, HZ, {"dp": 2 * q + core}).start()
    for q in x_near:
        remote(rows, rows, HX, {"dp": 2 * q + core}).start()

    loads[FRO].wait()
    for part in range(4):
        cols = slice(part * 256, (part + 1) * 256)
        new_k = dot(hid_b, fro[0, :, cols]).astype(BF16)
        new_v = dot(hid_b, fro[1, :, cols]).astype(BF16)
        for n in range(4):
            half = slice(RANK * n, RANK * (n + 1))
            base_send[4 * part + n] = jnp.concatenate([new_k[:, half], new_v[:, half]], axis=1)

    loads[LEN].wait()
    loads[QRY].wait()
    loads[KEY].wait()
    loads[VAL].wait()
    out_row = iota((128, 128), 0)
    head = 2 * lax.div(out_row, 8) + lax.rem(lax.div(out_row, STEPS), 2)
    source = lax.rem(out_row, STEPS) * 32 + head
    perm = jnp.where(iota((128, 128), 1) == source, 1.0, 0.0).astype(BF16)
    lane_n = iota((128, CACHE_DEV * KVH), 1)
    own_group = lax.rem(lane_n, KVH) == lax.div(iota((128, CACHE_DEV * KVH), 0), 16)
    position = tp * CACHE_DEV + lax.div(lane_n, KVH)
    st_lane = iota((128, 128), 1)

    def attend(i, stats):
        q = dot(perm, qry[i])
        qp[i] = q
        score = dot_nt(q.astype(BF16), key[i]) * score_scale
        valid = jnp.logical_and(own_group, position < lens[i])
        score = jnp.where(valid, score, masked_score)
        high = jnp.max(score, axis=1, keepdims=True)
        weight = jnp.where(valid, jnp.exp(score - high), 0.0)
        total = jnp.sum(weight, axis=1, keepdims=True)
        mix = dot(weight.astype(BF16), val[i])
        stats = jnp.where(st_lane == i, high, stats)
        stats = jnp.where(st_lane == i + ROWS, total, stats)
        return mix.reshape(N_TP, 8, HD), stats

    def attend_pair(n, stats):
        m0, stats = attend(2 * n, stats)
        m1, stats = attend(2 * n + 1, stats)
        mix_send[:, pl.ds(pl.multiple_of(16 * n, 16), 16), :] = jnp.concatenate(
            [m0, m1], axis=1
        ).astype(BF16)
        return stats

    stats = lax.fori_loop(0, 4, attend_pair, jnp.zeros((128, 128), F32))
    st_send[...] = stats.reshape(N_TP, 8, 128)

    owned_k = lax.div(tp, N_Y)
    owned_r = lax.div(lax.rem(tp, N_Y), 2)
    owned_half = lax.rem(tp, 2)

    def products_sum(part, chan_in, chan_out):
        @pl.when(core == 1)
        def _():
            landed(rs1.at[part], chan_in)
            for c in range(2):
                none = jnp.zeros((16, 128), F32)
                ag1_send[part, c] = summed(none, rs1.at[part, c], 0, N_TP).astype(BF16)
                for t in tps:
                    device = {"dp": middle + owned_k, "tensor": t}
                    place = ag1.at[part, c, owned_r, owned_half]
                    remote(ag1_send.at[part, c], place, chan_out, device).start()

    products_sum(0, RS1B, AG1B)

    products_sum(1, RS1P, AG1P)

    landed(h_all.at[0, pl.ds(0, 3)], HZ)
    for q in x_near:
        for n in z_near:
            rows = h_all.at[core, n]
            remote(rows, rows, HX, {"dp": 2 * q + core}).start()
    rows = h_all.at[core, pl.ds(column, 4)]
    remote(rows, rows, HC1, to_core).start()

    for s, to in enumerate(ys[:-1]):
        for z in range(2):
            t = N_Y * z + to
            device = {"tensor": N_Y * z_hi + to}
            remote(base_send.at[t], base_r.at[s, z], BASEY, device).start()

    landed(x_c, XC)
    landed(wt_c, WC)
    landed(h_all.at[0, pl.ds(0, 4)], HC1)
    down_b = down[core].astype(BF16)
    for c in range(2):
        h_down[c] = fold(dot_nt(h_all[c, chip], down_b))

    for s, to in enumerate(ys[:-1]):
        for z in range(2):
            t = N_Y * z + to
            device = {"tensor": N_Y * z_hi + to}
            remote(st_send.at[t], st_r.at[s, z], STATY, device).start()
            remote(mix_send.at[t], mix_r.at[s, z], MIXY, device).start()

    landed(ag1.at[0], AG1B)

    g_down = dot(by_tiles(ag1[0, core]), x[...]) + dot(by_tiles(ag1[0, 1 - core]), x_c[...])
    g_down = g_down.astype(BF16)
    for n in range(N_CHIP):
        r, c = n // 4, n % 4
        g_send[n] = g_down[16 * r : 16 * (r + 1), 128 * c : 128 * (c + 1)]
    for s, q in enumerate(chips):
        remote(g_send.at[q], rs2.at[s], RS2, {"dp": 2 * q + core}).start()

    def rows_product(xo, c):
        places = pl.ds(lax.rem(column + 4 * xo, N_CHIP), 4)
        part = step_size * adapter_scale * dot_nt(h_all[c, places].reshape(128, FEAT), g_down)
        part = part.reshape(4, 2, 16, RANK)
        l_send[c, places] = jnp.concatenate([part[:, 0], part[:, 1]], axis=2).astype(BF16)

    def rows_send(xo, zo, half):
        q = lax.rem(column + 4 * xo, N_CHIP) + lax.rem(z_lo + zo, 4)
        slot = 2 * (4 * xo + zo) + lax.rem(half + z_hi, 2)
        device = {"dp": 2 * q + 1, "tensor": N_Y * half + y}
        place = l_r.at[2 * N_CHIP * core + slot]
        remote(l_send.at[half, two_along_z(q)], place, LRS, device).start()

    for c in range(2):
        rows_product(0, c)
        own = step_size * adapter_scale * fold(dot_nt(h_all[c, chip], g_down))
        l_send[c, chip] = (own + h_down[c]).astype(BF16)
    for zo in (2, 1, 3):
        rows_send(0, zo, 1 - z_hi)
        rows_send(0, zo, z_hi)
    rows_send(0, 0, 1 - z_hi)
    last = l_send.at[z_hi, two_along_z(chip)]

    @pl.when(core == 0)
    def _():
        remote(last, l_r.at[0], LRS, to_core).start()

    @pl.when(core == 1)
    def _():
        l_r[2 * N_CHIP] = last[...]

    landed(ag1.at[1], AG1P)

    g_up = dot_nt(by_tiles(ag1[1, core]), wt[core]) + dot_nt(by_tiles(ag1[1, 1 - core]), wt_c[...])
    g_up = fold(g_up)
    for n in range(N_CHIP):
        gu_send[n] = g_up[2 * n : 2 * (n + 1)]
    for s, q in enumerate(chips):
        remote(gu_send.at[q], rs2u.at[s], RS2U, {"dp": 2 * q + core}).start()

    landed(h_all.at[0, pl.ds(0, 12)], HX)
    for q in x_near:
        rows = h_all.at[core, pl.ds(4 * lax.div(q, 4), 4)]
        remote(rows, rows, HC2, to_core).start()

    for xo in (2, 1, 3):
        rows_product(xo, core)
    for zo in (2, 1, 3, 0):
        for xo in (2, 1, 3):
            rows_send(xo, zo, core)
    landed(h_all.at[0, pl.ds(0, 12)], HC2)
    for xo in (2, 1, 3):
        rows_product(xo, 1 - core)
    for zo in (2, 1, 3, 0):
        for xo in (2, 1, 3):
            rows_send(xo, zo, 1 - core)

    landed(base_r, BASEY)

    def base_sum(z):
        first = base_send[N_Y * z + y].astype(F32)
        return lax.fori_loop(
            0, N_Y - 1, lambda s, acc: acc + base_r[s, z].astype(F32), first
        )

    to_half = {"tensor": other_half}
    basez_send[...] = base_sum(1 - z_hi)
    remote(basez_send, basez_r, BASEZ, to_half).start()
    base = base_sum(z_hi)

    landed(rs2, RS2)

    ag2[chip] = summed(g_send[chip].astype(F32), rs2, 0, N_CHIP - 1).astype(BF16)

    for q in chips:
        remote(ag2.at[chip], ag2.at[chip], AG2, {"dp": 2 * q + core}).start()

    landed(rs2u, RS2U)
    agu[chip] = summed(gu_send[chip], rs2u, 0, N_CHIP - 1)
    for q in chips:
        remote(agu.at[chip], agu.at[chip], AG2U, {"dp": 2 * q + core}).start()

    landed(st_r, STATY)
    landed(mix_r, MIXY)

    def combine(st, mix, count):
        top = st(0)
        for s in range(1, count):
            top = jnp.maximum(top, st(s))
        total = jnp.zeros((8, 128), F32)
        acc = [jnp.zeros((8, 128), F32)] * ROWS
        for s in range(count):
            factor = jnp.exp(st(s) - top)
            total = total + factor * pltpu.roll(st(s), 128 - ROWS, 1)
            block = mix(s)
            for i in range(ROWS):
                acc[i] = acc[i] + factor[:, i : i + 1] * block[8 * i : 8 * (i + 1)].astype(F32)
        return top, total, acc

    def combine_y(z):
        t = N_Y * z + y
        return combine(
            lambda s: st_send[t] if s == 0 else st_r[s - 1, z],
            lambda s: mix_send[t] if s == 0 else mix_r[s - 1, z],
            N_Y,
        )

    def packed(top, total):
        return jnp.where(iota((8, 128), 1) < ROWS, top, pltpu.roll(total, ROWS, 1))

    top, total, acc = combine_y(1 - z_hi)
    stz_send[...] = packed(top, total)
    remote(stz_send, stz_r, STATZ, to_half).start()
    mixz_send[...] = jnp.concatenate(acc, axis=0).astype(BF16)
    remote(mixz_send, mixz_r, MIXZ, to_half).start()
    top, total, acc = combine_y(z_hi)
    own_st = packed(top, total)
    own_mix = jnp.concatenate(acc, axis=0)

    @pl.when(core == 1)
    def _():
        landed(l_r.at[pl.ds(0, 4 * N_CHIP - 1)], LRS)
        for k in range(2):
            none = jnp.zeros((16, 128), F32)
            total = summed(none, l_r, 2 * N_CHIP * k, 2 * N_CHIP * (k + 1))
            low_send[k] = total.astype(BF16)
        for t in tps:
            device = {"dp": middle + z_hi, "tensor": t}
            remote(low_send, low_r.at[y], LOW, device).start()

    landed(basez_r, BASEZ)
    base = base + basez_r[...]
    basep_send[...] = base
    remote(basep_send, basep_r, BASEP, {"tensor": pair}).start()

    landed(ag2.at[pl.ds(0, N_CHIP - 1)], AG2)
    remote(ag2, ag2_c, DOWNC, to_core).start()

    def tiles_of(ref):
        return jnp.concatenate(
            [jnp.concatenate([ref[4 * r + c] for c in range(4)], axis=1) for r in range(4)], axis=0
        ).astype(F32)

    od[core] = down[core] + step_size * (adapter_scale * tiles_of(ag2))

    landed(agu.at[pl.ds(0, N_CHIP - 1)], AG2U)

    def up_updated(k, grad):
        return up[k] + step_size * (adapter_scale * unfold(grad.reshape(32, 128)))

    new_up = up_updated(core, agu[...])
    upx_send[...] = fold(new_up).astype(BF16).reshape(2, 16, 128)
    remote(agu, agu_c, UPC, to_core).start()
    remote(upx_send, upx_r.at[0], UPX, {"tensor": pair}).start()
    remote(upx_send, upx_r.at[1], UPX, {"dp": other_core, "tensor": pair}).start()
    ou[core] = new_up

    landed(ag2_c, DOWNC)
    od[1 - core] = down[1 - core] + step_size * (adapter_scale * tiles_of(ag2_c))
    landed(agu_c, UPC)
    new_up_c = up_updated(1 - core, agu_c[...])
    ou[1 - core] = new_up_c

    landed(upx_r, UPX)
    even = lax.rem(tp, 2) == 0

    def both(mine, theirs):
        left = jnp.where(even, mine, theirs)
        right = jnp.where(even, theirs, mine)
        return jnp.concatenate([left, right], axis=1)

    def columns(mine, theirs):
        return both(mine, unfold(theirs.reshape(32, 128)).astype(F32)).astype(BF16)

    up_own = columns(new_up, upx_r[0])
    up_oth = columns(new_up_c, upx_r[1])
    landed(basep_r, BASEP)
    base_k = both(base[:, :RANK], basep_r[:, :RANK])
    base_v = both(base[:, RANK:], basep_r[:, RANK:])

    landed(stz_r, STATZ)
    landed(mixz_r, MIXZ)
    top, total, acc = combine(
        lambda s: stz_r[...] if s else own_st, lambda s: mixz_r[...] if s else own_mix, 2
    )
    old_high = jnp.concatenate([top[:, i : i + 1] for i in range(ROWS)], axis=0)
    old_total = jnp.concatenate([total[:, i : i + 1] for i in range(ROWS)], axis=0)
    old_mix = jnp.concatenate(acc, axis=0)
    own_q = qp[:, pl.ds(pl.multiple_of(8 * tp, 8), 8), :].reshape(64, HD).astype(BF16)

    landed(low_r, LOW)

    def total_of(k):
        acc = low_r[0, k].astype(F32)
        for n in range(1, N_Y):
            acc = acc + low_r[n, k].astype(F32)
        return acc

    low_own = unfold(total_of(core)).astype(BF16)
    low_oth = unfold(total_of(1 - core)).astype(BF16)
    from_own = adapter_scale * dot(low_own, up_own)
    from_oth = adapter_scale * dot(low_oth, up_oth)
    first = core == 0
    new_k = (base_k + jnp.where(first, from_own, from_oth)).astype(BF16)
    new_v = (base_v + jnp.where(first, from_oth, from_own)).astype(BF16)
    row = iota((64, 32), 0)
    col = iota((64, 32), 1)
    causal = jnp.logical_and(
        lax.div(row, 8) == lax.div(col, STEPS), lax.rem(col, STEPS) <= lax.rem(row, STEPS)
    )
    score = jnp.where(causal, dot_nt(own_q, new_k) * score_scale, masked_score)
    new_high = jnp.max(score, axis=1, keepdims=True)
    weight = jnp.where(causal, jnp.exp(score - new_high), 0.0)
    new_total = jnp.sum(weight, axis=1, keepdims=True)
    new_mix = dot(weight.astype(BF16), new_v)
    highest = jnp.maximum(old_high, new_high)
    f_old = jnp.exp(old_high - highest)
    f_new = jnp.exp(new_high - highest)
    out = (f_old * old_mix + f_new * new_mix) / (f_old * old_total + f_new * new_total)
    out = out.reshape(ROWS, 8, HD)
    oa[:, :, 0:HD] = out[:, 0:STEPS].astype(BF16)
    oa[:, :, HD:] = out[:, STEPS:].astype(BF16)

    @pl.when(core == 0)
    def _():
        sent(SENT_0)

    @pl.when(core == 1)
    def _():
        sent(SENT_1)


def store(a, b, c, a_h, b_h, c_h, sem):
    copies = [
        pltpu.make_async_copy(src, dst, sem.at[n])
        for n, (src, dst) in enumerate(((a, a_h), (b, b_h), (c, c_h)))
    ]
    for copy in copies:
        copy.start()
    for copy in copies:
        copy.wait()


def shards(
    learn_input,
    cotangent,
    rewards,
    group_ids,
    adapter_down,
    adapter_up,
    frozen_weight,
    hidden,
    queries,
    key_cache,
    value_cache,
    cache_lengths,
):
    hbm = pl.BlockSpec(memory_space=pltpu.HBM)
    operands = (
        learn_input,
        jnp.transpose(cotangent, (1, 2, 0)).reshape(128, TOK),
        adapter_down,
        adapter_up,
        hidden,
        frozen_weight,
        queries.reshape(ROWS, 128, HD),
        key_cache.reshape(ROWS, CACHE_DEV * KVH, HD),
        value_cache.reshape(ROWS, CACHE_DEV * KVH, HD),
    )
    out_shape = (
        jax.ShapeDtypeStruct((2, RANK, FEAT), F32),
        jax.ShapeDtypeStruct((2, RANK, RANK), F32),
        jax.ShapeDtypeStruct((ROWS, STEPS, 2 * HD), BF16),
    )
    vmem = pl.BlockSpec(memory_space=pltpu.VMEM)
    results = pl.pallas_call(
        kernel,
        out_shape=out_shape,
        in_specs=[hbm] * 12,
        out_specs=(vmem,) * 3,
        scratch_shapes=[
            pltpu.SMEM((SEQ_DEV,), F32),
            pltpu.SMEM((SEQ_DEV,), jnp.int32),
            pltpu.SMEM((ROWS,), jnp.int32),
        ]
        + [pltpu.VMEM(o.shape, o.dtype) for o in operands]
        + [
            pltpu.VMEM((TOK, FEAT), BF16),
            pltpu.VMEM((2, RANK, TOK), BF16),
            pltpu.VMEM((RANK, TOK), BF16),
            pltpu.VMEM((ROWS * STEPS, FEAT), F32),
            pltpu.VMEM((2, 16, ROWS * STEPS, FEAT), BF16),
            pltpu.VMEM((2, 16, 128), F32),
            pltpu.VMEM((2, 16, 16, 128), BF16),
            pltpu.VMEM((64, 16, 128), BF16),
            pltpu.VMEM((2, 16, 16, 128), BF16),
            pltpu.VMEM((2, 2, 16, 16, 128), BF16),
            pltpu.VMEM((2, 2, 16, 128), BF16),
            pltpu.VMEM((2, 2, 4, 2, 16, 128), BF16),
            pltpu.VMEM((16, 16, 128), BF16),
            pltpu.VMEM((15, 16, 128), BF16),
            pltpu.VMEM((16, 16, 128), BF16),
            pltpu.VMEM((16, 16, 128), BF16),
            pltpu.VMEM((16, 2, 128), F32),
            pltpu.VMEM((15, 2, 128), F32),
            pltpu.VMEM((16, 2, 128), F32),
            pltpu.VMEM((16, 2, 128), F32),
            pltpu.VMEM((16, 32, 128), BF16),
            pltpu.VMEM((7, 2, 32, 128), BF16),
            pltpu.VMEM((32, 128), F32),
            pltpu.VMEM((32, 128), F32),
            pltpu.VMEM((32, 128), F32),
            pltpu.VMEM((32, 128), F32),
            pltpu.VMEM((16, 64, HD), BF16),
            pltpu.VMEM((7, 2, 64, HD), BF16),
            pltpu.VMEM((64, HD), BF16),
            pltpu.VMEM((64, HD), BF16),
            pltpu.VMEM((16, 8, 128), F32),
            pltpu.VMEM((7, 2, 8, 128), F32),
            pltpu.VMEM((8, 128), F32),
            pltpu.VMEM((8, 128), F32),
            pltpu.VMEM((2, 16, 128), BF16),
            pltpu.VMEM((8, 2, 16, 128), BF16),
            pltpu.VMEM((2, 16, 128), BF16),
            pltpu.VMEM((2, 2, 16, 128), BF16),
            pltpu.VMEM((ROWS, 128, HD), F32),
            pltpu.VMEM((SENT_1, 2, 128), F32),
            pltpu.SemaphoreType.DMA((12,)),
            pltpu.SemaphoreType.DMA((1,)),
            pltpu.SemaphoreType.DMA((N_CHAN,)),
        ],
        compiler_params=pltpu.CompilerParams(
            collective_id=0, has_side_effects=True, vmem_limit_bytes=VMEM_LIMIT
        ),
    )(
        *(
            pltpu.with_memory_space_constraint(o, pltpu.HBM)
            for o in (rewards, group_ids, cache_lengths, *operands)
        )
    )
    return pl.pallas_call(
        store,
        out_shape=out_shape,
        in_specs=[vmem] * 3,
        out_specs=(hbm,) * 3,
        scratch_shapes=[pltpu.SemaphoreType.DMA((3,))],
    )(*(pltpu.with_memory_space_constraint(r, pltpu.VMEM) for r in results))


def solution(mesh):
    return jax.shard_map(
        shards,
        mesh=mesh,
        in_specs=(
            P("dp", "tensor"),
            P("dp", None, "tensor"),
            P("dp"),
            P("dp"),
            P(None, None, "tensor"),
            P(None, None, "tensor"),
            P(None, "tensor", None),
            P("dp", None, "tensor"),
            P("dp", None, None, None),
            P("dp", "tensor", None, None),
            P("dp", "tensor", None, None),
            P("dp"),
        ),
        out_specs=(P(None, None, "tensor"), P(None, None, "tensor"), P("dp", None, "tensor")),
        check_vma=False,
    )
```

```python
import math

import jax
import jax.numpy as jnp
from jax import lax
from jax.experimental import pallas as pl
from jax.experimental.pallas import tpu as pltpu
from jax.sharding import PartitionSpec as P

MESH = pl.DeviceIdType.MESH
F32 = jnp.float32
BF16 = jnp.bfloat16

N_TP = 16
N_Y = 8
N_CHIP = 16
RANK = 64
SEQ_DEV = 8
SEQ_LEN = 32
TOK = SEQ_DEV * SEQ_LEN
FEAT = 512
ROWS = 8
STEPS = 4
CACHE_DEV = 48
KVH = 8
HD = 128
VMEM_LIMIT = 32 * 1024 * 1024

adapter_scale = 2.0
step_size = 0.004
masked_score = -1e30
score_scale = 1.0 / math.sqrt(HD)

(REW, GID, COT, UP, X, DOWN, HID, FRO, LEN, QRY, KEY, VAL) = range(12)
(
    RS1B,
    RS1P,
    AG1B,
    AG1P,
    XC,
    WC,
    HZ,
    HX,
    HC1,
    HC2A,
    HC2B,
    HC2C,
    LRS,
    RS2,
    RS2U,
    AG2,
    AG2U,
    BASEY,
    BASEZ,
    BASEP,
    MIXY,
    STATY,
    MIXZ,
    STATZ,
    LOW,
    DOWNC,
    UPC,
    UPX,
    N_CHAN,
) = range(29)


TILE = 4
SENT_BOTH = (
    2 * 16 * TILE
    + 32 + 256
    + (3 + 12 + 4 + 12) * 32
    + 31 * TILE
    + 2 * 15 * TILE + 64
    + 2 * 15 + 16 + 2 * 8
    + 14 * 8 + 2 * 16
    + 14 * (16 + TILE) + 16 + TILE
)
SENT_0 = SENT_BOTH + TILE
SENT_1 = SENT_BOTH + 2 * 2 * 16 * TILE + 16 * 2 * TILE


def dot(a, b):
    return lax.dot_general(a, b, (((1,), (0,)), ((), ())), preferred_element_type=F32)


def dot_nt(a, b):
    return lax.dot_general(a, b, (((1,), (1,)), ((), ())), preferred_element_type=F32)


def iota(shape, axis):
    return lax.broadcasted_iota(jnp.int32, shape, axis)


def fold(a):
    n = a.shape[0] // 2
    return jnp.concatenate([a[:n], a[n:]], axis=1)


def unfold(a):
    return jnp.concatenate([a[:, :RANK], a[:, RANK:]], axis=0)


def by_tiles(tiles):
    return jnp.concatenate(
        [jnp.concatenate([tiles[r, 0], tiles[r, 1]], axis=1) for r in range(4)], axis=0
    )


def kernel(
    rew_h,
    gid_h,
    len_h,
    x_h,
    cot_h,
    down_h,
    up_h,
    hid_h,
    fro_h,
    q_h,
    k_h,
    v_h,
    od,
    ou,
    oa,
    rew,
    gid,
    lens,
    x,
    cot,
    down,
    up,
    hid,
    fro,
    qry,
    key,
    val,
    x_c,
    wt,
    wt_c,
    hid_f,
    h_all,
    h_down,
    l_send,
    l_r,
    pb_send,
    rs1,
    ag1_send,
    ag1,
    g_send,
    rs2,
    ag2,
    ag2_c,
    gu_send,
    rs2u,
    agu,
    agu_c,
    base_send,
    base_r,
    basez_send,
    basez_r,
    basep_send,
    basep_r,
    mix_send,
    mix_r,
    mixz_send,
    mixz_r,
    st_send,
    st_r,
    stz_send,
    stz_r,
    low_send,
    low_r,
    upx_send,
    upx_r,
    qp,
    all_sent,
    in_sem,
    send,
    recv,
):
    dp = lax.axis_index("dp")
    tp = lax.axis_index("tensor")
    chip = lax.div(dp, 2)
    core = lax.rem(dp, 2)
    z_hi = lax.div(tp, N_Y)
    y = lax.rem(tp, N_Y)
    def two_along_z(q):
        return q + 2 - 4 * lax.rem(lax.div(q, 2), 2)

    middle = 2 * two_along_z(chip)
    column = 4 * lax.div(chip, 4)
    z_lo = lax.rem(chip, 4)
    other_core = 2 * chip + 1 - core
    pair = tp + 1 - 2 * lax.rem(tp, 2)
    other_half = y + N_Y * (1 - z_hi)

    hbm = (rew_h, gid_h, cot_h, up_h, x_h, down_h, hid_h, fro_h, len_h, q_h, k_h, v_h)
    own = (rew, gid, cot, up, x, down, hid, fro, lens, qry, key, val)
    loads = [pltpu.make_async_copy(h, v, in_sem.at[n]) for n, (h, v) in enumerate(zip(hbm, own))]
    for load in loads:
        load.start()

    ys = [lax.rem(y + o, N_Y) for o in (4, 3, 5, 2, 6, 1, 7, 0)]
    tps = [N_Y * h + t for t in ys for h in (1 - z_hi, z_hi)]
    chips = [lax.rem(chip + o, N_CHIP) for o in (8, 7, 9, 6, 10, 5, 11, 4, 12, 3, 13, 2, 14, 1, 15)]

    z_near = [column + lax.rem(z_lo + o, 4) for o in (2, 1, 3)]
    x_near = [lax.rem(chip + 4 * o, N_CHIP) for o in (2, 1, 3)]

    barrier = pltpu.get_barrier_semaphore()

    def greet(device):
        pl.semaphore_signal(barrier, inc=1, device_id=device, device_id_type=MESH)

    @pl.when(core == 1)
    def _():
        for t in tps:
            greet({"dp": middle, "tensor": t})
            greet({"dp": middle + 1, "tensor": t})

    for q in chips:
        greet({"dp": 2 * q + core})
    greet({"dp": other_core})
    for t in ys[:-1]:
        greet({"tensor": N_Y * z_hi + t})

    def remote(src, dst, chan, device):
        return pltpu.make_async_remote_copy(
            src_ref=src,
            dst_ref=dst,
            send_sem=send.at[0],
            recv_sem=recv.at[chan],
            device_id=device,
            device_id_type=MESH,
        )

    def landed(ref, chan):
        pltpu.make_async_copy(ref, ref, recv.at[chan]).wait()

    def sent(size):
        ref = all_sent.at[pl.ds(0, size)]
        pltpu.make_async_copy(ref, ref, send.at[0]).wait()

    def summed(ref, start, stop):
        blocks = [ref[n].astype(F32) for n in range(start, stop)]
        while len(blocks) > 1:
            blocks = [sum(blocks[n + 1 : n + 2], blocks[n]) for n in range(0, len(blocks), 2)]
        return blocks[0]

    loads[REW].wait()
    loads[GID].wait()
    lane_seq = lax.div(iota((1, TOK), 1), SEQ_LEN)
    rew_l = jnp.zeros((1, TOK), F32)
    gid_l = jnp.zeros((1, TOK), jnp.int32)
    for s in range(SEQ_DEV):
        rew_l = jnp.where(lane_seq == s, rew[s], rew_l)
        gid_l = jnp.where(lane_seq == s, gid[s], gid_l)
    cnt = jnp.zeros((1, TOK), F32)
    tot = jnp.zeros((1, TOK), F32)
    for s in range(SEQ_DEV):
        same = gid_l == gid[s]
        cnt = cnt + jnp.where(same, 1.0, 0.0)
        tot = tot + jnp.where(same, rew[s], 0.0)
    mean = tot / cnt
    spread = jnp.zeros((1, TOK), F32)
    for s in range(SEQ_DEV):
        off = rew[s] - mean
        spread = spread + jnp.where(gid_l == gid[s], off * off, 0.0)
    adv = (rew_l - mean) / jnp.maximum(jnp.sqrt(spread / cnt), 1.0)
    token_weight = adv / SEQ_LEN

    def put_pieces(part, k, product):
        product = product.astype(BF16)
        for r in range(4):
            for half in range(2):
                pb_send[part, (4 * k + r) * 2 + half] = product[
                    16 * r : 16 * (r + 1), 128 * half : 128 * (half + 1)
                ]

    loads[COT].wait()
    loads[UP].wait()
    for k in range(2):
        wt[k] = (cot[RANK * k : RANK * (k + 1)].astype(F32) * token_weight).astype(BF16)
        put_pieces(0, k, dot(up[k].astype(BF16), wt[k]))

    pl.semaphore_wait(barrier, N_TP + N_CHIP + N_Y - 1)

    def send_pieces(part, chan):
        for s, t in enumerate(tps):
            device = {"dp": middle + 1, "tensor": t}
            remote(pb_send.at[part, t], rs1.at[part, core, s], chan, device).start()

    send_pieces(0, RS1B)
    loads[X].wait()
    loads[DOWN].wait()
    for k in range(2):
        put_pieces(1, k, dot_nt(down[k].astype(BF16), x[...]))
    send_pieces(1, RS1P)
    to_core = {"dp": other_core}
    remote(wt.at[1 - core], wt_c, WC, to_core).start()
    remote(x, x_c, XC, to_core).start()

    loads[HID].wait()
    for i in range(ROWS):
        hid_f[STEPS * i : STEPS * (i + 1), :] = hid[i].astype(F32)
    hid_b = hid_f[...].astype(BF16)
    h_all[core, chip] = hid_b
    rows = h_all.at[core, chip]
    for q in z_near:
        remote(rows, rows, HZ, {"dp": 2 * q + core}).start()
    for q in x_near:
        remote(rows, rows, HX, {"dp": 2 * q + core}).start()

    loads[FRO].wait()
    for part in range(4):
        cols = slice(part * 256, (part + 1) * 256)
        new_k = dot(hid_b, fro[0, :, cols]).astype(BF16)
        new_v = dot(hid_b, fro[1, :, cols]).astype(BF16)
        for n in range(4):
            half = slice(RANK * n, RANK * (n + 1))
            base_send[4 * part + n] = jnp.concatenate([new_k[:, half], new_v[:, half]], axis=1)

    for s, to in enumerate(ys[:-1]):
        for z in range(2):
            t = N_Y * z + to
            device = {"tensor": N_Y * z_hi + to}
            remote(base_send.at[t], base_r.at[s, z], BASEY, device).start()

    loads[LEN].wait()
    loads[QRY].wait()
    loads[KEY].wait()
    loads[VAL].wait()
    out_row = iota((128, 128), 0)
    head = 2 * lax.div(out_row, 8) + lax.rem(lax.div(out_row, STEPS), 2)
    source = lax.rem(out_row, STEPS) * 32 + head
    perm = jnp.where(iota((128, 128), 1) == source, 1.0, 0.0).astype(BF16)
    lane_n = iota((128, CACHE_DEV * KVH), 1)
    own_group = lax.rem(lane_n, KVH) == lax.div(iota((128, CACHE_DEV * KVH), 0), 16)
    position = tp * CACHE_DEV + lax.div(lane_n, KVH)
    st_lane = iota((128, 128), 1)

    def attend(i, stats):
        q = dot(perm, qry[i])
        qp[i] = q
        score = dot_nt(q.astype(BF16), key[i]) * score_scale
        valid = jnp.logical_and(own_group, position < lens[i])
        score = jnp.where(valid, score, masked_score)
        high = jnp.max(score, axis=1, keepdims=True)
        weight = jnp.where(valid, jnp.exp(score - high), 0.0)
        total = jnp.sum(weight, axis=1, keepdims=True)
        mix = dot(weight.astype(BF16), val[i])
        stats = jnp.where(st_lane == i, high, stats)
        stats = jnp.where(st_lane == i + ROWS, total, stats)
        return mix.reshape(N_TP, 8, HD), stats

    def attend_pair(n, stats):
        m0, stats = attend(2 * n, stats)
        m1, stats = attend(2 * n + 1, stats)
        mix_send[:, pl.ds(pl.multiple_of(16 * n, 16), 16), :] = jnp.concatenate(
            [m0, m1], axis=1
        ).astype(BF16)
        return stats

    stats = lax.fori_loop(0, 4, attend_pair, jnp.zeros((128, 128), F32))
    st_send[...] = stats.reshape(N_TP, 8, 128)

    owned_k = lax.div(tp, N_Y)
    owned_r = lax.div(lax.rem(tp, N_Y), 2)
    owned_half = lax.rem(tp, 2)

    def products_sum(part, chan_in, chan_out):
        @pl.when(core == 1)
        def _():
            landed(rs1.at[part], chan_in)
            for c in range(2):
                ag1_send[part, c] = summed(rs1.at[part, c], 0, N_TP).astype(BF16)
                for t in tps:
                    device = {"dp": middle + owned_k, "tensor": t}
                    place = ag1.at[part, c, owned_r, owned_half]
                    remote(ag1_send.at[part, c], place, chan_out, device).start()

    products_sum(0, RS1B, AG1B)

    products_sum(1, RS1P, AG1P)

    landed(h_all.at[0, pl.ds(0, 3)], HZ)
    for q in x_near:
        for n in z_near:
            rows = h_all.at[core, n]
            remote(rows, rows, HX, {"dp": 2 * q + core}).start()
    rows = h_all.at[core, pl.ds(column, 4)]
    remote(rows, rows, HC1, to_core).start()

    landed(x_c, XC)
    landed(wt_c, WC)
    landed(h_all.at[0, pl.ds(0, 4)], HC1)
    down_b = down[core].astype(BF16)
    for c in range(2):
        h_down[c] = fold(dot_nt(h_all[c, chip], down_b))

    for s, to in enumerate(ys[:-1]):
        for z in range(2):
            t = N_Y * z + to
            device = {"tensor": N_Y * z_hi + to}
            remote(st_send.at[t], st_r.at[s, z], STATY, device).start()
            remote(mix_send.at[t], mix_r.at[s, z], MIXY, device).start()

    landed(ag1.at[0], AG1B)

    g_down = dot(by_tiles(ag1[0, core]), x[...]) + dot(by_tiles(ag1[0, 1 - core]), x_c[...])
    g_down = g_down.astype(BF16)
    for n in range(N_CHIP):
        r, c = n // 4, n % 4
        g_send[n] = g_down[16 * r : 16 * (r + 1), 128 * c : 128 * (c + 1)]
    for s, q in enumerate(chips):
        remote(g_send.at[q], rs2.at[s], RS2, {"dp": 2 * q + core}).start()

    def rows_product(xo, c):
        places = pl.ds(lax.rem(column + 4 * xo, N_CHIP), 4)
        part = step_size * adapter_scale * dot_nt(h_all[c, places].reshape(128, FEAT), g_down)
        part = part.reshape(4, 2, 16, RANK)
        l_send[c, places] = jnp.concatenate([part[:, 0], part[:, 1]], axis=2).astype(BF16)

    def rows_send(xo, zo, half):
        q = lax.rem(column + 4 * xo, N_CHIP) + lax.rem(z_lo + zo, 4)
        slot = 2 * (4 * xo + zo) + lax.rem(half + z_hi, 2)
        device = {"dp": 2 * q + 1, "tensor": N_Y * half + y}
        place = l_r.at[2 * N_CHIP * core + slot]
        remote(l_send.at[half, two_along_z(q)], place, LRS, device).start()

    for c in range(2):
        rows_product(0, c)
        own = step_size * adapter_scale * fold(dot_nt(h_all[c, chip], g_down))
        l_send[c, chip] = (own + h_down[c]).astype(BF16)
    for zo in (2, 1, 3):
        rows_send(0, zo, 1 - z_hi)
        rows_send(0, zo, z_hi)
    rows_send(0, 0, 1 - z_hi)
    last = l_send.at[z_hi, two_along_z(chip)]

    @pl.when(core == 0)
    def _():
        remote(last, l_r.at[0], LRS, to_core).start()

    @pl.when(core == 1)
    def _():
        l_r[2 * N_CHIP] = last[...]

    landed(ag1.at[1], AG1P)

    g_up = dot_nt(by_tiles(ag1[1, core]), wt[core]) + dot_nt(by_tiles(ag1[1, 1 - core]), wt_c[...])
    g_up = fold(g_up)
    for n in range(N_CHIP):
        gu_send[n] = g_up[2 * n : 2 * (n + 1)]
    for s, q in enumerate(chips):
        remote(gu_send.at[q], rs2u.at[s], RS2U, {"dp": 2 * q + core}).start()

    landed(h_all.at[0, pl.ds(0, 12)], HX)
    far_columns = ((1, HC2A), (2, HC2B), (3, HC2C))
    for xo, chan in far_columns:
        rows = h_all.at[core, pl.ds(lax.rem(column + 4 * xo, N_CHIP), 4)]
        remote(rows, rows, chan, to_core).start()

    for xo, _ in far_columns:
        rows_product(xo, core)
        for zo in (2, 1, 3, 0):
            rows_send(xo, zo, core)
    for xo, chan in far_columns:
        landed(h_all.at[0, pl.ds(0, 4)], chan)
        rows_product(xo, 1 - core)
        for zo in (2, 1, 3, 0):
            rows_send(xo, zo, 1 - core)

    landed(base_r, BASEY)

    def base_sum(z):
        first = base_send[N_Y * z + y].astype(F32)
        return lax.fori_loop(
            0, N_Y - 1, lambda s, acc: acc + base_r[s, z].astype(F32), first
        )

    to_half = {"tensor": other_half}
    basez_send[...] = base_sum(1 - z_hi)
    remote(basez_send, basez_r, BASEZ, to_half).start()
    base = base_sum(z_hi)

    landed(rs2, RS2)

    ag2[chip] = (g_send[chip].astype(F32) + summed(rs2, 0, N_CHIP - 1)).astype(BF16)

    for q in chips:
        remote(ag2.at[chip], ag2.at[chip], AG2, {"dp": 2 * q + core}).start()

    landed(rs2u, RS2U)
    agu[chip] = gu_send[chip] + summed(rs2u, 0, N_CHIP - 1)
    for q in chips:
        remote(agu.at[chip], agu.at[chip], AG2U, {"dp": 2 * q + core}).start()

    landed(st_r, STATY)
    landed(mix_r, MIXY)

    def combine(st, mix, count):
        top = st(0)
        for s in range(1, count):
            top = jnp.maximum(top, st(s))
        total = jnp.zeros((8, 128), F32)
        acc = [jnp.zeros((8, 128), F32)] * ROWS
        for s in range(count):
            factor = jnp.exp(st(s) - top)
            total = total + factor * pltpu.roll(st(s), 128 - ROWS, 1)
            block = mix(s)
            for i in range(ROWS):
                acc[i] = acc[i] + factor[:, i : i + 1] * block[8 * i : 8 * (i + 1)].astype(F32)
        return top, total, acc

    def combine_y(z):
        t = N_Y * z + y
        return combine(
            lambda s: st_send[t] if s == 0 else st_r[s - 1, z],
            lambda s: mix_send[t] if s == 0 else mix_r[s - 1, z],
            N_Y,
        )

    def packed(top, total):
        return jnp.where(iota((8, 128), 1) < ROWS, top, pltpu.roll(total, ROWS, 1))

    top, total, acc = combine_y(1 - z_hi)
    stz_send[...] = packed(top, total)
    remote(stz_send, stz_r, STATZ, to_half).start()
    mixz_send[...] = jnp.concatenate(acc, axis=0).astype(BF16)
    remote(mixz_send, mixz_r, MIXZ, to_half).start()
    top, total, acc = combine_y(z_hi)
    own_st = packed(top, total)
    own_mix = jnp.concatenate(acc, axis=0)

    @pl.when(core == 1)
    def _():
        landed(l_r.at[pl.ds(0, 4 * N_CHIP - 1)], LRS)
        for k in range(2):
            low_send[k] = summed(l_r, 2 * N_CHIP * k, 2 * N_CHIP * (k + 1)).astype(BF16)
        for t in tps:
            device = {"dp": middle + z_hi, "tensor": t}
            remote(low_send, low_r.at[y], LOW, device).start()

    landed(basez_r, BASEZ)
    base = base + basez_r[...]
    basep_send[...] = base
    remote(basep_send, basep_r, BASEP, {"tensor": pair}).start()

    landed(ag2.at[pl.ds(0, N_CHIP - 1)], AG2)
    remote(ag2, ag2_c, DOWNC, to_core).start()

    def tiles_of(ref):
        return jnp.concatenate(
            [jnp.concatenate([ref[4 * r + c] for c in range(4)], axis=1) for r in range(4)], axis=0
        ).astype(F32)

    od[core] = down[core] + step_size * (adapter_scale * tiles_of(ag2))

    landed(agu.at[pl.ds(0, N_CHIP - 1)], AG2U)

    def up_updated(k, grad):
        return up[k] + step_size * (adapter_scale * unfold(grad.reshape(32, 128)))

    new_up = up_updated(core, agu[...])
    upx_send[...] = fold(new_up).astype(BF16).reshape(2, 16, 128)
    remote(agu, agu_c, UPC, to_core).start()
    remote(upx_send, upx_r.at[0], UPX, {"tensor": pair}).start()
    remote(upx_send, upx_r.at[1], UPX, {"dp": other_core, "tensor": pair}).start()
    ou[core] = new_up

    landed(ag2_c, DOWNC)
    od[1 - core] = down[1 - core] + step_size * (adapter_scale * tiles_of(ag2_c))
    landed(agu_c, UPC)
    new_up_c = up_updated(1 - core, agu_c[...])
    ou[1 - core] = new_up_c

    landed(upx_r, UPX)
    even = lax.rem(tp, 2) == 0

    def both(mine, theirs):
        left = jnp.where(even, mine, theirs)
        right = jnp.where(even, theirs, mine)
        return jnp.concatenate([left, right], axis=1)

    def columns(mine, theirs):
        return both(mine, unfold(theirs.reshape(32, 128)).astype(F32)).astype(BF16)

    up_own = columns(new_up, upx_r[0])
    up_oth = columns(new_up_c, upx_r[1])
    landed(basep_r, BASEP)
    base_k = both(base[:, :RANK], basep_r[:, :RANK])
    base_v = both(base[:, RANK:], basep_r[:, RANK:])

    landed(stz_r, STATZ)
    landed(mixz_r, MIXZ)
    top, total, acc = combine(
        lambda s: stz_r[...] if s else own_st, lambda s: mixz_r[...] if s else own_mix, 2
    )
    old_high = jnp.concatenate([top[:, i : i + 1] for i in range(ROWS)], axis=0)
    old_total = jnp.concatenate([total[:, i : i + 1] for i in range(ROWS)], axis=0)
    old_mix = jnp.concatenate(acc, axis=0)
    own_q = qp[:, pl.ds(pl.multiple_of(8 * tp, 8), 8), :].reshape(64, HD).astype(BF16)

    landed(low_r, LOW)

    low_own = unfold(summed(low_r.at[:, core], 0, N_Y)).astype(BF16)
    low_oth = unfold(summed(low_r.at[:, 1 - core], 0, N_Y)).astype(BF16)
    from_own = adapter_scale * dot(low_own, up_own)
    from_oth = adapter_scale * dot(low_oth, up_oth)
    first = core == 0
    new_k = (base_k + jnp.where(first, from_own, from_oth)).astype(BF16)
    new_v = (base_v + jnp.where(first, from_oth, from_own)).astype(BF16)
    row = iota((64, 32), 0)
    col = iota((64, 32), 1)
    causal = jnp.logical_and(
        lax.div(row, 8) == lax.div(col, STEPS), lax.rem(col, STEPS) <= lax.rem(row, STEPS)
    )
    score = jnp.where(causal, dot_nt(own_q, new_k) * score_scale, masked_score)
    new_high = jnp.max(score, axis=1, keepdims=True)
    weight = jnp.where(causal, jnp.exp(score - new_high), 0.0)
    new_total = jnp.sum(weight, axis=1, keepdims=True)
    new_mix = dot(weight.astype(BF16), new_v)
    highest = jnp.maximum(old_high, new_high)
    f_old = jnp.exp(old_high - highest)
    f_new = jnp.exp(new_high - highest)
    out = (f_old * old_mix + f_new * new_mix) / (f_old * old_total + f_new * new_total)
    out = out.reshape(ROWS, 8, HD)
    oa[:, :, 0:HD] = out[:, 0:STEPS].astype(BF16)
    oa[:, :, HD:] = out[:, STEPS:].astype(BF16)

    @pl.when(core == 0)
    def _():
        sent(SENT_0)

    @pl.when(core == 1)
    def _():
        sent(SENT_1)


def store(a, b, c, a_h, b_h, c_h, sem):
    copies = [
        pltpu.make_async_copy(src, dst, sem.at[n])
        for n, (src, dst) in enumerate(((a, a_h), (b, b_h), (c, c_h)))
    ]
    for copy in copies:
        copy.start()
    for copy in copies:
        copy.wait()


def shards(
    learn_input,
    cotangent,
    rewards,
    group_ids,
    adapter_down,
    adapter_up,
    frozen_weight,
    hidden,
    queries,
    key_cache,
    value_cache,
    cache_lengths,
):
    hbm = pl.BlockSpec(memory_space=pltpu.HBM)
    operands = (
        learn_input,
        jnp.transpose(cotangent, (1, 2, 0)).reshape(128, TOK),
        adapter_down,
        adapter_up,
        hidden,
        frozen_weight,
        queries.reshape(ROWS, 128, HD),
        key_cache.reshape(ROWS, CACHE_DEV * KVH, HD),
        value_cache.reshape(ROWS, CACHE_DEV * KVH, HD),
    )
    out_shape = (
        jax.ShapeDtypeStruct((2, RANK, FEAT), F32),
        jax.ShapeDtypeStruct((2, RANK, RANK), F32),
        jax.ShapeDtypeStruct((ROWS, STEPS, 2 * HD), BF16),
    )
    vmem = pl.BlockSpec(memory_space=pltpu.VMEM)
    results = pl.pallas_call(
        kernel,
        out_shape=out_shape,
        in_specs=[hbm] * 12,
        out_specs=(vmem,) * 3,
        scratch_shapes=[
            pltpu.SMEM((SEQ_DEV,), F32),
            pltpu.SMEM((SEQ_DEV,), jnp.int32),
            pltpu.SMEM((ROWS,), jnp.int32),
        ]
        + [pltpu.VMEM(o.shape, o.dtype) for o in operands]
        + [
            pltpu.VMEM((TOK, FEAT), BF16),
            pltpu.VMEM((2, RANK, TOK), BF16),
            pltpu.VMEM((RANK, TOK), BF16),
            pltpu.VMEM((ROWS * STEPS, FEAT), F32),
            pltpu.VMEM((2, 16, ROWS * STEPS, FEAT), BF16),
            pltpu.VMEM((2, 16, 128), F32),
            pltpu.VMEM((2, 16, 16, 128), BF16),
            pltpu.VMEM((64, 16, 128), BF16),
            pltpu.VMEM((2, 16, 16, 128), BF16),
            pltpu.VMEM((2, 2, 16, 16, 128), BF16),
            pltpu.VMEM((2, 2, 16, 128), BF16),
            pltpu.VMEM((2, 2, 4, 2, 16, 128), BF16),
            pltpu.VMEM((16, 16, 128), BF16),
            pltpu.VMEM((15, 16, 128), BF16),
            pltpu.VMEM((16, 16, 128), BF16),
            pltpu.VMEM((16, 16, 128), BF16),
            pltpu.VMEM((16, 2, 128), F32),
            pltpu.VMEM((15, 2, 128), F32),
            pltpu.VMEM((16, 2, 128), F32),
            pltpu.VMEM((16, 2, 128), F32),
            pltpu.VMEM((16, 32, 128), BF16),
            pltpu.VMEM((7, 2, 32, 128), BF16),
            pltpu.VMEM((32, 128), F32),
            pltpu.VMEM((32, 128), F32),
            pltpu.VMEM((32, 128), F32),
            pltpu.VMEM((32, 128), F32),
            pltpu.VMEM((16, 64, HD), BF16),
            pltpu.VMEM((7, 2, 64, HD), BF16),
            pltpu.VMEM((64, HD), BF16),
            pltpu.VMEM((64, HD), BF16),
            pltpu.VMEM((16, 8, 128), F32),
            pltpu.VMEM((7, 2, 8, 128), F32),
            pltpu.VMEM((8, 128), F32),
            pltpu.VMEM((8, 128), F32),
            pltpu.VMEM((2, 16, 128), BF16),
            pltpu.VMEM((8, 2, 16, 128), BF16),
            pltpu.VMEM((2, 16, 128), BF16),
            pltpu.VMEM((2, 2, 16, 128), BF16),
            pltpu.VMEM((ROWS, 128, HD), F32),
            pltpu.VMEM((SENT_1, 2, 128), F32),
            pltpu.SemaphoreType.DMA((12,)),
            pltpu.SemaphoreType.DMA((1,)),
            pltpu.SemaphoreType.DMA((N_CHAN,)),
        ],
        compiler_params=pltpu.CompilerParams(
            collective_id=0, has_side_effects=True, vmem_limit_bytes=VMEM_LIMIT
        ),
    )(
        *(
            pltpu.with_memory_space_constraint(o, pltpu.HBM)
            for o in (rewards, group_ids, cache_lengths, *operands)
        )
    )
    return pl.pallas_call(
        store,
        out_shape=out_shape,
        in_specs=[vmem] * 3,
        out_specs=(hbm,) * 3,
        scratch_shapes=[pltpu.SemaphoreType.DMA((3,))],
    )(*(pltpu.with_memory_space_constraint(r, pltpu.VMEM) for r in results))


def solution(mesh):
    return jax.shard_map(
        shards,
        mesh=mesh,
        in_specs=(
            P("dp", "tensor"),
            P("dp", None, "tensor"),
            P("dp"),
            P("dp"),
            P(None, None, "tensor"),
            P(None, None, "tensor"),
            P(None, "tensor", None),
            P("dp", None, "tensor"),
            P("dp", None, None, None),
            P("dp", "tensor", None, None),
            P("dp", "tensor", None, None),
            P("dp"),
        ),
        out_specs=(P(None, None, "tensor"), P(None, None, "tensor"), P("dp", None, "tensor")),
        check_vma=False,
    )
```

```python
import math

import jax
import jax.numpy as jnp
from jax import lax
from jax.experimental import pallas as pl
from jax.experimental.pallas import tpu as pltpu
from jax.sharding import PartitionSpec as P

MESH = pl.DeviceIdType.MESH
F32 = jnp.float32
BF16 = jnp.bfloat16

N_TP = 16
N_Y = 8
N_CHIP = 16
RANK = 64
SEQ_DEV = 8
SEQ_LEN = 32
TOK = SEQ_DEV * SEQ_LEN
FEAT = 512
ROWS = 8
STEPS = 4
CACHE_DEV = 48
KVH = 8
HD = 128
VMEM_LIMIT = 32 * 1024 * 1024

adapter_scale = 2.0
step_size = 0.004
masked_score = -1e30
score_scale = 1.0 / math.sqrt(HD)

(REW, GID, COT, UP, X, DOWN, HID, FRO, LEN, QRY, KEY, VAL) = range(12)
(
    RS1B,
    RS1P,
    AG1B,
    AG1P,
    XC,
    WC,
    HZ,
    HZ_1,
    HZ_2,
    HZ_3,
    HX,
    HC1,
    HC2A,
    HC2B,
    HC2C,
    LRS,
    RS2,
    RS2U,
    AG2,
    AG2U,
    BASEY,
    BASEZ,
    BASEP,
    MIXY,
    STATY,
    MIXZ,
    STATZ,
    LOW,
    DOWNC,
    UPC,
    UPX,
    N_CHAN,
) = range(32)


TILE = 4
SENT_BOTH = (
    2 * 16 * TILE
    + 32 + 256
    + (3 + 12 + 4 + 12) * 32
    + 31 * TILE
    + 2 * 15 * TILE + 64
    + 2 * 15 + 16 + 2 * 8
    + 14 * 8 + 2 * 16
    + 14 * (16 + TILE) + 16 + TILE
)
SENT_0 = SENT_BOTH + TILE
SENT_1 = SENT_BOTH + 2 * 2 * 16 * TILE + 16 * 2 * TILE


def dot(a, b):
    return lax.dot_general(a, b, (((1,), (0,)), ((), ())), preferred_element_type=F32)


def dot_nt(a, b):
    return lax.dot_general(a, b, (((1,), (1,)), ((), ())), preferred_element_type=F32)


def iota(shape, axis):
    return lax.broadcasted_iota(jnp.int32, shape, axis)


def fold(a):
    n = a.shape[0] // 2
    return jnp.concatenate([a[:n], a[n:]], axis=1)


def unfold(a):
    return jnp.concatenate([a[:, :RANK], a[:, RANK:]], axis=0)


def by_tiles(tiles):
    return jnp.concatenate(
        [jnp.concatenate([tiles[r, 0], tiles[r, 1]], axis=1) for r in range(4)], axis=0
    )


def kernel(
    rew_h,
    gid_h,
    len_h,
    x_h,
    cot_h,
    down_h,
    up_h,
    hid_h,
    fro_h,
    q_h,
    k_h,
    v_h,
    od,
    ou,
    oa,
    rew,
    gid,
    lens,
    x,
    cot,
    down,
    up,
    hid,
    fro,
    qry,
    key,
    val,
    x_c,
    wt,
    wt_c,
    hid_f,
    h_all,
    h_down,
    l_send,
    l_r,
    pb_send,
    rs1,
    ag1_send,
    ag1,
    g_send,
    rs2,
    ag2,
    ag2_c,
    gu_send,
    rs2u,
    agu,
    agu_c,
    base_send,
    base_r,
    basez_send,
    basez_r,
    basep_send,
    basep_r,
    mix_send,
    mix_r,
    mixz_send,
    mixz_r,
    st_send,
    st_r,
    stz_send,
    stz_r,
    low_send,
    low_r,
    upx_send,
    upx_r,
    qp,
    all_sent,
    in_sem,
    send,
    recv,
):
    dp = lax.axis_index("dp")
    tp = lax.axis_index("tensor")
    chip = lax.div(dp, 2)
    core = lax.rem(dp, 2)
    z_hi = lax.div(tp, N_Y)
    y = lax.rem(tp, N_Y)
    def two_along_z(q):
        return q + 2 - 4 * lax.rem(lax.div(q, 2), 2)

    middle = 2 * two_along_z(chip)
    column = 4 * lax.div(chip, 4)
    z_lo = lax.rem(chip, 4)
    other_core = 2 * chip + 1 - core
    pair = tp + 1 - 2 * lax.rem(tp, 2)
    other_half = y + N_Y * (1 - z_hi)

    hbm = (rew_h, gid_h, cot_h, up_h, x_h, down_h, hid_h, fro_h, len_h, q_h, k_h, v_h)
    own = (rew, gid, cot, up, x, down, hid, fro, lens, qry, key, val)
    loads = [pltpu.make_async_copy(h, v, in_sem.at[n]) for n, (h, v) in enumerate(zip(hbm, own))]
    for load in loads:
        load.start()

    ys = [lax.rem(y + o, N_Y) for o in (4, 3, 5, 2, 6, 1, 7, 0)]
    tps = [N_Y * h + t for t in ys for h in (1 - z_hi, z_hi)]
    chips = [lax.rem(chip + o, N_CHIP) for o in (8, 7, 9, 6, 10, 5, 11, 4, 12, 3, 13, 2, 14, 1, 15)]

    z_near = [column + lax.rem(z_lo + o, 4) for o in (2, 1, 3)]
    x_near = [lax.rem(chip + 4 * o, N_CHIP) for o in (2, 1, 3)]

    barrier = pltpu.get_barrier_semaphore()

    def greet(device):
        pl.semaphore_signal(barrier, inc=1, device_id=device, device_id_type=MESH)

    @pl.when(core == 1)
    def _():
        for t in tps:
            greet({"dp": middle, "tensor": t})
            greet({"dp": middle + 1, "tensor": t})

    for q in chips:
        greet({"dp": 2 * q + core})
    greet({"dp": other_core})
    for t in ys[:-1]:
        greet({"tensor": N_Y * z_hi + t})

    def remote(src, dst, chan, device):
        return pltpu.make_async_remote_copy(
            src_ref=src,
            dst_ref=dst,
            send_sem=send.at[0],
            recv_sem=recv.at[chan],
            device_id=device,
            device_id_type=MESH,
        )

    def landed(ref, chan):
        pltpu.make_async_copy(ref, ref, recv.at[chan]).wait()

    def sent(size):
        ref = all_sent.at[pl.ds(0, size)]
        pltpu.make_async_copy(ref, ref, send.at[0]).wait()

    def summed(ref, start, stop):
        blocks = [ref[n].astype(F32) for n in range(start, stop)]
        while len(blocks) > 1:
            blocks = [sum(blocks[n + 1 : n + 2], blocks[n]) for n in range(0, len(blocks), 2)]
        return blocks[0]

    loads[REW].wait()
    loads[GID].wait()
    lane_seq = lax.div(iota((1, TOK), 1), SEQ_LEN)
    rew_l = jnp.zeros((1, TOK), F32)
    gid_l = jnp.zeros((1, TOK), jnp.int32)
    for s in range(SEQ_DEV):
        rew_l = jnp.where(lane_seq == s, rew[s], rew_l)
        gid_l = jnp.where(lane_seq == s, gid[s], gid_l)
    cnt = jnp.zeros((1, TOK), F32)
    tot = jnp.zeros((1, TOK), F32)
    for s in range(SEQ_DEV):
        same = gid_l == gid[s]
        cnt = cnt + jnp.where(same, 1.0, 0.0)
        tot = tot + jnp.where(same, rew[s], 0.0)
    mean = tot / cnt
    spread = jnp.zeros((1, TOK), F32)
    for s in range(SEQ_DEV):
        off = rew[s] - mean
        spread = spread + jnp.where(gid_l == gid[s], off * off, 0.0)
    adv = (rew_l - mean) / jnp.maximum(jnp.sqrt(spread / cnt), 1.0)
    token_weight = adv / SEQ_LEN

    def put_pieces(part, k, product):
        product = product.astype(BF16)
        for r in range(4):
            for half in range(2):
                pb_send[part, (4 * k + r) * 2 + half] = product[
                    16 * r : 16 * (r + 1), 128 * half : 128 * (half + 1)
                ]

    loads[COT].wait()
    loads[UP].wait()
    for k in range(2):
        wt[k] = (cot[RANK * k : RANK * (k + 1)].astype(F32) * token_weight).astype(BF16)
        put_pieces(0, k, dot(up[k].astype(BF16), wt[k]))

    pl.semaphore_wait(barrier, N_TP + N_CHIP + N_Y - 1)

    def send_pieces(part, chan):
        for s, t in enumerate(tps):
            device = {"dp": middle + 1, "tensor": t}
            remote(pb_send.at[part, t], rs1.at[part, core, s], chan, device).start()

    send_pieces(0, RS1B)
    loads[X].wait()
    loads[DOWN].wait()
    for k in range(2):
        put_pieces(1, k, dot_nt(down[k].astype(BF16), x[...]))
    send_pieces(1, RS1P)
    to_core = {"dp": other_core}
    remote(wt.at[1 - core], wt_c, WC, to_core).start()
    remote(x, x_c, XC, to_core).start()

    loads[HID].wait()
    for i in range(ROWS):
        hid_f[STEPS * i : STEPS * (i + 1), :] = hid[i].astype(F32)
    hid_b = hid_f[...].astype(BF16)
    h_all[core, chip] = hid_b
    rows = h_all.at[core, chip]
    for q in z_near:
        remote(rows, rows, HZ + z_lo, {"dp": 2 * q + core}).start()
    for q in x_near:
        remote(rows, rows, HX, {"dp": 2 * q + core}).start()

    loads[FRO].wait()
    for part in range(4):
        cols = slice(part * 256, (part + 1) * 256)
        new_k = dot(hid_b, fro[0, :, cols]).astype(BF16)
        new_v = dot(hid_b, fro[1, :, cols]).astype(BF16)
        for n in range(4):
            half = slice(RANK * n, RANK * (n + 1))
            base_send[4 * part + n] = jnp.concatenate([new_k[:, half], new_v[:, half]], axis=1)

    for s, to in enumerate(ys[:-1]):
        for z in range(2):
            t = N_Y * z + to
            device = {"tensor": N_Y * z_hi + to}
            remote(base_send.at[t], base_r.at[s, z], BASEY, device).start()

    loads[LEN].wait()
    loads[QRY].wait()
    loads[KEY].wait()
    loads[VAL].wait()
    out_row = iota((128, 128), 0)
    head = 2 * lax.div(out_row, 8) + lax.rem(lax.div(out_row, STEPS), 2)
    source = lax.rem(out_row, STEPS) * 32 + head
    perm = jnp.where(iota((128, 128), 1) == source, 1.0, 0.0).astype(BF16)
    lane_n = iota((128, CACHE_DEV * KVH), 1)
    own_group = lax.rem(lane_n, KVH) == lax.div(iota((128, CACHE_DEV * KVH), 0), 16)
    position = tp * CACHE_DEV + lax.div(lane_n, KVH)
    st_lane = iota((128, 128), 1)

    def attend(i, stats):
        q = dot(perm, qry[i])
        qp[i] = q
        score = dot_nt(q.astype(BF16), key[i]) * score_scale
        valid = jnp.logical_and(own_group, position < lens[i])
        score = jnp.where(valid, score, masked_score)
        high = jnp.max(score, axis=1, keepdims=True)
        weight = jnp.where(valid, jnp.exp(score - high), 0.0)
        total = jnp.sum(weight, axis=1, keepdims=True)
        mix = dot(weight.astype(BF16), val[i])
        stats = jnp.where(st_lane == i, high, stats)
        stats = jnp.where(st_lane == i + ROWS, total, stats)
        return mix.reshape(N_TP, 8, HD), stats

    def attend_pair(n, stats):
        m0, stats = attend(2 * n, stats)
        m1, stats = attend(2 * n + 1, stats)
        mix_send[:, pl.ds(pl.multiple_of(16 * n, 16), 16), :] = jnp.concatenate(
            [m0, m1], axis=1
        ).astype(BF16)
        return stats

    stats = lax.fori_loop(0, 4, attend_pair, jnp.zeros((128, 128), F32))
    st_send[...] = stats.reshape(N_TP, 8, 128)

    owned_k = lax.div(tp, N_Y)
    owned_r = lax.div(lax.rem(tp, N_Y), 2)
    owned_half = lax.rem(tp, 2)

    def products_sum(part, chan_in, chan_out):
        @pl.when(core == 1)
        def _():
            landed(rs1.at[part], chan_in)
            for c in range(2):
                ag1_send[part, c] = summed(rs1.at[part, c], 0, N_TP).astype(BF16)
                for t in tps:
                    device = {"dp": middle + owned_k, "tensor": t}
                    place = ag1.at[part, c, owned_r, owned_half]
                    remote(ag1_send.at[part, c], place, chan_out, device).start()

    products_sum(0, RS1B, AG1B)

    def pass_on(z):
        rows = h_all.at[core, column + z]
        landed(rows, HZ + z)
        for q in x_near:
            remote(rows, rows, HX, {"dp": 2 * q + core}).start()

    column_order = (
        jnp.where(z_lo == 0, 2, 0),
        jnp.where(lax.rem(z_lo, 2) == 1, 2, 3),
        jnp.where(z_lo == 1, 3, 1),
    )
    pass_on(column_order[0])
    pass_on(column_order[1])

    products_sum(1, RS1P, AG1P)

    pass_on(column_order[2])
    rows = h_all.at[core, pl.ds(column, 4)]
    remote(rows, rows, HC1, to_core).start()

    landed(x_c, XC)
    landed(wt_c, WC)
    landed(h_all.at[0, pl.ds(0, 4)], HC1)
    down_b = down[core].astype(BF16)
    for c in range(2):
        h_down[c] = fold(dot_nt(h_all[c, chip], down_b))

    for s, to in enumerate(ys[:-1]):
        for z in range(2):
            t = N_Y * z + to
            device = {"tensor": N_Y * z_hi + to}
            remote(st_send.at[t], st_r.at[s, z], STATY, device).start()
            remote(mix_send.at[t], mix_r.at[s, z], MIXY, device).start()

    landed(ag1.at[0], AG1B)

    g_down = dot(by_tiles(ag1[0, core]), x[...]) + dot(by_tiles(ag1[0, 1 - core]), x_c[...])
    g_down = g_down.astype(BF16)
    for n in range(N_CHIP):
        r, c = n // 4, n % 4
        g_send[n] = g_down[16 * r : 16 * (r + 1), 128 * c : 128 * (c + 1)]
    for s, q in enumerate(chips):
        remote(g_send.at[q], rs2.at[s], RS2, {"dp": 2 * q + core}).start()

    def rows_product(xo, c):
        places = pl.ds(lax.rem(column + 4 * xo, N_CHIP), 4)
        part = step_size * adapter_scale * dot_nt(h_all[c, places].reshape(128, FEAT), g_down)
        part = part.reshape(4, 2, 16, RANK)
        l_send[c, places] = jnp.concatenate([part[:, 0], part[:, 1]], axis=2).astype(BF16)

    def rows_send(xo, zo, half):
        q = lax.rem(column + 4 * xo, N_CHIP) + lax.rem(z_lo + zo, 4)
        slot = 2 * (4 * xo + zo) + lax.rem(half + z_hi, 2)
        device = {"dp": 2 * q + 1, "tensor": N_Y * half + y}
        place = l_r.at[2 * N_CHIP * core + slot]
        remote(l_send.at[half, two_along_z(q)], place, LRS, device).start()

    for c in range(2):
        rows_product(0, c)
        own = step_size * adapter_scale * fold(dot_nt(h_all[c, chip], g_down))
        l_send[c, chip] = (own + h_down[c]).astype(BF16)
    for zo in (2, 1, 3):
        rows_send(0, zo, 1 - z_hi)
        rows_send(0, zo, z_hi)
    rows_send(0, 0, 1 - z_hi)
    last = l_send.at[z_hi, two_along_z(chip)]

    @pl.when(core == 0)
    def _():
        remote(last, l_r.at[0], LRS, to_core).start()

    @pl.when(core == 1)
    def _():
        l_r[2 * N_CHIP] = last[...]

    landed(ag1.at[1], AG1P)

    g_up = dot_nt(by_tiles(ag1[1, core]), wt[core]) + dot_nt(by_tiles(ag1[1, 1 - core]), wt_c[...])
    g_up = fold(g_up)
    for n in range(N_CHIP):
        gu_send[n] = g_up[2 * n : 2 * (n + 1)]
    for s, q in enumerate(chips):
        remote(gu_send.at[q], rs2u.at[s], RS2U, {"dp": 2 * q + core}).start()

    landed(h_all.at[0, pl.ds(0, 12)], HX)
    far_columns = ((1, HC2A), (2, HC2B), (3, HC2C))
    for xo, chan in far_columns:
        rows = h_all.at[core, pl.ds(lax.rem(column + 4 * xo, N_CHIP), 4)]
        remote(rows, rows, chan, to_core).start()

    for xo, _ in far_columns:
        rows_product(xo, core)
        for zo in (2, 1, 3, 0):
            rows_send(xo, zo, core)
    for xo, chan in far_columns:
        landed(h_all.at[0, pl.ds(0, 4)], chan)
        rows_product(xo, 1 - core)
        for zo in (2, 1, 3, 0):
            rows_send(xo, zo, 1 - core)

    landed(base_r, BASEY)

    def base_sum(z):
        first = base_send[N_Y * z + y].astype(F32)
        return lax.fori_loop(
            0, N_Y - 1, lambda s, acc: acc + base_r[s, z].astype(F32), first
        )

    to_half = {"tensor": other_half}
    basez_send[...] = base_sum(1 - z_hi)
    remote(basez_send, basez_r, BASEZ, to_half).start()
    base = base_sum(z_hi)

    landed(rs2, RS2)

    ag2[chip] = (g_send[chip].astype(F32) + summed(rs2, 0, N_CHIP - 1)).astype(BF16)

    for q in chips:
        remote(ag2.at[chip], ag2.at[chip], AG2, {"dp": 2 * q + core}).start()

    landed(rs2u, RS2U)
    agu[chip] = gu_send[chip] + summed(rs2u, 0, N_CHIP - 1)
    for q in chips:
        remote(agu.at[chip], agu.at[chip], AG2U, {"dp": 2 * q + core}).start()

    landed(st_r, STATY)
    landed(mix_r, MIXY)

    def combine(st, mix, count):
        top = st(0)
        for s in range(1, count):
            top = jnp.maximum(top, st(s))
        total = jnp.zeros((8, 128), F32)
        acc = [jnp.zeros((8, 128), F32)] * ROWS
        for s in range(count):
            factor = jnp.exp(st(s) - top)
            total = total + factor * pltpu.roll(st(s), 128 - ROWS, 1)
            block = mix(s)
            for i in range(ROWS):
                acc[i] = acc[i] + factor[:, i : i + 1] * block[8 * i : 8 * (i + 1)].astype(F32)
        return top, total, acc

    def combine_y(z):
        t = N_Y * z + y
        return combine(
            lambda s: st_send[t] if s == 0 else st_r[s - 1, z],
            lambda s: mix_send[t] if s == 0 else mix_r[s - 1, z],
            N_Y,
        )

    def packed(top, total):
        return jnp.where(iota((8, 128), 1) < ROWS, top, pltpu.roll(total, ROWS, 1))

    top, total, acc = combine_y(1 - z_hi)
    stz_send[...] = packed(top, total)
    remote(stz_send, stz_r, STATZ, to_half).start()
    mixz_send[...] = jnp.concatenate(acc, axis=0).astype(BF16)
    remote(mixz_send, mixz_r, MIXZ, to_half).start()
    top, total, acc = combine_y(z_hi)
    own_st = packed(top, total)
    own_mix = jnp.concatenate(acc, axis=0)

    @pl.when(core == 1)
    def _():
        landed(l_r.at[pl.ds(0, 4 * N_CHIP - 1)], LRS)
        for k in range(2):
            low_send[k] = summed(l_r, 2 * N_CHIP * k, 2 * N_CHIP * (k + 1)).astype(BF16)
        for t in tps:
            device = {"dp": middle + z_hi, "tensor": t}
            remote(low_send, low_r.at[y], LOW, device).start()

    landed(basez_r, BASEZ)
    base = base + basez_r[...]
    basep_send[...] = base
    remote(basep_send, basep_r, BASEP, {"tensor": pair}).start()

    landed(ag2.at[pl.ds(0, N_CHIP - 1)], AG2)
    remote(ag2, ag2_c, DOWNC, to_core).start()

    def tiles_of(ref):
        return jnp.concatenate(
            [jnp.concatenate([ref[4 * r + c] for c in range(4)], axis=1) for r in range(4)], axis=0
        ).astype(F32)

    od[core] = down[core] + step_size * (adapter_scale * tiles_of(ag2))

    landed(agu.at[pl.ds(0, N_CHIP - 1)], AG2U)

    def up_updated(k, grad):
        return up[k] + step_size * (adapter_scale * unfold(grad.reshape(32, 128)))

    new_up = up_updated(core, agu[...])
    upx_send[...] = fold(new_up).astype(BF16).reshape(2, 16, 128)
    remote(agu, agu_c, UPC, to_core).start()
    remote(upx_send, upx_r.at[0], UPX, {"tensor": pair}).start()
    remote(upx_send, upx_r.at[1], UPX, {"dp": other_core, "tensor": pair}).start()
    ou[core] = new_up

    landed(ag2_c, DOWNC)
    od[1 - core] = down[1 - core] + step_size * (adapter_scale * tiles_of(ag2_c))
    landed(agu_c, UPC)
    new_up_c = up_updated(1 - core, agu_c[...])
    ou[1 - core] = new_up_c

    landed(upx_r, UPX)
    even = lax.rem(tp, 2) == 0

    def both(mine, theirs):
        left = jnp.where(even, mine, theirs)
        right = jnp.where(even, theirs, mine)
        return jnp.concatenate([left, right], axis=1)

    def columns(mine, theirs):
        return both(mine, unfold(theirs.reshape(32, 128)).astype(F32)).astype(BF16)

    up_own = columns(new_up, upx_r[0])
    up_oth = columns(new_up_c, upx_r[1])
    landed(basep_r, BASEP)
    base_k = both(base[:, :RANK], basep_r[:, :RANK])
    base_v = both(base[:, RANK:], basep_r[:, RANK:])

    landed(stz_r, STATZ)
    landed(mixz_r, MIXZ)
    top, total, acc = combine(
        lambda s: stz_r[...] if s else own_st, lambda s: mixz_r[...] if s else own_mix, 2
    )
    old_high = jnp.concatenate([top[:, i : i + 1] for i in range(ROWS)], axis=0)
    old_total = jnp.concatenate([total[:, i : i + 1] for i in range(ROWS)], axis=0)
    old_mix = jnp.concatenate(acc, axis=0)
    own_q = qp[:, pl.ds(pl.multiple_of(8 * tp, 8), 8), :].reshape(64, HD).astype(BF16)

    landed(low_r, LOW)

    low_own = unfold(summed(low_r.at[:, core], 0, N_Y)).astype(BF16)
    low_oth = unfold(summed(low_r.at[:, 1 - core], 0, N_Y)).astype(BF16)
    from_own = adapter_scale * dot(low_own, up_own)
    from_oth = adapter_scale * dot(low_oth, up_oth)
    first = core == 0
    new_k = (base_k + jnp.where(first, from_own, from_oth)).astype(BF16)
    new_v = (base_v + jnp.where(first, from_oth, from_own)).astype(BF16)
    row = iota((64, 32), 0)
    col = iota((64, 32), 1)
    causal = jnp.logical_and(
        lax.div(row, 8) == lax.div(col, STEPS), lax.rem(col, STEPS) <= lax.rem(row, STEPS)
    )
    score = jnp.where(causal, dot_nt(own_q, new_k) * score_scale, masked_score)
    new_high = jnp.max(score, axis=1, keepdims=True)
    weight = jnp.where(causal, jnp.exp(score - new_high), 0.0)
    new_total = jnp.sum(weight, axis=1, keepdims=True)
    new_mix = dot(weight.astype(BF16), new_v)
    highest = jnp.maximum(old_high, new_high)
    f_old = jnp.exp(old_high - highest)
    f_new = jnp.exp(new_high - highest)
    out = (f_old * old_mix + f_new * new_mix) / (f_old * old_total + f_new * new_total)
    out = out.reshape(ROWS, 8, HD)
    oa[:, :, 0:HD] = out[:, 0:STEPS].astype(BF16)
    oa[:, :, HD:] = out[:, STEPS:].astype(BF16)

    @pl.when(core == 0)
    def _():
        sent(SENT_0)

    @pl.when(core == 1)
    def _():
        sent(SENT_1)


def store(a, b, c, a_h, b_h, c_h, sem):
    copies = [
        pltpu.make_async_copy(src, dst, sem.at[n])
        for n, (src, dst) in enumerate(((a, a_h), (b, b_h), (c, c_h)))
    ]
    for copy in copies:
        copy.start()
    for copy in copies:
        copy.wait()


def shards(
    learn_input,
    cotangent,
    rewards,
    group_ids,
    adapter_down,
    adapter_up,
    frozen_weight,
    hidden,
    queries,
    key_cache,
    value_cache,
    cache_lengths,
):
    hbm = pl.BlockSpec(memory_space=pltpu.HBM)
    operands = (
        learn_input,
        jnp.transpose(cotangent, (1, 2, 0)).reshape(128, TOK),
        adapter_down,
        adapter_up,
        hidden,
        frozen_weight,
        queries.reshape(ROWS, 128, HD),
        key_cache.reshape(ROWS, CACHE_DEV * KVH, HD),
        value_cache.reshape(ROWS, CACHE_DEV * KVH, HD),
    )
    out_shape = (
        jax.ShapeDtypeStruct((2, RANK, FEAT), F32),
        jax.ShapeDtypeStruct((2, RANK, RANK), F32),
        jax.ShapeDtypeStruct((ROWS, STEPS, 2 * HD), BF16),
    )
    vmem = pl.BlockSpec(memory_space=pltpu.VMEM)
    results = pl.pallas_call(
        kernel,
        out_shape=out_shape,
        in_specs=[hbm] * 12,
        out_specs=(vmem,) * 3,
        scratch_shapes=[
            pltpu.SMEM((SEQ_DEV,), F32),
            pltpu.SMEM((SEQ_DEV,), jnp.int32),
            pltpu.SMEM((ROWS,), jnp.int32),
        ]
        + [pltpu.VMEM(o.shape, o.dtype) for o in operands]
        + [
            pltpu.VMEM((TOK, FEAT), BF16),
            pltpu.VMEM((2, RANK, TOK), BF16),
            pltpu.VMEM((RANK, TOK), BF16),
            pltpu.VMEM((ROWS * STEPS, FEAT), F32),
            pltpu.VMEM((2, 16, ROWS * STEPS, FEAT), BF16),
            pltpu.VMEM((2, 16, 128), F32),
            pltpu.VMEM((2, 16, 16, 128), BF16),
            pltpu.VMEM((64, 16, 128), BF16),
            pltpu.VMEM((2, 16, 16, 128), BF16),
            pltpu.VMEM((2, 2, 16, 16, 128), BF16),
            pltpu.VMEM((2, 2, 16, 128), BF16),
            pltpu.VMEM((2, 2, 4, 2, 16, 128), BF16),
            pltpu.VMEM((16, 16, 128), BF16),
            pltpu.VMEM((15, 16, 128), BF16),
            pltpu.VMEM((16, 16, 128), BF16),
            pltpu.VMEM((16, 16, 128), BF16),
            pltpu.VMEM((16, 2, 128), F32),
            pltpu.VMEM((15, 2, 128), F32),
            pltpu.VMEM((16, 2, 128), F32),
            pltpu.VMEM((16, 2, 128), F32),
            pltpu.VMEM((16, 32, 128), BF16),
            pltpu.VMEM((7, 2, 32, 128), BF16),
            pltpu.VMEM((32, 128), F32),
            pltpu.VMEM((32, 128), F32),
            pltpu.VMEM((32, 128), F32),
            pltpu.VMEM((32, 128), F32),
            pltpu.VMEM((16, 64, HD), BF16),
            pltpu.VMEM((7, 2, 64, HD), BF16),
            pltpu.VMEM((64, HD), BF16),
            pltpu.VMEM((64, HD), BF16),
            pltpu.VMEM((16, 8, 128), F32),
            pltpu.VMEM((7, 2, 8, 128), F32),
            pltpu.VMEM((8, 128), F32),
            pltpu.VMEM((8, 128), F32),
            pltpu.VMEM((2, 16, 128), BF16),
            pltpu.VMEM((8, 2, 16, 128), BF16),
            pltpu.VMEM((2, 16, 128), BF16),
            pltpu.VMEM((2, 2, 16, 128), BF16),
            pltpu.VMEM((ROWS, 128, HD), F32),
            pltpu.VMEM((SENT_1, 2, 128), F32),
            pltpu.SemaphoreType.DMA((12,)),
            pltpu.SemaphoreType.DMA((1,)),
            pltpu.SemaphoreType.DMA((N_CHAN,)),
        ],
        compiler_params=pltpu.CompilerParams(
            collective_id=0, has_side_effects=True, vmem_limit_bytes=VMEM_LIMIT
        ),
    )(
        *(
            pltpu.with_memory_space_constraint(o, pltpu.HBM)
            for o in (rewards, group_ids, cache_lengths, *operands)
        )
    )
    return pl.pallas_call(
        store,
        out_shape=out_shape,
        in_specs=[vmem] * 3,
        out_specs=(hbm,) * 3,
        scratch_shapes=[pltpu.SemaphoreType.DMA((3,))],
    )(*(pltpu.with_memory_space_constraint(r, pltpu.VMEM) for r in results))


def solution(mesh):
    return jax.shard_map(
        shards,
        mesh=mesh,
        in_specs=(
            P("dp", "tensor"),
            P("dp", None, "tensor"),
            P("dp"),
            P("dp"),
            P(None, None, "tensor"),
            P(None, None, "tensor"),
            P(None, "tensor", None),
            P("dp", None, "tensor"),
            P("dp", None, None, None),
            P("dp", "tensor", None, None),
            P("dp", "tensor", None, None),
            P("dp"),
        ),
        out_specs=(P(None, None, "tensor"), P(None, None, "tensor"), P("dp", None, "tensor")),
        check_vma=False,
    )
```
